128 devices in a mesh: seq: 32 (over x, y, core), head: 4 (over z).
Axes of the slice: x: 4, y: 4, z: 4, core: 2. Of those that a mesh axis runs over, the one named last changes fastest.
Arguments:
- queries: bfloat16 [32768, 4096], P('seq', 'head'), may hold values from -90 to 90
- keys: bfloat16 [32768, 4096], P('seq', 'head'), may hold values from -50 to 50
- values: bfloat16 [32768, 4096], P('seq', 'head'), may hold values from -6 to 6
- cluster_ids: int32 [32768, 32], P('seq', 'head'), may hold values from 0 to 255, as said below
- out_weight: bfloat16 [4096, 4096], P('head', 'seq'), may hold values from -2.390625 to 2.390625
Outputs:
- mixed: bfloat16 [32768, 4096], P('seq', 'head')
The draws below stay inside these ranges and needn't reach their ends.
Inputs may be any that keep to these rules, and one draw needn't show every extreme that they name: `cluster_ids`: in every head each of the 256 clusters holds at least one token.
All inputs are finite; a program needn't handle non-finite values.
Results may differ from the reference program's by a relative error of at most 0.01.
Values may be sent and summed in bfloat16 or wider, within the bound.
No kernel may reach another device: no remote copies, remote signals or barrier semaphores. Data moves between devices by JAX's collectives and lax.ppermute only.
A program may use at most 128 MiB of HBM per device.

```python
import jax
import jax.numpy as jnp
from jax import lax

D = 4096
HEADS = 32
HDIM = 128
CLUSTERS = 256
TOK_DEV = 1024
TOKENS = 32768
HD = 4096
N_SEQ = 32
N_HEAD = 4


def label_table(key):
    base_key = jax.random.fold_in(key, 11)
    first_key, second_key = jax.random.split(base_key)
    labels = jax.random.randint(first_key, (TOKENS, HEADS), 0, CLUSTERS, dtype=jnp.int32)
    head_keys = jax.random.split(second_key, HEADS)

    def place(head_key, column):
        chosen_rows = jax.random.permutation(head_key, TOKENS)[:CLUSTERS]
        return column.at[chosen_rows].set(jnp.arange(CLUSTERS, dtype=jnp.int32))
    return jax.vmap(place, in_axes=(0, 1), out_axes=1)(head_keys, labels)


def draw_cluster_ids(key, part):
    return label_table(key)


def draw_queries(key, part):
    labels = label_table(key)
    centre_key, jitter_key = jax.random.split(jax.random.fold_in(key, 12))
    centre = 2.0 * jnp.clip(jax.random.normal(centre_key, (HEADS, CLUSTERS, HDIM), jnp.float32), -4.0, 4.0)
    member_centre = jax.vmap(lambda table, column: table[column], in_axes=(0, 1), out_axes=1)(centre, labels)
    jitter = jnp.clip(jax.random.normal(jitter_key, (TOKENS, HEADS, HDIM), jnp.float32), -4.0, 4.0)
    query_rows = member_centre + jitter
    return query_rows.reshape(TOKENS, HEADS * HDIM).astype(jnp.bfloat16)


def draw_keys(key, part):
    row_key = jax.random.fold_in(key, 21)
    key_rows = jnp.clip(jax.random.normal(row_key, (TOKENS, HEADS, HDIM), jnp.float32), -5.0, 5.0)
    return key_rows.reshape(TOKENS, HEADS * HDIM).astype(jnp.bfloat16)


def levels(rng, dims, cuts, smallest, high):
    def one(dim, blocks):
        steps = jax.random.uniform(jax.random.fold_in(jax.random.fold_in(rng, 6), dim), (blocks,), jnp.float32, smallest / len(cuts), high / len(cuts))
        return jnp.repeat(jnp.exp(steps), dims[dim] // blocks).reshape((-1,) + (1,) * (len(dims) - dim - 1))

    loudness = one(*cuts[0])
    for cut in cuts[1:]:
        loudness = loudness * one(*cut)
    return loudness


def centred(rng, extent, scale, limit, pieces=(), held_as=jnp.bfloat16):
    entries = jax.random.normal(rng, extent, jnp.float32) * scale
    if len(pieces) > 0:
        entries = levels(rng, extent, pieces, -0.22, 0.18) * entries
    return jnp.clip(entries, min=-limit, max=limit).astype(held_as)


def setup_inputs(seed: int = 0) -> dict:
    streams_of = jax.random.split(jax.random.key(seed), 6)
    queries = draw_queries(jax.random.fold_in(streams_of[5], 71), 0)
    keys = draw_keys(jax.random.fold_in(streams_of[5], 71), 0)
    values = centred(streams_of[2], (TOKENS, HD), 1.0, 6.0, ((0, 32), (1, 4)))
    cluster_ids = draw_cluster_ids(jax.random.fold_in(streams_of[5], 71), 0)
    out_weight = centred(streams_of[4], (HD, D), 0.4, 2.390625, ((0, 4), (1, 32)))
    return dict(queries=queries, keys=keys, values=values, cluster_ids=cluster_ids, out_weight=out_weight)


def per_head(head, queries, keys, values, cluster_ids):
    first_col = (head * HDIM).astype(jnp.int32)
    labels = lax.dynamic_slice_in_dim(cluster_ids, head.astype(jnp.int32), 1, 1)[:, 0]
    query_rows = lax.dynamic_slice_in_dim(queries, first_col, HDIM, 1).astype(jnp.float32)
    key_rows = lax.dynamic_slice_in_dim(keys, first_col, HDIM, 1).astype(jnp.float32)
    value_rows = lax.dynamic_slice_in_dim(values, first_col, HDIM, 1).astype(jnp.float32)
    member = (labels[:, None] == jnp.arange(CLUSTERS, dtype=jnp.int32)[None, :]).astype(jnp.float32)
    totals = jnp.dot(member.T, query_rows, precision=lax.Precision.HIGHEST)
    counts = jnp.sum(member, axis=0)
    centre = (totals / counts[:, None]).astype(jnp.bfloat16)
    centre = lax.optimization_barrier(centre).astype(jnp.float32)
    key_blocks = key_rows.reshape(N_SEQ, TOK_DEV, HDIM)
    value_blocks = value_rows.reshape(N_SEQ, TOK_DEV, HDIM)
    scores = jnp.einsum("cd,btd->cbt", centre, key_blocks, precision=lax.Precision.HIGHEST) * (1.0 / (HDIM ** 0.5))
    block_peak = jnp.max(scores, axis=2)
    weights = jnp.exp(scores - block_peak[:, :, None]).astype(jnp.bfloat16)
    weights = lax.optimization_barrier(weights).astype(jnp.float32)
    block_mass = jnp.sum(weights, axis=2)
    block_output = jnp.einsum("cbt,btd->cbd", weights, value_blocks, precision=lax.Precision.HIGHEST)
    global_peak = jnp.max(block_peak, axis=1)
    factor = jnp.exp(block_peak - global_peak[:, None])
    output_sum = jnp.sum(factor[:, :, None] * block_output, axis=1)
    mass_sum = jnp.sum(factor * block_mass, axis=1)
    centroid_out = (output_sum / mass_sum[:, None]).astype(jnp.bfloat16)
    return jnp.take(centroid_out, labels, axis=0)


def reference(queries, keys, values, cluster_ids, out_weight):
    def one_head(head):
        return per_head(head, queries, keys, values, cluster_ids)

    attended = lax.map(one_head, jnp.arange(HEADS, dtype=jnp.int32))
    attended = jnp.transpose(attended, (1, 0, 2)).reshape(TOKENS, HEADS * HDIM)
    group_rows = (HEADS * HDIM) // N_HEAD
    summed = jnp.zeros((TOKENS, D), jnp.float32)
    for group in range(N_HEAD):
        term = jnp.dot(attended[:, group * group_rows:(group + 1) * group_rows].astype(jnp.float32),
                       out_weight[group * group_rows:(group + 1) * group_rows, :].astype(jnp.float32),
                       precision=lax.Precision.HIGHEST)
        term = lax.optimization_barrier(term.astype(jnp.bfloat16))
        summed = summed + term.astype(jnp.float32)
    return summed.astype(jnp.bfloat16)
```

```python
import functools
import math

import jax
import jax.numpy as jnp
from jax import lax
from jax.experimental import pallas as pl
from jax.experimental.pallas import tpu as pltpu
from jax.sharding import Mesh
from jax.sharding import PartitionSpec as P

HDIM = 128
CLUSTERS = 256
HALF = 4
QUARTER = CLUSTERS // 4
SEQ = ("x", "y", "c")
PLANE = ("x", "y")
CUBE = ("z", "x", "y")
EXTRA = 8
TAIL = 16
LOG2_SCALE = math.log2(math.e) / math.sqrt(HDIM)
F32 = jnp.float32
BF16 = jnp.bfloat16
NT = (((1,), (1,)), ((), ()))


def params(mib):
    return pltpu.CompilerParams(vmem_limit_bytes=mib * 2**20)


def eye(rows, cols):
    r = lax.broadcasted_iota(jnp.int32, (rows, cols), 0)
    c = lax.broadcasted_iota(jnp.int32, (rows, cols), 1)
    return r == c


def totals_of_head(row, query):
    labels = lax.broadcasted_iota(jnp.int32, (CLUSTERS, row.shape[1]), 0)
    member = (labels == row).astype(F32).astype(BF16)
    total = jnp.dot(member, query, preferred_element_type=F32)
    ones = jnp.ones((EXTRA, row.shape[1]), BF16)
    count = lax.dot_general(ones, member, NT, preferred_element_type=F32)
    return total, count


def owners(total, count):
    spare = jnp.zeros((EXTRA, HDIM - QUARTER), F32)
    for k in range(4):
        lines = slice(k * QUARTER, (k + 1) * QUARTER)
        yield k, total[lines], jnp.concatenate([count[:, lines], spare], axis=1)


def theirs_kernel(side_ref, ids_ref, q_ref, out_ref):
    row = ids_ref[pl.ds(side_ref[0] * HALF + pl.program_id(0), 1), :]
    for k, upper, lower in owners(*totals_of_head(row, q_ref[...])):
        out_ref[k, :QUARTER, :] = upper
        out_ref[k, QUARTER:, :] = lower


def mine_kernel(side_ref, ids_ref, q_ref, in_ref, w_ref, *rest):
    del w_ref
    out_ref = rest[-2]
    row = ids_ref[pl.ds(side_ref[0] * HALF + pl.program_id(0), 1), :]
    for k, upper, lower in owners(*totals_of_head(row, q_ref[...])):
        out_ref[k, :QUARTER, :] = upper + in_ref[k, :QUARTER, :]
        out_ref[k, QUARTER:, :] = lower + in_ref[k, QUARTER:, :]


BY_OWNER = jax.ShapeDtypeStruct((4 * HALF, QUARTER + EXTRA, HDIM), F32)
OWNER_BLOCK = pl.BlockSpec((4, QUARTER + EXTRA, HDIM), lambda i, s: (i, 0, 0))
ANYWHERE = pl.BlockSpec(memory_space=pl.ANY)


def head_specs(ids, rows):
    return [
        pl.BlockSpec(ids.shape, lambda i, s: (0, 0)),
        pl.BlockSpec((rows, HDIM), lambda i, s: (0, s[0] * HALF + i)),
    ]


def theirs_of(side, ids, queries):
    return pl.pallas_call(
        theirs_kernel,
        out_shape=BY_OWNER,
        grid_spec=pltpu.PrefetchScalarGridSpec(
            num_scalar_prefetch=1,
            grid=(HALF,),
            in_specs=head_specs(ids, queries.shape[0]),
            out_specs=OWNER_BLOCK,
        ),
        compiler_params=params(56),
    )(side, ids, queries)


def mine_of(side, ids, queries, arrived, passed):
    others = passed[1:]
    return pl.pallas_call(
        mine_kernel,
        out_shape=(BY_OWNER, jax.ShapeDtypeStruct(passed[0].shape, passed[0].dtype)),
        grid_spec=pltpu.PrefetchScalarGridSpec(
            num_scalar_prefetch=1,
            grid=(HALF,),
            in_specs=head_specs(ids, queries.shape[0])
            + [OWNER_BLOCK]
            + [ANYWHERE] * len(passed),
            out_specs=(OWNER_BLOCK, ANYWHERE),
        ),
        input_output_aliases={4: 1},
        compiler_params=params(56),
    )(side, ids, queries, arrived, passed[0], *others)


def centre_kernel(in_ref, out_ref):
    whole = in_ref[0]
    for k in range(1, in_ref.shape[0]):
        whole += in_ref[k]
    count_row = whole[QUARTER : QUARTER + 1, :]
    spread = jnp.where(eye(QUARTER, HDIM), count_row, 0.0)
    count = jnp.sum(spread, axis=1, keepdims=True)
    centre = (whole[:QUARTER] / count).astype(BF16)
    for k in range(out_ref.shape[0]):
        out_ref[k] = centre


def attention_kernel(side_ref, centre_ref, k_ref, k_other_ref, v_ref, v_other_ref, out_ref):
    del side_ref
    centre = centre_ref[...]
    own = lax.dot_general(centre, k_ref[...], NT, preferred_element_type=F32)
    other = lax.dot_general(centre, k_other_ref[...], NT, preferred_element_type=F32)
    peak = jnp.maximum(
        jnp.max(own, axis=1, keepdims=True), jnp.max(other, axis=1, keepdims=True)
    )
    own_w = jnp.exp2((own - peak) * LOG2_SCALE).astype(BF16)
    other_w = jnp.exp2((other - peak) * LOG2_SCALE).astype(BF16)
    ones = jnp.ones(v_ref.shape, BF16)
    both = jnp.dot(
        own_w, jnp.concatenate([v_ref[...], ones], axis=1), preferred_element_type=F32
    ) + jnp.dot(
        other_w, jnp.concatenate([v_other_ref[...], ones], axis=1), preferred_element_type=F32
    )
    mass = both[:, HDIM:]
    part = (both[:, :HDIM] / mass).astype(BF16)
    level = peak * LOG2_SCALE + jnp.log2(mass)
    diagonal = eye(QUARTER, HDIM)
    line = lax.broadcasted_iota(jnp.int32, (TAIL, HDIM), 0)
    for k in range(4):
        lines = slice(k * QUARTER, (k + 1) * QUARTER)
        row = jnp.sum(jnp.where(diagonal, level[lines], 0.0), axis=0, keepdims=True)
        high = row.astype(BF16).astype(F32)
        mid = (row - high).astype(BF16).astype(F32)
        low = row - high - mid
        tail = jnp.where(line == 0, high, jnp.where(line == 1, mid, jnp.where(line == 2, low, 0.0)))
        out_ref[k, :QUARTER, :] = part[lines]
        out_ref[k, QUARTER:, :] = tail.astype(BF16)


def attention_of(side, centre, keys, keys_other, values, values_other):
    rows = keys.shape[0]
    wide = pl.BlockSpec((rows, HDIM), lambda i, s: (0, s[0] * HALF + i))
    narrow = pl.BlockSpec((rows, HDIM), lambda i, s: (0, i))
    return pl.pallas_call(
        attention_kernel,
        out_shape=jax.ShapeDtypeStruct((4 * HALF, QUARTER + TAIL, HDIM), BF16),
        grid_spec=pltpu.PrefetchScalarGridSpec(
            num_scalar_prefetch=1,
            grid=(HALF,),
            in_specs=[
                pl.BlockSpec((None, CLUSTERS, HDIM), lambda i, s: (i, 0, 0)),
                wide,
                narrow,
                wide,
                narrow,
            ],
            out_specs=pl.BlockSpec((4, QUARTER + TAIL, HDIM), lambda i, s: (i, 0, 0)),
        ),
        compiler_params=params(32),
    )(side, centre, keys, keys_other, values, values_other)


def combine_kernel(in_ref, out_ref):
    count = in_ref.shape[0]
    tails = [in_ref[k, QUARTER:, :].astype(F32) for k in range(count)]
    levels = [t[0:1] + t[1:2] + t[2:3] for t in tails]
    top = functools.reduce(jnp.maximum, levels)
    shares = [jnp.exp2(level - top) for level in levels]
    mass = functools.reduce(jnp.add, shares)
    diagonal = eye(QUARTER, HDIM)
    whole = jnp.zeros((QUARTER, HDIM), F32)
    for k in range(count):
        spread = jnp.where(diagonal, shares[k] / mass, 0.0)
        share = jnp.sum(spread, axis=1, keepdims=True)
        whole += share * in_ref[k, :QUARTER, :].astype(F32)
    whole = whole.astype(BF16)
    for k in range(out_ref.shape[0]):
        out_ref[k] = whole


def one_hot(column):
    labels = lax.broadcasted_iota(jnp.int32, (column.shape[0], CLUSTERS), 1)
    return (labels == column).astype(F32).astype(BF16)


def columns_of(ids, upper):
    turned = jnp.where(upper == 0, ids, pltpu.roll(ids, HALF, 0))
    return turned.T


def gather_kernel(place_ref, ids_ref, table_ref, out_ref):
    columns = columns_of(ids_ref[...], place_ref[0])
    for j in range(HALF):
        rows = jnp.dot(one_hot(columns[:, j : j + 1]), table_ref[j], preferred_element_type=F32)
        out_ref[:, j * HDIM : (j + 1) * HDIM] = rows.astype(BF16)


def group_at(i, place, groups):
    return lax.rem(place[1] + groups - i, groups)


def gather_of(place, ids, table):
    groups, lines, tokens = ids.shape
    return pl.pallas_call(
        gather_kernel,
        out_shape=jax.ShapeDtypeStruct((tokens, groups * HALF * HDIM), BF16),
        grid_spec=pltpu.PrefetchScalarGridSpec(
            num_scalar_prefetch=1,
            grid=(groups,),
            in_specs=[
                pl.BlockSpec((None, lines, tokens), lambda i, s: (i, 0, 0)),
                pl.BlockSpec(
                    (HALF, CLUSTERS, HDIM), lambda i, s: (group_at(i, s, groups), 0, 0)
                ),
            ],
            out_specs=pl.BlockSpec((tokens, HALF * HDIM), lambda i, s: (0, i)),
        ),
        compiler_params=params(24),
    )(place, ids, table)


def project_kernel(groups, place_ref, near_ref, ids_ref, table_ref, w_ref, out_ref, far_ref, acc_ref):
    step = pl.program_id(0)
    weight = jnp.concatenate([w_ref[k] for k in range(w_ref.shape[0])], axis=1)

    @pl.when(step == 0)
    def _():
        acc_ref[...] = jnp.dot(near_ref[...], weight, preferred_element_type=F32)

    @pl.when((step > 0) & (step < groups))
    def _():
        acc_ref[...] += jnp.dot(near_ref[...], weight, preferred_element_type=F32)

    @pl.when(step >= groups)
    def _():
        columns = columns_of(ids_ref[...], 1 - place_ref[0])
        for j in range(HALF):
            rows = jnp.dot(one_hot(columns[:, j : j + 1]), table_ref[j], preferred_element_type=F32)
            far_ref[:, j * HDIM : (j + 1) * HDIM] = rows.astype(BF16)
        acc_ref[...] += jnp.dot(far_ref[...], weight, preferred_element_type=F32)

    @pl.when(step == 2 * groups - 1)
    def _():
        out_ref[...] = acc_ref[...].astype(BF16)


def project_of(place, near, ids, table, weight):
    groups, lines, tokens = ids.shape
    depth = HALF * HDIM
    blocks = weight.shape[1]
    cols = blocks * weight.shape[3]

    def early(i):
        return jnp.minimum(i, groups - 1)

    def late(i):
        return jnp.maximum(i - groups, 0)

    def weight_at(i, s):
        near_half = i < groups
        group = group_at(jnp.where(near_half, i, i - groups), s, groups)
        return (group, 0, jnp.where(near_half, s[0], 1 - s[0]), 0)

    return pl.pallas_call(
        functools.partial(project_kernel, groups),
        out_shape=jax.ShapeDtypeStruct((tokens, cols), BF16),
        grid_spec=pltpu.PrefetchScalarGridSpec(
            num_scalar_prefetch=1,
            grid=(2 * groups,),
            in_specs=[
                pl.BlockSpec((tokens, depth), lambda i, s: (0, early(i))),
                pl.BlockSpec((None, lines, tokens), lambda i, s: (late(i), 0, 0)),
                pl.BlockSpec(
                    (HALF, CLUSTERS, HDIM), lambda i, s: (group_at(late(i), s, groups), 0, 0)
                ),
                pl.BlockSpec((None, blocks, depth, weight.shape[3]), weight_at),
            ],
            out_specs=pl.BlockSpec((tokens, cols), lambda i, s: (0, 0)),
            scratch_shapes=[pltpu.VMEM((tokens, depth), BF16), pltpu.VMEM((tokens, cols), F32)],
        ),
        compiler_params=params(50),
    )(place, near, ids, table, weight)


def other_core(value):
    return lax.ppermute(value, "c", [(0, 1), (1, 0)])


def exchanged(value, axes):
    return lax.all_to_all(value, axes, split_axis=0, concat_axis=0, tiled=True)


def from_all_groups(value):
    size = lax.axis_size("z")
    found = [value]
    for d in range(1, size):
        found.append(lax.ppermute(value, "z", [(i, (i + d) % size) for i in range(size)]))
    return found


def local(queries, keys, values, cluster_ids, out_weight):
    core = lax.axis_index("c").astype(jnp.int32)
    side = core[None]
    place = jnp.stack([core, lax.axis_index("z").astype(jnp.int32)])
    half_cols = HALF * HDIM
    ids = cluster_ids.T
    rows = keys.shape[0]
    far_cols = (1 - core) * half_cols

    arrived = other_core(theirs_of(1 - side, ids, queries))
    keys_other = other_core(lax.dynamic_slice(keys, (0, far_cols), (rows, half_cols)))
    values_other = other_core(lax.dynamic_slice(values, (0, far_cols), (rows, half_cols)))
    size = lax.axis_size("z")
    turned = [(a * size + b, b * size + a) for a in range(size) for b in range(size)]
    turned_weight = lax.ppermute(out_weight, ("x", "z"), turned)
    all_ids = from_all_groups(ids)

    totals, turned_weight = mine_of(side, ids, queries, arrived, [turned_weight, *all_ids[1:]])
    weight = lax.all_gather(turned_weight, SEQ, axis=0)
    weight = weight.reshape(size, -1, *weight.shape[1:])
    totals = exchanged(totals, PLANE)
    copies = lax.axis_size(PLANE)
    centre = pl.pallas_call(
        centre_kernel,
        out_shape=jax.ShapeDtypeStruct((copies, QUARTER, HDIM), BF16),
        compiler_params=params(8),
    )(totals)
    centre = exchanged(centre, PLANE).reshape(HALF, CLUSTERS, HDIM)
    parts = exchanged(
        attention_of(side, centre, keys, keys_other, values, values_other), PLANE
    )
    table = pl.pallas_call(
        combine_kernel,
        out_shape=jax.ShapeDtypeStruct((lax.axis_size(CUBE), QUARTER, HDIM), BF16),
        compiler_params=params(8),
    )(parts)
    table = exchanged(table, CUBE).reshape(size * HALF, CLUSTERS, HDIM)
    far_table = other_core(table)
    stacked = jnp.stack(all_ids)
    near = gather_of(place, stacked, table)
    return project_of(place, near, stacked, far_table, weight)


def solution(mesh):
    head = mesh.shape["head"]
    finer = Mesh(mesh.devices.reshape(4, 4, 2, head), ("x", "y", "c", "z"))
    in_specs = (P(SEQ, "z"), P(SEQ, "z"), P(SEQ, "z"), P(SEQ, "z"), P("z", SEQ))
    return jax.shard_map(
        local, mesh=finer, in_specs=in_specs, out_specs=P(SEQ, "z"), check_vma=False
    )
```

```python
import functools
import math

import jax
import jax.numpy as jnp
from jax import lax
from jax.experimental import pallas as pl
from jax.experimental.pallas import tpu as pltpu
from jax.sharding import Mesh
from jax.sharding import PartitionSpec as P

HDIM = 128
CLUSTERS = 256
HALF = 4
QUARTER = CLUSTERS // 4
SEQ = ("x", "y", "c")
PLANE = ("x", "y")
CUBE = ("z", "x", "y")
EXTRA = 8
TAIL = 16
LARGE = 61
LOG2_SCALE = math.log2(math.e) / math.sqrt(HDIM)
F32 = jnp.float32
BF16 = jnp.bfloat16
NT = (((1,), (1,)), ((), ()))
TN = (((0,), (0,)), ((), ()))


def params(mib):
    return pltpu.CompilerParams(vmem_limit_bytes=mib * 2**20)


def eye(rows, cols):
    r = lax.broadcasted_iota(jnp.int32, (rows, cols), 0)
    c = lax.broadcasted_iota(jnp.int32, (rows, cols), 1)
    return r == c


def member_of(row):
    labels = lax.broadcasted_iota(jnp.int32, (CLUSTERS, row.shape[1]), 0)
    return (labels == row).astype(F32).astype(BF16)


def totals_kernel(halves, side_ref, ids_ref, q_ref, *rest):
    sources, out_ref, copies = rest[:halves], rest[halves], rest[halves + 1 : 2 * halves + 1]
    held, arrived, copied = rest[2 * halves + 1 :]
    rows = q_ref.shape[0]
    first = side_ref[0] * HALF

    def fetch(i):
        start = pl.multiple_of((first + i) * HDIM, HDIM)
        return pltpu.make_async_copy(q_ref.at[:, pl.ds(start, HDIM)], held.at[i], arrived.at[i])

    def copy(k):
        start = pl.multiple_of((HALF - first) * HDIM, HALF * HDIM)
        return pltpu.make_async_copy(
            sources[k].at[:, pl.ds(start, HALF * HDIM)], copies[k], copied.at[k]
        )

    for i in range(HALF):
        fetch(i).start()
    for k in range(halves):
        copy(k).start()
    ones = jnp.ones((rows, HDIM), BF16)
    diagonal = eye(QUARTER, HDIM)
    for i in range(HALF):
        member = member_of(ids_ref[pl.ds(first + i, 1), :])
        fetch(i).wait()
        both = jnp.dot(
            member, jnp.concatenate([held[i], ones], axis=1), preferred_element_type=F32
        )
        for k in range(4):
            lines = slice(k * QUARTER, (k + 1) * QUARTER)
            count = jnp.sum(jnp.where(diagonal, both[lines, HDIM:], 0.0), axis=0, keepdims=True)
            out_ref[i * 4 + k, :QUARTER, :] = both[lines, :HDIM]
            out_ref[i * 4 + k, QUARTER:, :] = jnp.broadcast_to(count, (EXTRA, HDIM))
    for k in range(halves):
        copy(k).wait()


SCALARS = pl.BlockSpec(memory_space=pltpu.SMEM)
IN_VMEM = pl.BlockSpec(memory_space=pltpu.VMEM)
IN_HBM = pl.BlockSpec(memory_space=pltpu.HBM)


def totals_of(side, ids, queries, split=()):
    rows = queries.shape[0]
    halves = len(split)
    return pl.pallas_call(
        functools.partial(totals_kernel, halves),
        out_shape=[jax.ShapeDtypeStruct((4 * HALF, QUARTER + EXTRA, HDIM), F32)]
        + [jax.ShapeDtypeStruct((rows, HALF * HDIM), BF16)] * halves,
        in_specs=[SCALARS, IN_VMEM, IN_HBM] + [IN_HBM] * halves,
        out_specs=[IN_VMEM] + [IN_HBM] * halves,
        scratch_shapes=[
            pltpu.VMEM((HALF, rows, HDIM), BF16),
            pltpu.SemaphoreType.DMA((HALF,)),
            pltpu.SemaphoreType.DMA((max(halves, 1),)),
        ],
        compiler_params=params(LARGE),
    )(side, ids, queries, *split)


def add_kernel(a_ref, b_ref, passed_ref, out_ref, handed_ref):
    del passed_ref, handed_ref
    out_ref[...] = a_ref[...] + b_ref[...]


def add_after(a, b, passed):
    return pl.pallas_call(
        add_kernel,
        out_shape=(
            jax.ShapeDtypeStruct(a.shape, a.dtype),
            jax.ShapeDtypeStruct(passed.shape, passed.dtype),
        ),
        in_specs=[IN_VMEM, IN_VMEM, IN_HBM],
        out_specs=(IN_VMEM, IN_HBM),
        input_output_aliases={2: 1},
        compiler_params=params(8),
    )(a, b, passed)


def centre_kernel(in_ref, ids_ref, out_ref, ids_out_ref):
    whole = in_ref[0]
    for k in range(1, in_ref.shape[0]):
        whole += in_ref[k]
    spread = jnp.where(eye(QUARTER, HDIM), whole[QUARTER : QUARTER + 1, :], 0.0)
    count = jnp.sum(spread, axis=1, keepdims=True)
    centre = (whole[:QUARTER] / count).astype(BF16)
    for k in range(out_ref.shape[0]):
        out_ref[k] = centre
    ids_out_ref[...] = ids_ref[...]


def centre_of(totals, ids):
    return pl.pallas_call(
        centre_kernel,
        out_shape=(
            jax.ShapeDtypeStruct((totals.shape[0], QUARTER, HDIM), BF16),
            jax.ShapeDtypeStruct(ids.shape, ids.dtype),
        ),
        compiler_params=params(8),
    )(totals, ids)


def attention_kernel(groups, side_ref, centre_ref, *rest):
    ids_refs, sources = rest[:groups], rest[groups : groups + 4]
    out_ref, ids_out_ref, held, arrived, copied = rest[groups + 4 :]
    first = side_ref[0] * HALF

    def fetch(i):
        for k in range(4):
            start = i * HDIM if k % 2 else pl.multiple_of((first + i) * HDIM, HDIM)
            yield pltpu.make_async_copy(
                sources[k].at[:, pl.ds(start, HDIM)], held.at[i, k], arrived.at[i, k]
            )

    for i in range(HALF):
        for copy in fetch(i):
            copy.start()
    copies = [
        pltpu.make_async_copy(ids_refs[d], ids_out_ref.at[d], copied.at[d]) for d in range(groups)
    ]
    for copy in copies:
        copy.start()
    ones = jnp.ones(held.shape[2:], BF16)
    diagonal = eye(QUARTER, HDIM)
    line = lax.broadcasted_iota(jnp.int32, (TAIL, HDIM), 0)
    for i in range(HALF):
        for copy in fetch(i):
            copy.wait()
        centre = centre_ref[i]
        own = lax.dot_general(centre, held[i, 0], NT, preferred_element_type=F32)
        other = lax.dot_general(centre, held[i, 1], NT, preferred_element_type=F32)
        peak = jnp.maximum(
            jnp.max(own, axis=1, keepdims=True), jnp.max(other, axis=1, keepdims=True)
        )
        own_w = jnp.exp2((own - peak) * LOG2_SCALE).astype(BF16)
        other_w = jnp.exp2((other - peak) * LOG2_SCALE).astype(BF16)
        both = jnp.dot(
            own_w, jnp.concatenate([held[i, 2], ones], axis=1), preferred_element_type=F32
        ) + jnp.dot(
            other_w, jnp.concatenate([held[i, 3], ones], axis=1), preferred_element_type=F32
        )
        mass = both[:, HDIM:]
        part = (both[:, :HDIM] / mass).astype(BF16)
        level = peak * LOG2_SCALE + jnp.log2(mass)
        for k in range(4):
            lines = slice(k * QUARTER, (k + 1) * QUARTER)
            row = jnp.sum(jnp.where(diagonal, level[lines], 0.0), axis=0, keepdims=True)
            high = row.astype(BF16).astype(F32)
            mid = (row - high).astype(BF16).astype(F32)
            low = row - high - mid
            tail = jnp.where(
                line == 0, high, jnp.where(line == 1, mid, jnp.where(line == 2, low, 0.0))
            )
            out_ref[i * 4 + k, :QUARTER, :] = part[lines]
            out_ref[i * 4 + k, QUARTER:, :] = tail.astype(BF16)
    for copy in copies:
        copy.wait()


def attention_of(side, centre, all_ids, keys, keys_other, values, values_other):
    rows = keys.shape[0]
    groups = len(all_ids)
    return pl.pallas_call(
        functools.partial(attention_kernel, groups),
        out_shape=(
            jax.ShapeDtypeStruct((4 * HALF, QUARTER + TAIL, HDIM), BF16),
            jax.ShapeDtypeStruct((groups, *all_ids[0].shape), jnp.int32),
        ),
        in_specs=[SCALARS, IN_VMEM] + [IN_HBM] * groups + [IN_HBM] * 4,
        out_specs=(IN_VMEM, IN_VMEM),
        scratch_shapes=[
            pltpu.VMEM((HALF, 4, rows, HDIM), BF16),
            pltpu.SemaphoreType.DMA((HALF, 4)),
            pltpu.SemaphoreType.DMA((groups,)),
        ],
        compiler_params=params(LARGE),
    )(side, centre, *all_ids, keys, keys_other, values, values_other)


def combine_kernel(in_ref, out_ref):
    count = in_ref.shape[0]
    tails = [in_ref[k, QUARTER:, :].astype(F32) for k in range(count)]
    levels = [t[0:1] + t[1:2] + t[2:3] for t in tails]
    top = functools.reduce(jnp.maximum, levels)
    shares = [jnp.exp2(level - top) for level in levels]
    mass = functools.reduce(jnp.add, shares)
    diagonal = eye(QUARTER, HDIM)
    whole = jnp.zeros((QUARTER, HDIM), F32)
    for k in range(count):
        spread = jnp.where(diagonal, shares[k] / mass, 0.0)
        share = jnp.sum(spread, axis=1, keepdims=True)
        whole += share * in_ref[k, :QUARTER, :].astype(F32)
    whole = whole.astype(BF16)
    for k in range(out_ref.shape[0]):
        out_ref[k] = whole


def rows_of(ids_row, table):
    return lax.dot_general(member_of(ids_row), table, TN, preferred_element_type=F32).astype(BF16)


def group_at(i, place_ref, groups):
    return lax.rem(place_ref[1] + groups - i, groups)


def gather_kernel(place_ref, ids_ref, table_ref, out_ref):
    group = group_at(pl.program_id(0), place_ref, pl.num_programs(0))
    for j in range(HALF):
        row = ids_ref[pl.program_id(0), pl.ds(place_ref[0] * HALF + j, 1), :]
        out_ref[:, j * HDIM : (j + 1) * HDIM] = rows_of(row, table_ref[group * HALF + j])


def gather_of(place, ids, table):
    groups, lines, tokens = ids.shape
    return pl.pallas_call(
        gather_kernel,
        out_shape=jax.ShapeDtypeStruct((groups, tokens, HALF * HDIM), BF16),
        grid=(groups,),
        in_specs=[SCALARS, IN_VMEM, IN_VMEM],
        out_specs=pl.BlockSpec((None, tokens, HALF * HDIM), lambda i: (i, 0, 0)),
        compiler_params=params(LARGE),
    )(place, ids, table)


def project_kernel(
    place_ref, near_ref, ids_ref, table_ref, w_ref, out_ref, held, near, far, acc, arrived, come
):
    groups, blocks = w_ref.shape[:2]
    depth = HALF * HDIM

    def fetch(i):
        group = group_at(lax.rem(i, groups), place_ref, groups)
        entry = lax.rem(2 * place_ref[1] + groups - group, groups)
        side = jnp.where(i < groups, place_ref[0], 1 - place_ref[0])
        lines = pl.ds(pl.multiple_of(side * depth, depth), depth)
        return pltpu.make_async_copy(w_ref.at[entry, :, lines, :], held.at[i], arrived.at[i])

    def weight(i):
        return jnp.concatenate([held[i, k] for k in range(blocks)], axis=1)

    def bring(i):
        return pltpu.make_async_copy(near_ref.at[i], near.at[i], come.at[i])

    for i in range(groups):
        fetch(i).start()
        bring(i).start()
    for i in range(groups, 2 * groups):
        fetch(i).start()
    fetch(0).wait()
    bring(0).wait()
    acc[...] = jnp.dot(near[0], weight(0), preferred_element_type=F32)

    @pl.loop(1, groups)
    def _(i):
        fetch(i).wait()
        bring(i).wait()
        acc[...] += jnp.dot(near[i], weight(i), preferred_element_type=F32)

    @pl.loop(groups, 2 * groups)
    def _(i):
        group = group_at(i - groups, place_ref, groups)
        for j in range(HALF):
            row = ids_ref[i - groups, pl.ds((1 - place_ref[0]) * HALF + j, 1), :]
            far[:, j * HDIM : (j + 1) * HDIM] = rows_of(row, table_ref[group * HALF + j])
        fetch(i).wait()
        acc[...] += jnp.dot(far[...], weight(i), preferred_element_type=F32)

    out_ref[...] = acc[...].astype(BF16)


def project_of(place, near, ids, table, weight):
    groups, lines, tokens = ids.shape
    depth = HALF * HDIM
    blocks, width = weight.shape[1], weight.shape[3]
    cols = blocks * width
    return pl.pallas_call(
        project_kernel,
        out_shape=jax.ShapeDtypeStruct((tokens, cols), BF16),
        in_specs=[SCALARS, IN_HBM, IN_VMEM, IN_VMEM, IN_HBM],
        out_specs=IN_VMEM,
        scratch_shapes=[
            pltpu.VMEM((2 * groups, blocks, depth, width), BF16),
            pltpu.VMEM((groups, tokens, depth), BF16),
            pltpu.VMEM((tokens, depth), BF16),
            pltpu.VMEM((tokens, cols), F32),
            pltpu.SemaphoreType.DMA((2 * groups,)),
            pltpu.SemaphoreType.DMA((groups,)),
        ],
        compiler_params=params(56),
    )(place, near, ids, table, weight)


def other_core(value):
    return lax.ppermute(value, "c", [(0, 1), (1, 0)])


def exchanged(value, axes):
    return lax.all_to_all(value, axes, split_axis=0, concat_axis=0, tiled=True)


def from_all_groups(value):
    size = lax.axis_size("z")
    found = [value]
    for d in range(1, size):
        found.append(lax.ppermute(value, "z", [(i, (i + d) % size) for i in range(size)]))
    return found


def local(queries, keys, values, cluster_ids, out_weight):
    core = lax.axis_index("c").astype(jnp.int32)
    side = core[None]
    place = jnp.stack([core, lax.axis_index("z").astype(jnp.int32)])
    ids = cluster_ids.T
    size = lax.axis_size("z")
    turned = [
        (x * size + z, (2 * x - z) % size * size + x) for x in range(size) for z in range(size)
    ]
    turned_weight = lax.ppermute(out_weight, ("x", "z"), turned)

    (theirs,) = totals_of(1 - side, ids, queries)
    arrived = other_core(theirs)
    mine, keys_far, values_far = totals_of(side, ids, queries, (keys, values))
    keys_other, values_other = other_core(keys_far), other_core(values_far)
    totals, turned_weight = add_after(mine, arrived, turned_weight)
    weight = lax.all_gather(turned_weight, SEQ, axis=0)
    weight = weight.reshape(size, -1, *weight.shape[1:])

    centre, ids = centre_of(exchanged(totals, PLANE), ids)
    all_ids = from_all_groups(ids)
    centre = exchanged(centre, PLANE).reshape(HALF, CLUSTERS, HDIM)
    parts, all_ids = attention_of(
        side, centre, all_ids, keys, keys_other, values, values_other
    )
    parts = exchanged(parts, PLANE)
    table = pl.pallas_call(
        combine_kernel,
        out_shape=jax.ShapeDtypeStruct((lax.axis_size(CUBE), QUARTER, HDIM), BF16),
        compiler_params=params(8),
    )(parts)
    table = exchanged(table, CUBE).reshape(size * HALF, CLUSTERS, HDIM)
    far_table = other_core(table)
    near = gather_of(place, all_ids, table)
    return project_of(place, near, all_ids, far_table, weight)


def solution(mesh):
    head = mesh.shape["head"]
    finer = Mesh(mesh.devices.reshape(4, 4, 2, head), ("x", "y", "c", "z"))
    in_specs = (P(SEQ, "z"), P(SEQ, "z"), P(SEQ, "z"), P(SEQ, "z"), P("z", SEQ))
    return jax.shard_map(
        local, mesh=finer, in_specs=in_specs, out_specs=P(SEQ, "z"), check_vma=False
    )
```

```python
import functools
import math

import jax
import jax.numpy as jnp
from jax import lax
from jax.experimental import pallas as pl
from jax.experimental.pallas import tpu as pltpu
from jax.sharding import Mesh
from jax.sharding import PartitionSpec as P

HDIM = 128
CLUSTERS = 256
HALF = 4
QUARTER = CLUSTERS // 4
SEQ = ("x", "y", "c")
PLANE = ("x", "y")
CUBE = ("z", "x", "y")
EXTRA = 8
TAIL = 16
LARGE = 61
LOG2_SCALE = math.log2(math.e) / math.sqrt(HDIM)
F32 = jnp.float32
BF16 = jnp.bfloat16
NT = (((1,), (1,)), ((), ()))
TN = (((0,), (0,)), ((), ()))


def params(mib):
    return pltpu.CompilerParams(vmem_limit_bytes=mib * 2**20)


def eye(rows, cols):
    r = lax.broadcasted_iota(jnp.int32, (rows, cols), 0)
    c = lax.broadcasted_iota(jnp.int32, (rows, cols), 1)
    return r == c


def member_of(row):
    labels = lax.broadcasted_iota(jnp.int32, (CLUSTERS, row.shape[1]), 0)
    return (labels == row).astype(F32).astype(BF16)


def totals_kernel(side_ref, ids_ref, q_ref, theirs_ref, mine_ref, held, arrived):
    rows = q_ref.shape[0]
    firsts = (HALF - side_ref[0] * HALF, side_ref[0] * HALF)

    def fetch(k):
        start = pl.multiple_of(firsts[k] * HDIM, HALF * HDIM)
        return pltpu.make_async_copy(
            q_ref.at[:, pl.ds(start, HALF * HDIM)], held.at[k], arrived.at[k]
        )

    for k in range(2):
        fetch(k).start()
    ones = jnp.ones((rows, HDIM), BF16)
    diagonal = eye(QUARTER, HDIM)
    for k, out_ref in enumerate((theirs_ref, mine_ref)):
        fetch(k).wait()
        for i in range(HALF):
            member = member_of(ids_ref[pl.ds(firsts[k] + i, 1), :])
            query = held[k, :, i * HDIM : (i + 1) * HDIM]
            both = jnp.dot(
                member, jnp.concatenate([query, ones], axis=1), preferred_element_type=F32
            )
            for q in range(4):
                lines = slice(q * QUARTER, (q + 1) * QUARTER)
                count = jnp.sum(
                    jnp.where(diagonal, both[lines, HDIM:], 0.0), axis=0, keepdims=True
                )
                out_ref[i * 4 + q, :QUARTER, :] = both[lines, :HDIM]
                out_ref[i * 4 + q, QUARTER:, :] = jnp.broadcast_to(count, (EXTRA, HDIM))


SCALARS = pl.BlockSpec(memory_space=pltpu.SMEM)
IN_VMEM = pl.BlockSpec(memory_space=pltpu.VMEM)
IN_HBM = pl.BlockSpec(memory_space=pltpu.HBM)


def totals_of(side, ids, queries):
    rows = queries.shape[0]
    return pl.pallas_call(
        totals_kernel,
        out_shape=[jax.ShapeDtypeStruct((4 * HALF, QUARTER + EXTRA, HDIM), F32)] * 2,
        in_specs=[SCALARS, IN_VMEM, IN_HBM],
        out_specs=[IN_VMEM] * 2,
        scratch_shapes=[
            pltpu.VMEM((2, rows, HALF * HDIM), BF16),
            pltpu.SemaphoreType.DMA((2,)),
        ],
        compiler_params=params(LARGE),
    )(side, ids, queries)


def halves_kernel(side_ref, after_ref, k_ref, v_ref, k_out_ref, v_out_ref, held, come, gone):
    del after_ref
    start = pl.multiple_of((1 - side_ref[0]) * HALF * HDIM, HALF * HDIM)

    def fetch(k, source):
        return pltpu.make_async_copy(
            source.at[:, pl.ds(start, HALF * HDIM)], held.at[k], come.at[k]
        )

    def put(k, target):
        return pltpu.make_async_copy(held.at[k], target, gone.at[k])

    fetch(0, k_ref).start()
    fetch(1, v_ref).start()
    fetch(0, k_ref).wait()
    put(0, k_out_ref).start()
    fetch(1, v_ref).wait()
    put(1, v_out_ref).start()
    put(0, k_out_ref).wait()
    put(1, v_out_ref).wait()


def halves_of(side, after, keys, values):
    half = jax.ShapeDtypeStruct((keys.shape[0], HALF * HDIM), BF16)
    return pl.pallas_call(
        halves_kernel,
        out_shape=(half, half),
        in_specs=[SCALARS, IN_HBM, IN_HBM, IN_HBM],
        out_specs=(IN_HBM, IN_HBM),
        scratch_shapes=[
            pltpu.VMEM((2, *half.shape), BF16),
            pltpu.SemaphoreType.DMA((2,)),
            pltpu.SemaphoreType.DMA((2,)),
        ],
        compiler_params=params(LARGE),
    )(side, after, keys, values)


def add_kernel(a_ref, b_ref, passed_ref, out_ref, handed_ref):
    del passed_ref, handed_ref
    out_ref[...] = a_ref[...] + b_ref[...]


def add_after(a, b, passed):
    return pl.pallas_call(
        add_kernel,
        out_shape=(
            jax.ShapeDtypeStruct(a.shape, a.dtype),
            jax.ShapeDtypeStruct(passed.shape, passed.dtype),
        ),
        in_specs=[IN_VMEM, IN_VMEM, IN_HBM],
        out_specs=(IN_VMEM, IN_HBM),
        input_output_aliases={2: 1},
        compiler_params=params(8),
    )(a, b, passed)


def centre_kernel(in_ref, ids_ref, out_ref, ids_out_ref):
    whole = in_ref[0]
    for k in range(1, in_ref.shape[0]):
        whole += in_ref[k]
    spread = jnp.where(eye(QUARTER, HDIM), whole[QUARTER : QUARTER + 1, :], 0.0)
    count = jnp.sum(spread, axis=1, keepdims=True)
    centre = (whole[:QUARTER] / count).astype(BF16)
    for k in range(out_ref.shape[0]):
        out_ref[k] = centre
    ids_out_ref[...] = ids_ref[...]


def centre_of(totals, ids):
    return pl.pallas_call(
        centre_kernel,
        out_shape=(
            jax.ShapeDtypeStruct((totals.shape[0], QUARTER, HDIM), BF16),
            jax.ShapeDtypeStruct(ids.shape, ids.dtype),
        ),
        compiler_params=params(8),
    )(totals, ids)


def attention_kernel(groups, side_ref, centre_ref, *rest):
    ids_refs, sources = rest[:groups], rest[groups : groups + 4]
    out_ref, ids_out_ref, held, arrived, copied = rest[groups + 4 :]
    first = side_ref[0] * HALF

    def fetch(k):
        source = sources[k]
        if k % 2 == 0:
            source = source.at[:, pl.ds(pl.multiple_of(first * HDIM, HALF * HDIM), HALF * HDIM)]
        return pltpu.make_async_copy(source, held.at[k], arrived.at[k])

    for k in range(4):
        fetch(k).start()
    copies = [
        pltpu.make_async_copy(ids_refs[d], ids_out_ref.at[d], copied.at[d]) for d in range(groups)
    ]
    for copy in copies:
        copy.start()
    ones = jnp.ones((held.shape[1], HDIM), BF16)
    diagonal = eye(QUARTER, HDIM)
    line = lax.broadcasted_iota(jnp.int32, (TAIL, HDIM), 0)
    for i in range(HALF):
        if i == 0:
            fetch(0).wait()
            fetch(1).wait()
        cols = slice(i * HDIM, (i + 1) * HDIM)
        centre = centre_ref[i]
        own = lax.dot_general(centre, held[0, :, cols], NT, preferred_element_type=F32)
        other = lax.dot_general(centre, held[1, :, cols], NT, preferred_element_type=F32)
        peak = jnp.maximum(
            jnp.max(own, axis=1, keepdims=True), jnp.max(other, axis=1, keepdims=True)
        )
        own_w = jnp.exp2((own - peak) * LOG2_SCALE).astype(BF16)
        other_w = jnp.exp2((other - peak) * LOG2_SCALE).astype(BF16)
        if i == 0:
            fetch(2).wait()
            fetch(3).wait()
        both = jnp.dot(
            own_w, jnp.concatenate([held[2, :, cols], ones], axis=1), preferred_element_type=F32
        ) + jnp.dot(
            other_w, jnp.concatenate([held[3, :, cols], ones], axis=1), preferred_element_type=F32
        )
        mass = both[:, HDIM:]
        part = (both[:, :HDIM] / mass).astype(BF16)
        level = peak * LOG2_SCALE + jnp.log2(mass)
        for k in range(4):
            lines = slice(k * QUARTER, (k + 1) * QUARTER)
            row = jnp.sum(jnp.where(diagonal, level[lines], 0.0), axis=0, keepdims=True)
            high = row.astype(BF16).astype(F32)
            mid = (row - high).astype(BF16).astype(F32)
            low = row - high - mid
            tail = jnp.where(
                line == 0, high, jnp.where(line == 1, mid, jnp.where(line == 2, low, 0.0))
            )
            out_ref[i * 4 + k, :QUARTER, :] = part[lines]
            out_ref[i * 4 + k, QUARTER:, :] = tail.astype(BF16)
    for copy in copies:
        copy.wait()


def attention_of(side, centre, all_ids, keys, keys_other, values, values_other):
    rows = keys.shape[0]
    groups = len(all_ids)
    return pl.pallas_call(
        functools.partial(attention_kernel, groups),
        out_shape=(
            jax.ShapeDtypeStruct((4 * HALF, QUARTER + TAIL, HDIM), BF16),
            jax.ShapeDtypeStruct((groups, *all_ids[0].shape), jnp.int32),
        ),
        in_specs=[SCALARS, IN_VMEM] + [IN_HBM] * groups + [IN_HBM] * 4,
        out_specs=(IN_VMEM, IN_VMEM),
        scratch_shapes=[
            pltpu.VMEM((4, rows, HALF * HDIM), BF16),
            pltpu.SemaphoreType.DMA((4,)),
            pltpu.SemaphoreType.DMA((groups,)),
        ],
        compiler_params=params(LARGE),
    )(side, centre, *all_ids, keys, keys_other, values, values_other)


def combine_kernel(in_ref, out_ref):
    count = in_ref.shape[0]
    tails = [in_ref[k, QUARTER:, :].astype(F32) for k in range(count)]
    levels = [t[0:1] + t[1:2] + t[2:3] for t in tails]
    top = functools.reduce(jnp.maximum, levels)
    shares = [jnp.exp2(level - top) for level in levels]
    mass = functools.reduce(jnp.add, shares)
    diagonal = eye(QUARTER, HDIM)
    whole = jnp.zeros((QUARTER, HDIM), F32)
    for k in range(count):
        spread = jnp.where(diagonal, shares[k] / mass, 0.0)
        share = jnp.sum(spread, axis=1, keepdims=True)
        whole += share * in_ref[k, :QUARTER, :].astype(F32)
    whole = whole.astype(BF16)
    for k in range(out_ref.shape[0]):
        out_ref[k] = whole


def rows_of(ids_row, table):
    return lax.dot_general(member_of(ids_row), table, TN, preferred_element_type=F32).astype(BF16)


def group_at(i, z_ref, groups):
    return lax.rem(z_ref[0] + groups - i, groups)


def gather_kernel(side_ref, z_ref, ids_ref, table_ref, after_ref, out_ref):
    del after_ref
    group = group_at(pl.program_id(0), z_ref, pl.num_programs(0))
    for j in range(HALF):
        row = ids_ref[pl.program_id(0), pl.ds(side_ref[0] * HALF + j, 1), :]
        out_ref[:, j * HDIM : (j + 1) * HDIM] = rows_of(row, table_ref[group * HALF + j])


def gather_of(side, z, ids, table, after):
    groups, lines, tokens = ids.shape
    return pl.pallas_call(
        gather_kernel,
        out_shape=jax.ShapeDtypeStruct((groups, tokens, HALF * HDIM), BF16),
        grid=(groups,),
        in_specs=[SCALARS, SCALARS, IN_VMEM, IN_VMEM, IN_HBM],
        out_specs=pl.BlockSpec((None, tokens, HALF * HDIM), lambda i: (i, 0, 0)),
        compiler_params=params(24),
    )(side, z, ids, table, after)


def project_kernel(
    side_ref,
    z_ref,
    near_ref,
    ids_ref,
    table_ref,
    w_ref,
    out_ref,
    held,
    near,
    far,
    acc,
    arrived,
    come,
):
    groups, blocks = w_ref.shape[:2]
    depth = HALF * HDIM

    def fetch(i):
        group = group_at(lax.rem(i, groups), z_ref, groups)
        entry = lax.rem(2 * z_ref[0] + groups - group, groups)
        side = jnp.where(i < groups, side_ref[0], 1 - side_ref[0])
        lines = pl.ds(pl.multiple_of(side * depth, depth), depth)
        return pltpu.make_async_copy(w_ref.at[entry, :, lines, :], held.at[i], arrived.at[i])

    def weight(i):
        return jnp.concatenate([held[i, k] for k in range(blocks)], axis=1)

    def bring(i):
        return pltpu.make_async_copy(near_ref.at[i], near.at[i], come.at[i])

    for i in range(groups):
        fetch(i).start()
        bring(i).start()
    for i in range(groups, 2 * groups):
        fetch(i).start()
    fetch(0).wait()
    bring(0).wait()
    acc[...] = jnp.dot(near[0], weight(0), preferred_element_type=F32)

    @pl.loop(1, groups)
    def _(i):
        fetch(i).wait()
        bring(i).wait()
        acc[...] += jnp.dot(near[i], weight(i), preferred_element_type=F32)

    @pl.loop(groups, 2 * groups)
    def _(i):
        group = group_at(i - groups, z_ref, groups)
        for j in range(HALF):
            row = ids_ref[i - groups, pl.ds((1 - side_ref[0]) * HALF + j, 1), :]
            far[:, j * HDIM : (j + 1) * HDIM] = rows_of(row, table_ref[group * HALF + j])
        fetch(i).wait()
        acc[...] += jnp.dot(far[...], weight(i), preferred_element_type=F32)

    out_ref[...] = acc[...].astype(BF16)


def project_of(side, z, near, ids, table, weight):
    groups, lines, tokens = ids.shape
    depth = HALF * HDIM
    blocks, width = weight.shape[1], weight.shape[3]
    cols = blocks * width
    return pl.pallas_call(
        project_kernel,
        out_shape=jax.ShapeDtypeStruct((tokens, cols), BF16),
        in_specs=[SCALARS, SCALARS, IN_HBM, IN_VMEM, IN_VMEM, IN_HBM],
        out_specs=IN_VMEM,
        scratch_shapes=[
            pltpu.VMEM((2 * groups, blocks, depth, width), BF16),
            pltpu.VMEM((groups, tokens, depth), BF16),
            pltpu.VMEM((tokens, depth), BF16),
            pltpu.VMEM((tokens, cols), F32),
            pltpu.SemaphoreType.DMA((2 * groups,)),
            pltpu.SemaphoreType.DMA((groups,)),
        ],
        compiler_params=params(40),
    )(side, z, near, ids, table, weight)


def other_core(value):
    return lax.ppermute(value, "c", [(0, 1), (1, 0)])


def exchanged(value, axes):
    return lax.all_to_all(value, axes, split_axis=0, concat_axis=0, tiled=True)


def from_all_groups(value):
    size = lax.axis_size("z")
    found = [value]
    for d in range(1, size):
        found.append(lax.ppermute(value, "z", [(i, (i + d) % size) for i in range(size)]))
    return found


def local(queries, keys, values, cluster_ids, out_weight):
    core = lax.axis_index("c").astype(jnp.int32)
    side = core[None]
    z = lax.axis_index("z").astype(jnp.int32)[None]
    ids = cluster_ids.T
    size = lax.axis_size("z")
    turned = [
        (x * size + z, (2 * x - z) % size * size + x) for x in range(size) for z in range(size)
    ]
    turned_weight = lax.ppermute(out_weight, ("x", "z"), turned)

    theirs, mine = totals_of(side, ids, queries)
    arrived = other_core(theirs)
    keys_far, values_far = halves_of(side, theirs, keys, values)
    keys_other, values_other = other_core(keys_far), other_core(values_far)
    totals, turned_weight = add_after(mine, arrived, turned_weight)
    weight = lax.all_gather(turned_weight, SEQ, axis=0)
    weight = weight.reshape(size, -1, *weight.shape[1:])

    centre, ids = centre_of(exchanged(totals, PLANE), ids)
    all_ids = from_all_groups(ids)
    centre = exchanged(centre, PLANE).reshape(HALF, CLUSTERS, HDIM)
    parts, all_ids = attention_of(
        side, centre, all_ids, keys, keys_other, values, values_other
    )
    parts = exchanged(parts, PLANE)
    table = pl.pallas_call(
        combine_kernel,
        out_shape=jax.ShapeDtypeStruct((lax.axis_size(CUBE), QUARTER, HDIM), BF16),
        compiler_params=params(8),
    )(parts)
    table = exchanged(table, CUBE).reshape(size * HALF, CLUSTERS, HDIM)
    far_table = other_core(table)
    near = gather_of(side, z, all_ids, table, weight[0, 0, :16])
    return project_of(side, z, near, all_ids, far_table, weight)


def solution(mesh):
    head = mesh.shape["head"]
    finer = Mesh(mesh.devices.reshape(4, 4, 2, head), ("x", "y", "c", "z"))
    in_specs = (P(SEQ, "z"), P(SEQ, "z"), P(SEQ, "z"), P(SEQ, "z"), P("z", SEQ))
    return jax.shard_map(
        local, mesh=finer, in_specs=in_specs, out_specs=P(SEQ, "z"), check_vma=False
    )
```

```python
import functools
import math

import jax
import jax.numpy as jnp
from jax import lax
from jax.experimental import pallas as pl
from jax.experimental.pallas import tpu as pltpu
from jax.sharding import Mesh
from jax.sharding import PartitionSpec as P

HDIM = 128
CLUSTERS = 256
HALF = 4
QUARTER = CLUSTERS // 4
SEQ = ("x", "y", "c")
PLANE = ("x", "y")
CUBE = ("z", "x", "y")
EXTRA = 8
TAIL = 16
LARGE = 61
LOG2_SCALE = math.log2(math.e) / math.sqrt(HDIM)
F32 = jnp.float32
BF16 = jnp.bfloat16
NT = (((1,), (1,)), ((), ()))
TN = (((0,), (0,)), ((), ()))


def params(mib):
    return pltpu.CompilerParams(vmem_limit_bytes=mib * 2**20)


def eye(rows, cols):
    r = lax.broadcasted_iota(jnp.int32, (rows, cols), 0)
    c = lax.broadcasted_iota(jnp.int32, (rows, cols), 1)
    return r == c


def member_of(row):
    labels = lax.broadcasted_iota(jnp.int32, (CLUSTERS, row.shape[1]), 0)
    return (labels == row).astype(F32).astype(BF16)


def totals_kernel(side_ref, ids_ref, q_ref, theirs_ref, mine_ref, held, arrived):
    rows = q_ref.shape[0]
    firsts = (HALF - side_ref[0] * HALF, side_ref[0] * HALF)

    def fetch(k):
        start = pl.multiple_of(firsts[k] * HDIM, HALF * HDIM)
        return pltpu.make_async_copy(
            q_ref.at[:, pl.ds(start, HALF * HDIM)], held.at[k], arrived.at[k]
        )

    for k in range(2):
        fetch(k).start()
    ones = jnp.ones((rows, HDIM), BF16)
    diagonal = eye(QUARTER, HDIM)
    for k, out_ref in enumerate((theirs_ref, mine_ref)):
        fetch(k).wait()
        for i in range(HALF):
            member = member_of(ids_ref[pl.ds(firsts[k] + i, 1), :])
            query = held[k, :, i * HDIM : (i + 1) * HDIM]
            both = jnp.dot(
                member, jnp.concatenate([query, ones], axis=1), preferred_element_type=F32
            )
            for q in range(4):
                lines = slice(q * QUARTER, (q + 1) * QUARTER)
                count = jnp.sum(
                    jnp.where(diagonal, both[lines, HDIM:], 0.0), axis=0, keepdims=True
                )
                out_ref[i * 4 + q, :QUARTER, :] = both[lines, :HDIM]
                out_ref[i * 4 + q, QUARTER:, :] = jnp.broadcast_to(count, (EXTRA, HDIM))


SCALARS = pl.BlockSpec(memory_space=pltpu.SMEM)
IN_VMEM = pl.BlockSpec(memory_space=pltpu.VMEM)
IN_HBM = pl.BlockSpec(memory_space=pltpu.HBM)


def totals_of(side, ids, queries):
    rows = queries.shape[0]
    return pl.pallas_call(
        totals_kernel,
        out_shape=[jax.ShapeDtypeStruct((4 * HALF, QUARTER + EXTRA, HDIM), F32)] * 2,
        in_specs=[SCALARS, IN_VMEM, IN_HBM],
        out_specs=[IN_VMEM] * 2,
        scratch_shapes=[
            pltpu.VMEM((2, rows, HALF * HDIM), BF16),
            pltpu.SemaphoreType.DMA((2,)),
        ],
        compiler_params=params(60),
    )(side, ids, queries)


def halves_kernel(side_ref, after_ref, k_ref, v_ref, k_out_ref, v_out_ref, held, come, gone):
    del after_ref
    start = pl.multiple_of((1 - side_ref[0]) * HALF * HDIM, HALF * HDIM)

    def fetch(k, source):
        return pltpu.make_async_copy(
            source.at[:, pl.ds(start, HALF * HDIM)], held.at[k], come.at[k]
        )

    def put(k, target):
        return pltpu.make_async_copy(held.at[k], target, gone.at[k])

    fetch(0, k_ref).start()
    fetch(1, v_ref).start()
    fetch(0, k_ref).wait()
    put(0, k_out_ref).start()
    fetch(1, v_ref).wait()
    put(1, v_out_ref).start()
    put(0, k_out_ref).wait()
    put(1, v_out_ref).wait()


def halves_of(side, after, keys, values):
    half = jax.ShapeDtypeStruct((keys.shape[0], HALF * HDIM), BF16)
    return pl.pallas_call(
        halves_kernel,
        out_shape=(half, half),
        in_specs=[SCALARS, IN_HBM, IN_HBM, IN_HBM],
        out_specs=(IN_HBM, IN_HBM),
        scratch_shapes=[
            pltpu.VMEM((2, *half.shape), BF16),
            pltpu.SemaphoreType.DMA((2,)),
            pltpu.SemaphoreType.DMA((2,)),
        ],
        compiler_params=params(LARGE),
    )(side, after, keys, values)


def centre_kernel(in_ref, ids_ref, passed_ref, out_ref, ids_out_ref, handed_ref):
    del passed_ref, handed_ref
    whole = in_ref[0]
    for k in range(1, in_ref.shape[0]):
        whole += in_ref[k]
    spread = jnp.where(eye(QUARTER, HDIM), whole[QUARTER : QUARTER + 1, :], 0.0)
    count = jnp.sum(spread, axis=1, keepdims=True)
    centre = (whole[:QUARTER] / count).astype(BF16)
    for k in range(out_ref.shape[0]):
        out_ref[k] = centre
    ids_out_ref[...] = ids_ref[...]


def centre_of(totals, ids, passed):
    return pl.pallas_call(
        centre_kernel,
        out_shape=(
            jax.ShapeDtypeStruct((totals.shape[0], QUARTER, HDIM), BF16),
            jax.ShapeDtypeStruct(ids.shape, ids.dtype),
            jax.ShapeDtypeStruct(passed.shape, passed.dtype),
        ),
        in_specs=[IN_VMEM, IN_VMEM, IN_HBM],
        out_specs=(IN_VMEM, IN_VMEM, IN_HBM),
        input_output_aliases={2: 2},
        compiler_params=params(8),
    )(totals, ids, passed)


def attention_kernel(groups, side_ref, centre_ref, *rest):
    ids_refs, sources = rest[:groups], rest[groups : groups + 4]
    out_ref, ids_out_ref, held, arrived, copied = rest[groups + 4 :]
    first = side_ref[0] * HALF

    def fetch(k):
        source = sources[k]
        if k % 2 == 0:
            source = source.at[:, pl.ds(pl.multiple_of(first * HDIM, HALF * HDIM), HALF * HDIM)]
        return pltpu.make_async_copy(source, held.at[k], arrived.at[k])

    for k in range(4):
        fetch(k).start()
    copies = [
        pltpu.make_async_copy(ids_refs[d], ids_out_ref.at[d], copied.at[d]) for d in range(groups)
    ]
    for copy in copies:
        copy.start()
    ones = jnp.ones((held.shape[1], HDIM), BF16)
    diagonal = eye(QUARTER, HDIM)
    line = lax.broadcasted_iota(jnp.int32, (TAIL, HDIM), 0)
    for i in range(HALF):
        if i == 0:
            fetch(0).wait()
            fetch(1).wait()
        cols = slice(i * HDIM, (i + 1) * HDIM)
        centre = centre_ref[i]
        own = lax.dot_general(centre, held[0, :, cols], NT, preferred_element_type=F32)
        other = lax.dot_general(centre, held[1, :, cols], NT, preferred_element_type=F32)
        peak = jnp.maximum(
            jnp.max(own, axis=1, keepdims=True), jnp.max(other, axis=1, keepdims=True)
        )
        own_w = jnp.exp2((own - peak) * LOG2_SCALE).astype(BF16)
        other_w = jnp.exp2((other - peak) * LOG2_SCALE).astype(BF16)
        if i == 0:
            fetch(2).wait()
            fetch(3).wait()
        both = jnp.dot(
            own_w, jnp.concatenate([held[2, :, cols], ones], axis=1), preferred_element_type=F32
        ) + jnp.dot(
            other_w, jnp.concatenate([held[3, :, cols], ones], axis=1), preferred_element_type=F32
        )
        mass = both[:, HDIM:]
        part = (both[:, :HDIM] / mass).astype(BF16)
        level = peak * LOG2_SCALE + jnp.log2(mass)
        for k in range(4):
            lines = slice(k * QUARTER, (k + 1) * QUARTER)
            row = jnp.sum(jnp.where(diagonal, level[lines], 0.0), axis=0, keepdims=True)
            high = row.astype(BF16).astype(F32)
            mid = (row - high).astype(BF16).astype(F32)
            low = row - high - mid
            tail = jnp.where(
                line == 0, high, jnp.where(line == 1, mid, jnp.where(line == 2, low, 0.0))
            )
            out_ref[i * 4 + k, :QUARTER, :] = part[lines]
            out_ref[i * 4 + k, QUARTER:, :] = tail.astype(BF16)
    for copy in copies:
        copy.wait()


def attention_of(side, centre, all_ids, keys, keys_other, values, values_other):
    rows = keys.shape[0]
    groups = len(all_ids)
    return pl.pallas_call(
        functools.partial(attention_kernel, groups),
        out_shape=(
            jax.ShapeDtypeStruct((4 * HALF, QUARTER + TAIL, HDIM), BF16),
            jax.ShapeDtypeStruct((groups, *all_ids[0].shape), jnp.int32),
        ),
        in_specs=[SCALARS, IN_VMEM] + [IN_HBM] * groups + [IN_HBM] * 4,
        out_specs=(IN_VMEM, IN_VMEM),
        scratch_shapes=[
            pltpu.VMEM((4, rows, HALF * HDIM), BF16),
            pltpu.SemaphoreType.DMA((4,)),
            pltpu.SemaphoreType.DMA((groups,)),
        ],
        compiler_params=params(LARGE),
    )(side, centre, *all_ids, keys, keys_other, values, values_other)


def combine_kernel(in_ref, out_ref):
    count = in_ref.shape[0]
    tails = [in_ref[k, QUARTER:, :].astype(F32) for k in range(count)]
    levels = [t[0:1] + t[1:2] + t[2:3] for t in tails]
    top = functools.reduce(jnp.maximum, levels)
    shares = [jnp.exp2(level - top) for level in levels]
    mass = functools.reduce(jnp.add, shares)
    diagonal = eye(QUARTER, HDIM)
    whole = jnp.zeros((QUARTER, HDIM), F32)
    for k in range(count):
        spread = jnp.where(diagonal, shares[k] / mass, 0.0)
        share = jnp.sum(spread, axis=1, keepdims=True)
        whole += share * in_ref[k, :QUARTER, :].astype(F32)
    whole = whole.astype(BF16)
    for k in range(out_ref.shape[0]):
        out_ref[k] = whole


def rows_of(ids_row, table):
    return lax.dot_general(member_of(ids_row), table, TN, preferred_element_type=F32).astype(BF16)


def group_at(i, z_ref, groups):
    return lax.rem(z_ref[0] + groups - i, groups)


def gather_kernel(side_ref, z_ref, ids_ref, table_ref, after_ref, out_ref):
    del after_ref
    group = group_at(pl.program_id(0), z_ref, pl.num_programs(0))
    for j in range(HALF):
        row = ids_ref[pl.program_id(0), pl.ds(side_ref[0] * HALF + j, 1), :]
        out_ref[:, j * HDIM : (j + 1) * HDIM] = rows_of(row, table_ref[group * HALF + j])


def gather_of(side, z, ids, table, after):
    groups, lines, tokens = ids.shape
    return pl.pallas_call(
        gather_kernel,
        out_shape=jax.ShapeDtypeStruct((groups, tokens, HALF * HDIM), BF16),
        grid=(groups,),
        in_specs=[SCALARS, SCALARS, IN_VMEM, IN_VMEM, IN_HBM],
        out_specs=pl.BlockSpec((None, tokens, HALF * HDIM), lambda i: (i, 0, 0)),
        compiler_params=params(57),
    )(side, z, ids, table, after)


def project_kernel(
    side_ref,
    z_ref,
    near_ref,
    ids_ref,
    table_ref,
    w_ref,
    out_ref,
    held,
    near,
    far,
    acc,
    arrived,
    come,
):
    groups, blocks = w_ref.shape[:2]
    depth = HALF * HDIM

    def fetch(i):
        group = group_at(lax.rem(i, groups), z_ref, groups)
        entry = lax.rem(2 * z_ref[0] + groups - group, groups)
        side = jnp.where(i < groups, side_ref[0], 1 - side_ref[0])
        lines = pl.ds(pl.multiple_of(side * depth, depth), depth)
        return pltpu.make_async_copy(w_ref.at[entry, :, lines, :], held.at[i], arrived.at[i])

    def weight(i):
        return jnp.concatenate([held[i, k] for k in range(blocks)], axis=1)

    def bring(i):
        return pltpu.make_async_copy(near_ref.at[i], near.at[i], come.at[i])

    for i in range(groups):
        fetch(i).start()
        bring(i).start()
    for i in range(groups, 2 * groups):
        fetch(i).start()
    fetch(0).wait()
    bring(0).wait()
    acc[...] = jnp.dot(near[0], weight(0), preferred_element_type=F32)

    @pl.loop(1, groups)
    def _(i):
        fetch(i).wait()
        bring(i).wait()
        acc[...] += jnp.dot(near[i], weight(i), preferred_element_type=F32)

    @pl.loop(groups, 2 * groups)
    def _(i):
        group = group_at(i - groups, z_ref, groups)
        for j in range(HALF):
            row = ids_ref[i - groups, pl.ds((1 - side_ref[0]) * HALF + j, 1), :]
            far[:, j * HDIM : (j + 1) * HDIM] = rows_of(row, table_ref[group * HALF + j])
        fetch(i).wait()
        acc[...] += jnp.dot(far[...], weight(i), preferred_element_type=F32)

    out_ref[...] = acc[...].astype(BF16)


def project_of(side, z, near, ids, table, weight):
    groups, lines, tokens = ids.shape
    depth = HALF * HDIM
    blocks, width = weight.shape[1], weight.shape[3]
    cols = blocks * width
    return pl.pallas_call(
        project_kernel,
        out_shape=jax.ShapeDtypeStruct((tokens, cols), BF16),
        in_specs=[SCALARS, SCALARS, IN_HBM, IN_VMEM, IN_VMEM, IN_HBM],
        out_specs=IN_VMEM,
        scratch_shapes=[
            pltpu.VMEM((2 * groups, blocks, depth, width), BF16),
            pltpu.VMEM((groups, tokens, depth), BF16),
            pltpu.VMEM((tokens, depth), BF16),
            pltpu.VMEM((tokens, cols), F32),
            pltpu.SemaphoreType.DMA((2 * groups,)),
            pltpu.SemaphoreType.DMA((groups,)),
        ],
        compiler_params=params(57),
    )(side, z, near, ids, table, weight)


def other_core(value):
    return lax.ppermute(value, "c", [(0, 1), (1, 0)])


def exchanged(value, axes):
    return lax.all_to_all(value, axes, split_axis=0, concat_axis=0, tiled=True)


def from_all_groups(value):
    size = lax.axis_size("z")
    found = [value]
    for d in range(1, size):
        found.append(lax.ppermute(value, "z", [(i, (i + d) % size) for i in range(size)]))
    return found


def local(queries, keys, values, cluster_ids, out_weight):
    core = lax.axis_index("c").astype(jnp.int32)
    side = core[None]
    z = lax.axis_index("z").astype(jnp.int32)[None]
    ids = cluster_ids.T
    size = lax.axis_size("z")
    turned = [
        (x * size + z, (2 * x - z) % size * size + x) for x in range(size) for z in range(size)
    ]
    turned_weight = lax.ppermute(out_weight, ("x", "z"), turned)

    theirs, mine = totals_of(side, ids, queries)
    arrived = other_core(theirs)
    keys_far, values_far = halves_of(side, theirs, keys, values)
    keys_other, values_other = other_core(keys_far), other_core(values_far)
    totals = exchanged(mine + arrived, PLANE)
    centre, ids, turned_weight = centre_of(totals, ids, turned_weight)
    weight = lax.all_gather(turned_weight, SEQ, axis=0)
    weight = weight.reshape(size, -1, *weight.shape[1:])
    all_ids = from_all_groups(ids)
    centre = exchanged(centre, PLANE).reshape(HALF, CLUSTERS, HDIM)
    parts, all_ids = attention_of(
        side, centre, all_ids, keys, keys_other, values, values_other
    )
    parts = exchanged(parts, PLANE)
    table = pl.pallas_call(
        combine_kernel,
        out_shape=jax.ShapeDtypeStruct((lax.axis_size(CUBE), QUARTER, HDIM), BF16),
        compiler_params=params(8),
    )(parts)
    table = exchanged(table, CUBE).reshape(size * HALF, CLUSTERS, HDIM)
    far_table = other_core(table)
    near = gather_of(side, z, all_ids, table, weight)
    return project_of(side, z, near, all_ids, far_table, weight)


def solution(mesh):
    head = mesh.shape["head"]
    finer = Mesh(mesh.devices.reshape(4, 4, 2, head), ("x", "y", "c", "z"))
    in_specs = (P(SEQ, "z"), P(SEQ, "z"), P(SEQ, "z"), P(SEQ, "z"), P("z", SEQ))
    return jax.shard_map(
        local, mesh=finer, in_specs=in_specs, out_specs=P(SEQ, "z"), check_vma=False
    )
```

```python
import functools
import math

import jax
import jax.numpy as jnp
from jax import lax
from jax.experimental import pallas as pl
from jax.experimental.pallas import tpu as pltpu
from jax.sharding import Mesh
from jax.sharding import PartitionSpec as P

HDIM = 128
CLUSTERS = 256
PIECES = 4
HALF = 4
QUARTER = CLUSTERS // 4
SEQ = ("x", "y", "c")
PLANE = ("x", "y")
CUBE = ("z", "x", "y")
EXTRA = 8
TAIL = 16
LARGE = 61
LOG2_SCALE = math.log2(math.e) / math.sqrt(HDIM)
F32 = jnp.float32
BF16 = jnp.bfloat16
NT = (((1,), (1,)), ((), ()))
TN = (((0,), (0,)), ((), ()))


def params(mib):
    return pltpu.CompilerParams(vmem_limit_bytes=mib * 2**20)


def eye(rows, cols):
    r = lax.broadcasted_iota(jnp.int32, (rows, cols), 0)
    c = lax.broadcasted_iota(jnp.int32, (rows, cols), 1)
    return r == c


def member_of(row):
    labels = lax.broadcasted_iota(jnp.int32, (CLUSTERS, row.shape[1]), 0)
    return (labels == row).astype(F32).astype(BF16)


def totals_kernel(side_ref, ids_ref, q_ref, *rest):
    theirs_refs, (mine_ref, held, arrived) = rest[:PIECES], rest[PIECES:]
    each = HALF // PIECES
    rows = q_ref.shape[0]
    firsts = (HALF - side_ref[0] * HALF, side_ref[0] * HALF)

    def fetch(k):
        start = pl.multiple_of(firsts[k] * HDIM, HALF * HDIM)
        return pltpu.make_async_copy(
            q_ref.at[:, pl.ds(start, HALF * HDIM)], held.at[k], arrived.at[k]
        )

    for k in range(2):
        fetch(k).start()
    ones = jnp.ones((rows, HDIM), BF16)
    diagonal = eye(QUARTER, HDIM)
    for k in range(2):
        fetch(k).wait()
        for i in range(HALF):
            out_ref, base = (mine_ref, i * 4) if k else (theirs_refs[i // each], i % each * 4)
            member = member_of(ids_ref[pl.ds(firsts[k] + i, 1), :])
            query = held[k, :, i * HDIM : (i + 1) * HDIM]
            both = jnp.dot(
                member, jnp.concatenate([query, ones], axis=1), preferred_element_type=F32
            )
            for q in range(4):
                lines = slice(q * QUARTER, (q + 1) * QUARTER)
                count = jnp.sum(
                    jnp.where(diagonal, both[lines, HDIM:], 0.0), axis=0, keepdims=True
                )
                out_ref[base + q, :QUARTER, :] = both[lines, :HDIM]
                out_ref[base + q, QUARTER:, :] = jnp.broadcast_to(count, (EXTRA, HDIM))


SCALARS = pl.BlockSpec(memory_space=pltpu.SMEM)
IN_VMEM = pl.BlockSpec(memory_space=pltpu.VMEM)
IN_HBM = pl.BlockSpec(memory_space=pltpu.HBM)


def totals_of(side, ids, queries):
    rows = queries.shape[0]
    return pl.pallas_call(
        totals_kernel,
        out_shape=[
            jax.ShapeDtypeStruct((4 * HALF // PIECES, QUARTER + EXTRA, HDIM), F32),
        ]
        * PIECES
        + [jax.ShapeDtypeStruct((4 * HALF, QUARTER + EXTRA, HDIM), F32)],
        in_specs=[SCALARS, IN_VMEM, IN_HBM],
        out_specs=[IN_VMEM] * (PIECES + 1),
        scratch_shapes=[
            pltpu.VMEM((2, rows, HALF * HDIM), BF16),
            pltpu.SemaphoreType.DMA((2,)),
        ],
        compiler_params=params(58),
    )(side, ids, queries)


def halves_kernel(
    side_ref, after_ref, k_ref, v_ref, k_out_ref, v_out_ref, token_ref, held, come, gone
):
    del after_ref
    token_ref[...] = jnp.zeros(token_ref.shape, token_ref.dtype)
    start = pl.multiple_of((1 - side_ref[0]) * HALF * HDIM, HALF * HDIM)

    def fetch(k, source):
        return pltpu.make_async_copy(
            source.at[:, pl.ds(start, HALF * HDIM)], held.at[k], come.at[k]
        )

    def put(k, target):
        return pltpu.make_async_copy(held.at[k], target, gone.at[k])

    fetch(0, k_ref).start()
    fetch(1, v_ref).start()
    fetch(0, k_ref).wait()
    put(0, k_out_ref).start()
    fetch(1, v_ref).wait()
    put(1, v_out_ref).start()
    put(0, k_out_ref).wait()
    put(1, v_out_ref).wait()


def halves_of(side, after, keys, values):
    half = jax.ShapeDtypeStruct((keys.shape[0], HALF * HDIM), BF16)
    return pl.pallas_call(
        halves_kernel,
        out_shape=(half, half, jax.ShapeDtypeStruct((8, HDIM), F32)),
        in_specs=[SCALARS, IN_HBM, IN_HBM, IN_HBM],
        out_specs=(IN_HBM, IN_HBM, IN_VMEM),
        scratch_shapes=[
            pltpu.VMEM((2, *half.shape), BF16),
            pltpu.SemaphoreType.DMA((2,)),
            pltpu.SemaphoreType.DMA((2,)),
        ],
        compiler_params=params(LARGE),
    )(side, after, keys, values)


def add_kernel(a_ref, *rest):
    out_ref = rest[PIECES + 2]
    size = a_ref.shape[0] // PIECES
    for k in range(PIECES):
        lines = slice(k * size, (k + 1) * size)
        out_ref[lines] = a_ref[lines] + rest[k][...]


def add_after(a, b, passed, after):
    return pl.pallas_call(
        add_kernel,
        out_shape=(
            jax.ShapeDtypeStruct(a.shape, a.dtype),
            jax.ShapeDtypeStruct(passed.shape, passed.dtype),
        ),
        in_specs=[IN_VMEM] * (PIECES + 1) + [IN_HBM, IN_HBM],
        out_specs=(IN_VMEM, IN_HBM),
        input_output_aliases={PIECES + 1: 1},
        compiler_params=params(8),
    )(a, *b, passed, after)


def centre_kernel(in_ref, ids_ref, out_ref, ids_out_ref):
    whole = in_ref[0]
    for k in range(1, in_ref.shape[0]):
        whole += in_ref[k]
    spread = jnp.where(eye(QUARTER, HDIM), whole[QUARTER : QUARTER + 1, :], 0.0)
    count = jnp.sum(spread, axis=1, keepdims=True)
    centre = (whole[:QUARTER] / count).astype(BF16)
    for k in range(out_ref.shape[0]):
        out_ref[k] = centre
    ids_out_ref[...] = ids_ref[...]


def centre_of(totals, ids):
    return pl.pallas_call(
        centre_kernel,
        out_shape=(
            jax.ShapeDtypeStruct((totals.shape[0], QUARTER, HDIM), BF16),
            jax.ShapeDtypeStruct(ids.shape, ids.dtype),
        ),
        compiler_params=params(8),
    )(totals, ids)


def attention_kernel(groups, side_ref, centre_ref, *rest):
    ids_refs, sources = rest[:groups], rest[groups : groups + 4]
    out_ref, ids_out_ref, held, arrived, copied = rest[groups + 4 :]
    first = side_ref[0] * HALF

    def fetch(k):
        source = sources[k]
        if k % 2 == 0:
            source = source.at[:, pl.ds(pl.multiple_of(first * HDIM, HALF * HDIM), HALF * HDIM)]
        return pltpu.make_async_copy(source, held.at[k], arrived.at[k])

    for k in range(4):
        fetch(k).start()
    copies = [
        pltpu.make_async_copy(ids_refs[d], ids_out_ref.at[d], copied.at[d]) for d in range(groups)
    ]
    for copy in copies:
        copy.start()
    ones = jnp.ones((held.shape[1], HDIM), BF16)
    diagonal = eye(QUARTER, HDIM)
    line = lax.broadcasted_iota(jnp.int32, (TAIL, HDIM), 0)
    for i in range(HALF):
        if i == 0:
            fetch(0).wait()
            fetch(1).wait()
        cols = slice(i * HDIM, (i + 1) * HDIM)
        centre = centre_ref[i]
        own = lax.dot_general(centre, held[0, :, cols], NT, preferred_element_type=F32)
        other = lax.dot_general(centre, held[1, :, cols], NT, preferred_element_type=F32)
        peak = jnp.maximum(
            jnp.max(own, axis=1, keepdims=True), jnp.max(other, axis=1, keepdims=True)
        )
        own_w = jnp.exp2((own - peak) * LOG2_SCALE).astype(BF16)
        other_w = jnp.exp2((other - peak) * LOG2_SCALE).astype(BF16)
        if i == 0:
            fetch(2).wait()
            fetch(3).wait()
        both = jnp.dot(
            own_w, jnp.concatenate([held[2, :, cols], ones], axis=1), preferred_element_type=F32
        ) + jnp.dot(
            other_w, jnp.concatenate([held[3, :, cols], ones], axis=1), preferred_element_type=F32
        )
        mass = both[:, HDIM:]
        part = (both[:, :HDIM] / mass).astype(BF16)
        level = peak * LOG2_SCALE + jnp.log2(mass)
        for k in range(4):
            lines = slice(k * QUARTER, (k + 1) * QUARTER)
            row = jnp.sum(jnp.where(diagonal, level[lines], 0.0), axis=0, keepdims=True)
            high = row.astype(BF16).astype(F32)
            mid = (row - high).astype(BF16).astype(F32)
            low = row - high - mid
            tail = jnp.where(
                line == 0, high, jnp.where(line == 1, mid, jnp.where(line == 2, low, 0.0))
            )
            out_ref[i * 4 + k, :QUARTER, :] = part[lines]
            out_ref[i * 4 + k, QUARTER:, :] = tail.astype(BF16)
    for copy in copies:
        copy.wait()


def attention_of(side, centre, all_ids, keys, keys_other, values, values_other):
    rows = keys.shape[0]
    groups = len(all_ids)
    return pl.pallas_call(
        functools.partial(attention_kernel, groups),
        out_shape=(
            jax.ShapeDtypeStruct((4 * HALF, QUARTER + TAIL, HDIM), BF16),
            jax.ShapeDtypeStruct((groups, *all_ids[0].shape), jnp.int32),
        ),
        in_specs=[SCALARS, IN_VMEM] + [IN_HBM] * groups + [IN_HBM] * 4,
        out_specs=(IN_VMEM, IN_VMEM),
        scratch_shapes=[
            pltpu.VMEM((4, rows, HALF * HDIM), BF16),
            pltpu.SemaphoreType.DMA((4,)),
            pltpu.SemaphoreType.DMA((groups,)),
        ],
        compiler_params=params(LARGE),
    )(side, centre, *all_ids, keys, keys_other, values, values_other)


def combine_kernel(in_ref, out_ref):
    count = in_ref.shape[0]
    tails = [in_ref[k, QUARTER:, :].astype(F32) for k in range(count)]
    levels = [t[0:1] + t[1:2] + t[2:3] for t in tails]
    top = functools.reduce(jnp.maximum, levels)
    shares = [jnp.exp2(level - top) for level in levels]
    mass = functools.reduce(jnp.add, shares)
    diagonal = eye(QUARTER, HDIM)
    whole = jnp.zeros((QUARTER, HDIM), F32)
    for k in range(count):
        spread = jnp.where(diagonal, shares[k] / mass, 0.0)
        share = jnp.sum(spread, axis=1, keepdims=True)
        whole += share * in_ref[k, :QUARTER, :].astype(F32)
    whole = whole.astype(BF16)
    for k in range(out_ref.shape[0]):
        out_ref[k] = whole


def rows_of(ids_row, table):
    return lax.dot_general(member_of(ids_row), table, TN, preferred_element_type=F32).astype(BF16)


def group_at(i, z_ref, groups):
    return lax.rem(z_ref[0] + groups - i, groups)


def gather_kernel(side_ref, z_ref, ids_ref, table_ref, after_ref, out_ref):
    del after_ref
    group = group_at(pl.program_id(0), z_ref, pl.num_programs(0))
    for j in range(HALF):
        row = ids_ref[pl.program_id(0), pl.ds(side_ref[0] * HALF + j, 1), :]
        out_ref[:, j * HDIM : (j + 1) * HDIM] = rows_of(row, table_ref[group * HALF + j])


def gather_of(side, z, ids, table, after):
    groups, lines, tokens = ids.shape
    return pl.pallas_call(
        gather_kernel,
        out_shape=jax.ShapeDtypeStruct((groups, tokens, HALF * HDIM), BF16),
        grid=(groups,),
        in_specs=[SCALARS, SCALARS, IN_VMEM, IN_VMEM, IN_HBM],
        out_specs=pl.BlockSpec((None, tokens, HALF * HDIM), lambda i: (i, 0, 0)),
        compiler_params=params(51),
    )(side, z, ids, table, after)


def project_kernel(
    side_ref,
    z_ref,
    near_ref,
    ids_ref,
    table_ref,
    w_ref,
    out_ref,
    held,
    near,
    far,
    acc,
    arrived,
    come,
):
    groups, blocks = w_ref.shape[:2]
    depth = HALF * HDIM

    def fetch(i):
        group = group_at(lax.rem(i, groups), z_ref, groups)
        entry = lax.rem(2 * z_ref[0] + groups - group, groups)
        side = jnp.where(i < groups, side_ref[0], 1 - side_ref[0])
        lines = pl.ds(pl.multiple_of(side * depth, depth), depth)
        return pltpu.make_async_copy(w_ref.at[entry, :, lines, :], held.at[i], arrived.at[i])

    def weight(i):
        return jnp.concatenate([held[i, k] for k in range(blocks)], axis=1)

    def bring(i):
        return pltpu.make_async_copy(near_ref.at[i], near.at[i], come.at[i])

    for i in range(groups):
        fetch(i).start()
        bring(i).start()
    for i in range(groups, 2 * groups):
        fetch(i).start()
    fetch(0).wait()
    bring(0).wait()
    acc[...] = jnp.dot(near[0], weight(0), preferred_element_type=F32)

    @pl.loop(1, groups)
    def _(i):
        fetch(i).wait()
        bring(i).wait()
        acc[...] += jnp.dot(near[i], weight(i), preferred_element_type=F32)

    @pl.loop(groups, 2 * groups)
    def _(i):
        group = group_at(i - groups, z_ref, groups)
        for j in range(HALF):
            row = ids_ref[i - groups, pl.ds((1 - side_ref[0]) * HALF + j, 1), :]
            far[:, j * HDIM : (j + 1) * HDIM] = rows_of(row, table_ref[group * HALF + j])
        fetch(i).wait()
        acc[...] += jnp.dot(far[...], weight(i), preferred_element_type=F32)

    out_ref[...] = acc[...].astype(BF16)


def project_of(side, z, near, ids, table, weight):
    groups, lines, tokens = ids.shape
    depth = HALF * HDIM
    blocks, width = weight.shape[1], weight.shape[3]
    cols = blocks * width
    return pl.pallas_call(
        project_kernel,
        out_shape=jax.ShapeDtypeStruct((tokens, cols), BF16),
        in_specs=[SCALARS, SCALARS, IN_HBM, IN_VMEM, IN_VMEM, IN_HBM],
        out_specs=IN_VMEM,
        scratch_shapes=[
            pltpu.VMEM((2 * groups, blocks, depth, width), BF16),
            pltpu.VMEM((groups, tokens, depth), BF16),
            pltpu.VMEM((tokens, depth), BF16),
            pltpu.VMEM((tokens, cols), F32),
            pltpu.SemaphoreType.DMA((2 * groups,)),
            pltpu.SemaphoreType.DMA((groups,)),
        ],
        compiler_params=params(51),
    )(side, z, near, ids, table, weight)


def other_core(value):
    return lax.ppermute(value, "c", [(0, 1), (1, 0)])


def exchanged(value, axes):
    return lax.all_to_all(value, axes, split_axis=0, concat_axis=0, tiled=True)


def from_all_groups(value):
    size = lax.axis_size("z")
    found = [value]
    for d in range(1, size):
        found.append(lax.ppermute(value, "z", [(i, (i + d) % size) for i in range(size)]))
    return found


def local(queries, keys, values, cluster_ids, out_weight):
    core = lax.axis_index("c").astype(jnp.int32)
    side = core[None]
    z = lax.axis_index("z").astype(jnp.int32)[None]
    ids = cluster_ids.T
    size = lax.axis_size("z")
    turned = [
        (x * size + z, (2 * x - z) % size * size + x) for x in range(size) for z in range(size)
    ]
    turned_weight = lax.ppermute(out_weight, ("x", "z"), turned)

    *theirs, mine = totals_of(side, ids, queries)
    arrived = [other_core(piece) for piece in theirs]
    keys_far, values_far, token = halves_of(side, theirs[0], keys, values)
    keys_other, values_other = other_core(keys_far), other_core(values_far)
    totals, turned_weight = add_after(mine, arrived, turned_weight, token)
    centre, ids = centre_of(exchanged(totals, PLANE), ids)
    weight = lax.all_gather(turned_weight, SEQ, axis=0)
    weight = weight.reshape(size, -1, *weight.shape[1:])
    all_ids = from_all_groups(ids)
    centre = exchanged(centre, PLANE).reshape(HALF, CLUSTERS, HDIM)
    parts, all_ids = attention_of(
        side, centre, all_ids, keys, keys_other, values, values_other
    )
    parts = exchanged(parts, PLANE)
    table = pl.pallas_call(
        combine_kernel,
        out_shape=jax.ShapeDtypeStruct((lax.axis_size(CUBE), QUARTER, HDIM), BF16),
        compiler_params=params(8),
    )(parts)
    table = exchanged(table, CUBE).reshape(size * HALF, CLUSTERS, HDIM)
    far_table = other_core(table)
    near = gather_of(side, z, all_ids, table, weight)
    return project_of(side, z, near, all_ids, far_table, weight)


def solution(mesh):
    head = mesh.shape["head"]
    finer = Mesh(mesh.devices.reshape(4, 4, 2, head), ("x", "y", "c", "z"))
    in_specs = (P(SEQ, "z"), P(SEQ, "z"), P(SEQ, "z"), P(SEQ, "z"), P("z", SEQ))
    return jax.shard_map(
        local, mesh=finer, in_specs=in_specs, out_specs=P(SEQ, "z"), check_vma=False
    )
```

```python
import functools
import math

import jax
import jax.numpy as jnp
from jax import lax
from jax.experimental import pallas as pl
from jax.experimental.pallas import tpu as pltpu
from jax.sharding import Mesh
from jax.sharding import PartitionSpec as P

HDIM = 128
CLUSTERS = 256
PIECES = 4
HALF = 4
QUARTER = CLUSTERS // 4
SEQ = ("x", "y", "c")
PLANE = ("x", "y")
CUBE = ("z", "x", "y")
EXTRA = 8
TAIL = 16
LARGE = 61
LOG2_SCALE = math.log2(math.e) / math.sqrt(HDIM)
F32 = jnp.float32
BF16 = jnp.bfloat16
NT = (((1,), (1,)), ((), ()))
TN = (((0,), (0,)), ((), ()))


def params(mib):
    return pltpu.CompilerParams(vmem_limit_bytes=mib * 2**20)


def eye(rows, cols):
    r = lax.broadcasted_iota(jnp.int32, (rows, cols), 0)
    c = lax.broadcasted_iota(jnp.int32, (rows, cols), 1)
    return r == c


def member_of(row):
    labels = lax.broadcasted_iota(jnp.int32, (CLUSTERS, row.shape[1]), 0)
    return (labels == row).astype(F32).astype(BF16)


def totals_kernel(side_ref, ids_ref, q_ref, *rest):
    theirs_refs, (mine_ref, held, arrived) = rest[:PIECES], rest[PIECES:]
    each = HALF // PIECES
    rows = q_ref.shape[0]
    firsts = (HALF - side_ref[0] * HALF, side_ref[0] * HALF)

    def fetch(k):
        start = pl.multiple_of(firsts[k] * HDIM, HALF * HDIM)
        return pltpu.make_async_copy(
            q_ref.at[:, pl.ds(start, HALF * HDIM)], held.at[k], arrived.at[k]
        )

    for k in range(2):
        fetch(k).start()
    ones = jnp.ones((rows, HDIM), BF16)
    diagonal = eye(QUARTER, HDIM)
    for k in range(2):
        fetch(k).wait()
        for i in range(HALF):
            out_ref, base = (mine_ref, i * 4) if k else (theirs_refs[i // each], i % each * 4)
            member = member_of(ids_ref[pl.ds(firsts[k] + i, 1), :])
            query = held[k, :, i * HDIM : (i + 1) * HDIM]
            both = jnp.dot(
                member, jnp.concatenate([query, ones], axis=1), preferred_element_type=F32
            )
            for q in range(4):
                lines = slice(q * QUARTER, (q + 1) * QUARTER)
                count = jnp.sum(
                    jnp.where(diagonal, both[lines, HDIM:], 0.0), axis=0, keepdims=True
                )
                out_ref[base + q, :QUARTER, :] = both[lines, :HDIM]
                out_ref[base + q, QUARTER:, :] = jnp.broadcast_to(count, (EXTRA, HDIM))


SCALARS = pl.BlockSpec(memory_space=pltpu.SMEM)
IN_VMEM = pl.BlockSpec(memory_space=pltpu.VMEM)
ANYWHERE = pl.BlockSpec(memory_space=pl.ANY)
IN_HBM = pl.BlockSpec(memory_space=pltpu.HBM)


def totals_of(side, ids, queries):
    rows = queries.shape[0]
    return pl.pallas_call(
        totals_kernel,
        out_shape=[
            jax.ShapeDtypeStruct((4 * HALF // PIECES, QUARTER + EXTRA, HDIM), F32),
        ]
        * PIECES
        + [jax.ShapeDtypeStruct((4 * HALF, QUARTER + EXTRA, HDIM), F32)],
        in_specs=[SCALARS, IN_VMEM, IN_HBM],
        out_specs=[IN_VMEM] * (PIECES + 1),
        scratch_shapes=[
            pltpu.VMEM((2, rows, HALF * HDIM), BF16),
            pltpu.SemaphoreType.DMA((2,)),
        ],
        compiler_params=params(58),
    )(side, ids, queries)


def halves_kernel(
    side_ref, after_ref, k_ref, v_ref, k_out_ref, v_out_ref, token_ref, held, come, gone
):
    del after_ref
    token_ref[...] = jnp.zeros(token_ref.shape, token_ref.dtype)
    start = pl.multiple_of((1 - side_ref[0]) * HALF * HDIM, HALF * HDIM)

    def fetch(k, source):
        return pltpu.make_async_copy(
            source.at[:, pl.ds(start, HALF * HDIM)], held.at[k], come.at[k]
        )

    def put(k, target):
        return pltpu.make_async_copy(held.at[k], target, gone.at[k])

    fetch(0, k_ref).start()
    fetch(1, v_ref).start()
    fetch(0, k_ref).wait()
    put(0, k_out_ref).start()
    fetch(1, v_ref).wait()
    put(1, v_out_ref).start()
    put(0, k_out_ref).wait()
    put(1, v_out_ref).wait()


def halves_of(side, after, keys, values):
    half = jax.ShapeDtypeStruct((keys.shape[0], HALF * HDIM), BF16)
    return pl.pallas_call(
        halves_kernel,
        out_shape=(half, half, jax.ShapeDtypeStruct((8, HDIM), F32)),
        in_specs=[SCALARS, IN_HBM, IN_HBM, IN_HBM],
        out_specs=(IN_HBM, IN_HBM, IN_VMEM),
        scratch_shapes=[
            pltpu.VMEM((2, *half.shape), BF16),
            pltpu.SemaphoreType.DMA((2,)),
            pltpu.SemaphoreType.DMA((2,)),
        ],
        compiler_params=params(LARGE),
    )(side, after, keys, values)


def add_kernel(a_ref, *rest):
    ids_ref, out_ref, ids_out_ref = rest[PIECES + 2], rest[PIECES + 3], rest[PIECES + 5]
    ids_out_ref[...] = ids_ref[...]
    size = a_ref.shape[0] // PIECES
    for k in range(PIECES):
        lines = slice(k * size, (k + 1) * size)
        out_ref[lines] = a_ref[lines] + rest[k][...]


def add_after(a, b, passed, after, ids):
    return pl.pallas_call(
        add_kernel,
        out_shape=(
            jax.ShapeDtypeStruct(a.shape, a.dtype),
            jax.ShapeDtypeStruct(passed.shape, passed.dtype),
            jax.ShapeDtypeStruct(ids.shape, ids.dtype),
        ),
        in_specs=[IN_VMEM] * (PIECES + 1) + [IN_HBM, IN_HBM, IN_VMEM],
        out_specs=(IN_VMEM, IN_HBM, IN_VMEM),
        input_output_aliases={PIECES + 1: 1},
        compiler_params=params(8),
    )(a, *b, passed, after, ids)


def centre_kernel(in_ref, *rest):
    out_ref = rest[-1]
    whole = in_ref[0]
    for k in range(1, in_ref.shape[0]):
        whole += in_ref[k]
    spread = jnp.where(eye(QUARTER, HDIM), whole[QUARTER : QUARTER + 1, :], 0.0)
    count = jnp.sum(spread, axis=1, keepdims=True)
    centre = (whole[:QUARTER] / count).astype(BF16)
    for k in range(out_ref.shape[0]):
        out_ref[k] = centre


def centre_of(totals, after):
    return pl.pallas_call(
        centre_kernel,
        out_shape=jax.ShapeDtypeStruct((totals.shape[0], QUARTER, HDIM), BF16),
        in_specs=[IN_VMEM] + [ANYWHERE] * len(after),
        out_specs=IN_VMEM,
        compiler_params=params(8),
    )(totals, *after)


def attention_kernel(groups, side_ref, centre_ref, *rest):
    ids_refs, sources = rest[:groups], rest[groups : groups + 4]
    out_ref, ids_out_ref, held, arrived, copied = rest[groups + 4 :]
    first = side_ref[0] * HALF

    def fetch(k):
        source = sources[k]
        if k % 2 == 0:
            source = source.at[:, pl.ds(pl.multiple_of(first * HDIM, HALF * HDIM), HALF * HDIM)]
        return pltpu.make_async_copy(source, held.at[k], arrived.at[k])

    for k in range(2):
        fetch(k).start()
    copies = [
        pltpu.make_async_copy(ids_refs[d], ids_out_ref.at[d], copied.at[d]) for d in range(groups)
    ]
    for copy in copies:
        copy.start()
    ones = jnp.ones((held.shape[1], HDIM), BF16)
    diagonal = eye(QUARTER, HDIM)
    line = lax.broadcasted_iota(jnp.int32, (TAIL, HDIM), 0)
    for i in range(HALF):
        if i == 0:
            for k in range(2):
                fetch(k).wait()
            for k in range(2, 4):
                fetch(k).start()
        cols = slice(i * HDIM, (i + 1) * HDIM)
        centre = centre_ref[i]
        own = lax.dot_general(centre, held[0, :, cols], NT, preferred_element_type=F32)
        other = lax.dot_general(centre, held[1, :, cols], NT, preferred_element_type=F32)
        peak = jnp.maximum(
            jnp.max(own, axis=1, keepdims=True), jnp.max(other, axis=1, keepdims=True)
        )
        own_w = jnp.exp2((own - peak) * LOG2_SCALE).astype(BF16)
        other_w = jnp.exp2((other - peak) * LOG2_SCALE).astype(BF16)
        if i == 0:
            for k in range(2, 4):
                fetch(k).wait()
        both = jnp.dot(
            own_w, jnp.concatenate([held[2, :, cols], ones], axis=1), preferred_element_type=F32
        ) + jnp.dot(
            other_w, jnp.concatenate([held[3, :, cols], ones], axis=1), preferred_element_type=F32
        )
        mass = both[:, HDIM:]
        part = (both[:, :HDIM] / mass).astype(BF16)
        level = peak * LOG2_SCALE + jnp.log2(mass)
        for k in range(4):
            lines = slice(k * QUARTER, (k + 1) * QUARTER)
            row = jnp.sum(jnp.where(diagonal, level[lines], 0.0), axis=0, keepdims=True)
            high = row.astype(BF16).astype(F32)
            mid = (row - high).astype(BF16).astype(F32)
            low = row - high - mid
            tail = jnp.where(
                line == 0, high, jnp.where(line == 1, mid, jnp.where(line == 2, low, 0.0))
            )
            out_ref[i * 4 + k, :QUARTER, :] = part[lines]
            out_ref[i * 4 + k, QUARTER:, :] = tail.astype(BF16)
    for copy in copies:
        copy.wait()


def attention_of(side, centre, all_ids, keys, keys_other, values, values_other):
    rows = keys.shape[0]
    groups = len(all_ids)
    return pl.pallas_call(
        functools.partial(attention_kernel, groups),
        out_shape=(
            jax.ShapeDtypeStruct((4 * HALF, QUARTER + TAIL, HDIM), BF16),
            jax.ShapeDtypeStruct((groups, *all_ids[0].shape), jnp.int32),
        ),
        in_specs=[SCALARS, IN_VMEM] + [IN_HBM] * (groups + 4),
        out_specs=(IN_VMEM, IN_VMEM),
        scratch_shapes=[
            pltpu.VMEM((4, rows, HALF * HDIM), BF16),
            pltpu.SemaphoreType.DMA((4,)),
            pltpu.SemaphoreType.DMA((groups,)),
        ],
        compiler_params=params(52),
    )(side, centre, *all_ids, keys, keys_other, values, values_other)


def combine_kernel(in_ref, out_ref):
    count = in_ref.shape[0]
    tails = [in_ref[k, QUARTER:, :].astype(F32) for k in range(count)]
    levels = [t[0:1] + t[1:2] + t[2:3] for t in tails]
    top = functools.reduce(jnp.maximum, levels)
    shares = [jnp.exp2(level - top) for level in levels]
    mass = functools.reduce(jnp.add, shares)
    diagonal = eye(QUARTER, HDIM)
    whole = jnp.zeros((QUARTER, HDIM), F32)
    for k in range(count):
        spread = jnp.where(diagonal, shares[k] / mass, 0.0)
        share = jnp.sum(spread, axis=1, keepdims=True)
        whole += share * in_ref[k, :QUARTER, :].astype(F32)
    whole = whole.astype(BF16)
    for k in range(out_ref.shape[0]):
        out_ref[k] = whole


def rows_of(ids_row, table):
    return lax.dot_general(member_of(ids_row), table, TN, preferred_element_type=F32).astype(BF16)


def group_at(i, z_ref, groups):
    return lax.rem(z_ref[0] + groups - i, groups)


def gather_kernel(side_ref, z_ref, ids_ref, table_ref, after_ref, out_ref):
    del after_ref
    group = group_at(pl.program_id(0), z_ref, pl.num_programs(0))
    for j in range(HALF):
        row = ids_ref[pl.program_id(0), pl.ds(side_ref[0] * HALF + j, 1), :]
        out_ref[:, j * HDIM : (j + 1) * HDIM] = rows_of(row, table_ref[group * HALF + j])


def gather_of(side, z, ids, table, after):
    groups, lines, tokens = ids.shape
    return pl.pallas_call(
        gather_kernel,
        out_shape=jax.ShapeDtypeStruct((groups, tokens, HALF * HDIM), BF16),
        grid=(groups,),
        in_specs=[SCALARS, SCALARS, IN_VMEM, IN_VMEM, IN_HBM],
        out_specs=pl.BlockSpec((None, tokens, HALF * HDIM), lambda i: (i, 0, 0)),
        compiler_params=params(51),
    )(side, z, ids, table, after)


def project_kernel(
    side_ref, z_ref, near_ref, ids_ref, table_ref, w_ref, out_ref, held, rows_ref, arrived, come
):
    groups, blocks = w_ref.shape[:2]
    half = HALF * HDIM
    depth = 2 * half
    width = out_ref.shape[1] // 2
    own = pl.multiple_of(side_ref[0] * half, half)
    other = pl.multiple_of(half - side_ref[0] * half, half)

    def fetch(i):
        entry = lax.rem(z_ref[0] + i, groups)
        return pltpu.make_async_copy(w_ref.at[entry], held.at[i], arrived.at[i])

    def bring(i):
        target = rows_ref.at[:, pl.ds(i * depth + own, half)]
        return pltpu.make_async_copy(near_ref.at[i], target, come.at[i])

    for i in range(groups):
        bring(i).start()
        fetch(i).start()

    @pl.loop(0, groups)
    def _(i):
        group = group_at(i, z_ref, groups)
        for j in range(HALF):
            row = ids_ref[i, pl.ds((1 - side_ref[0]) * HALF + j, 1), :]
            start = pl.multiple_of(i * depth + other + j * HDIM, HDIM)
            rows_ref[:, pl.ds(start, HDIM)] = rows_of(row, table_ref[group * HALF + j])

    for i in range(groups):
        bring(i).wait()
        fetch(i).wait()

    @pl.loop(0, 2)
    def _(b):
        each = blocks // 2
        weight = jnp.concatenate(
            [
                jnp.concatenate([held[i, b * each + k] for k in range(each)], axis=1)
                for i in range(groups)
            ],
            axis=0,
        )
        cols = pl.ds(pl.multiple_of(b * width, width), width)
        tall = out_ref.shape[0] // 2
        for m in range(2):
            lines = slice(m * tall, (m + 1) * tall)
            product = jnp.dot(rows_ref[lines, :], weight, preferred_element_type=F32)
            out_ref[lines, cols] = product.astype(BF16)


def project_of(side, z, near, ids, table, weight):
    groups, lines, tokens = ids.shape
    blocks, depth, width = weight.shape[1:]
    return pl.pallas_call(
        project_kernel,
        out_shape=jax.ShapeDtypeStruct((tokens, blocks * width), BF16),
        in_specs=[SCALARS, SCALARS, IN_HBM, IN_VMEM, IN_VMEM, IN_HBM],
        out_specs=IN_VMEM,
        scratch_shapes=[
            pltpu.VMEM(weight.shape, BF16),
            pltpu.VMEM((tokens, groups * depth), BF16),
            pltpu.SemaphoreType.DMA((groups,)),
            pltpu.SemaphoreType.DMA((groups,)),
        ],
        compiler_params=params(51),
    )(side, z, near, ids, table, weight)


def other_core(value):
    return lax.ppermute(value, "c", [(0, 1), (1, 0)])


def exchanged(value, axes):
    return lax.all_to_all(value, axes, split_axis=0, concat_axis=0, tiled=True)


def from_all_groups(value):
    size = lax.axis_size("z")
    found = [value]
    for d in range(1, size):
        found.append(lax.ppermute(value, "z", [(i, (i + d) % size) for i in range(size)]))
    return found


def local(queries, keys, values, cluster_ids, out_weight):
    core = lax.axis_index("c").astype(jnp.int32)
    side = core[None]
    z = lax.axis_index("z").astype(jnp.int32)[None]
    ids = cluster_ids.T
    size = lax.axis_size("z")
    turned = [
        (x * size + z, (2 * x - z) % size * size + x) for x in range(size) for z in range(size)
    ]
    turned_weight = lax.ppermute(out_weight, ("x", "z"), turned)

    *theirs, mine = totals_of(side, ids, queries)
    arrived = [other_core(piece) for piece in theirs]
    keys_far, values_far, token = halves_of(side, theirs[0], keys, values)
    keys_other, values_other = other_core(keys_far), other_core(values_far)
    totals, turned_weight, ids = add_after(mine, arrived, turned_weight, token, ids)
    weight = lax.all_gather(turned_weight, SEQ, axis=0)
    weight = weight.reshape(size, -1, *weight.shape[1:])
    all_ids = from_all_groups(ids)
    centre = centre_of(exchanged(totals, PLANE), all_ids[1:])
    centre = exchanged(centre, PLANE).reshape(HALF, CLUSTERS, HDIM)
    parts, all_ids = attention_of(
        side, centre, all_ids, keys, keys_other, values, values_other
    )
    parts = exchanged(parts, PLANE)
    table = pl.pallas_call(
        combine_kernel,
        out_shape=jax.ShapeDtypeStruct((lax.axis_size(CUBE), QUARTER, HDIM), BF16),
        compiler_params=params(8),
    )(parts)
    table = exchanged(table, CUBE).reshape(size * HALF, CLUSTERS, HDIM)
    far_table = other_core(table)
    near = gather_of(side, z, all_ids, table, weight)
    return project_of(side, z, near, all_ids, far_table, weight)


def solution(mesh):
    head = mesh.shape["head"]
    finer = Mesh(mesh.devices.reshape(4, 4, 2, head), ("x", "y", "c", "z"))
    in_specs = (P(SEQ, "z"), P(SEQ, "z"), P(SEQ, "z"), P(SEQ, "z"), P("z", SEQ))
    return jax.shard_map(
        local, mesh=finer, in_specs=in_specs, out_specs=P(SEQ, "z"), check_vma=False
    )
```

```python
import functools
import math

import jax
import jax.numpy as jnp
from jax import lax
from jax.experimental import pallas as pl
from jax.experimental.pallas import tpu as pltpu
from jax.sharding import Mesh
from jax.sharding import PartitionSpec as P

HDIM = 128
CLUSTERS = 256
PIECES = 4
HALF = 4
QUARTER = CLUSTERS // 4
SEQ = ("x", "y", "c")
PLANE = ("x", "y")
CUBE = ("z", "x", "y")
EXTRA = 8
TAIL = 16
LARGE = 61
LOG2_SCALE = math.log2(math.e) / math.sqrt(HDIM)
F32 = jnp.float32
BF16 = jnp.bfloat16
NT = (((1,), (1,)), ((), ()))
TN = (((0,), (0,)), ((), ()))


def params(mib):
    return pltpu.CompilerParams(vmem_limit_bytes=mib * 2**20)


def eye(rows, cols):
    r = lax.broadcasted_iota(jnp.int32, (rows, cols), 0)
    c = lax.broadcasted_iota(jnp.int32, (rows, cols), 1)
    return r == c


def member_of(row):
    labels = lax.broadcasted_iota(jnp.int32, (CLUSTERS, row.shape[1]), 0)
    return (labels == row).astype(F32).astype(BF16)


def totals_kernel(side_ref, ids_ref, q_ref, *rest):
    theirs_refs, (mine_ref, held, arrived) = rest[:PIECES], rest[PIECES:]
    each = HALF // PIECES
    rows = q_ref.shape[0]
    firsts = (HALF - side_ref[0] * HALF, side_ref[0] * HALF)

    def fetch(k):
        start = pl.multiple_of(firsts[k] * HDIM, HALF * HDIM)
        return pltpu.make_async_copy(
            q_ref.at[:, pl.ds(start, HALF * HDIM)], held.at[k], arrived.at[k]
        )

    for k in range(2):
        fetch(k).start()
    ones = jnp.ones((rows, HDIM), BF16)
    diagonal = eye(QUARTER, HDIM)
    for k in range(2):
        fetch(k).wait()
        for i in range(HALF):
            out_ref, base = (mine_ref, i * 4) if k else (theirs_refs[i // each], i % each * 4)
            member = member_of(ids_ref[pl.ds(firsts[k] + i, 1), :])
            query = held[k, :, i * HDIM : (i + 1) * HDIM]
            both = jnp.dot(
                member, jnp.concatenate([query, ones], axis=1), preferred_element_type=F32
            )
            for q in range(4):
                lines = slice(q * QUARTER, (q + 1) * QUARTER)
                count = jnp.sum(
                    jnp.where(diagonal, both[lines, HDIM:], 0.0), axis=0, keepdims=True
                )
                out_ref[base + q, :QUARTER, :] = both[lines, :HDIM]
                out_ref[base + q, QUARTER:, :] = jnp.broadcast_to(count, (EXTRA, HDIM))


SCALARS = pl.BlockSpec(memory_space=pltpu.SMEM)
IN_VMEM = pl.BlockSpec(memory_space=pltpu.VMEM)
ANYWHERE = pl.BlockSpec(memory_space=pl.ANY)
IN_HBM = pl.BlockSpec(memory_space=pltpu.HBM)


def totals_of(side, ids, queries):
    rows = queries.shape[0]
    return pl.pallas_call(
        totals_kernel,
        out_shape=[
            jax.ShapeDtypeStruct((4 * HALF // PIECES, QUARTER + EXTRA, HDIM), F32),
        ]
        * PIECES
        + [jax.ShapeDtypeStruct((4 * HALF, QUARTER + EXTRA, HDIM), F32)],
        in_specs=[SCALARS, IN_VMEM, IN_HBM],
        out_specs=[IN_VMEM] * (PIECES + 1),
        scratch_shapes=[
            pltpu.VMEM((2, rows, HALF * HDIM), BF16),
            pltpu.SemaphoreType.DMA((2,)),
        ],
        compiler_params=params(58),
    )(side, ids, queries)


def halves_kernel(
    side_ref, after_ref, k_ref, v_ref, k_out_ref, v_out_ref, token_ref, held, come, gone
):
    del after_ref
    token_ref[0] = side_ref[0]
    start = pl.multiple_of((1 - side_ref[0]) * HALF * HDIM, HALF * HDIM)

    def fetch(k, source):
        return pltpu.make_async_copy(
            source.at[:, pl.ds(start, HALF * HDIM)], held.at[k], come.at[k]
        )

    def put(k, target):
        return pltpu.make_async_copy(held.at[k], target, gone.at[k])

    fetch(0, k_ref).start()
    fetch(1, v_ref).start()
    fetch(0, k_ref).wait()
    put(0, k_out_ref).start()
    fetch(1, v_ref).wait()
    put(1, v_out_ref).start()
    put(0, k_out_ref).wait()
    put(1, v_out_ref).wait()


def halves_of(side, after, keys, values):
    half = jax.ShapeDtypeStruct((keys.shape[0], HALF * HDIM), BF16)
    return pl.pallas_call(
        halves_kernel,
        out_shape=(half, half, jax.ShapeDtypeStruct((1,), jnp.int32)),
        in_specs=[SCALARS, IN_HBM, IN_HBM, IN_HBM],
        out_specs=(IN_HBM, IN_HBM, SCALARS),
        scratch_shapes=[
            pltpu.VMEM((2, *half.shape), BF16),
            pltpu.SemaphoreType.DMA((2,)),
            pltpu.SemaphoreType.DMA((2,)),
        ],
        compiler_params=params(LARGE),
    )(side, after, keys, values)


def add_kernel(a_ref, *rest):
    ids_ref, out_ref, ids_out_ref = rest[PIECES + 1], rest[PIECES + 3], rest[PIECES + 5]
    ids_out_ref[...] = ids_ref[...]
    size = a_ref.shape[0] // PIECES
    for k in range(PIECES):
        lines = slice(k * size, (k + 1) * size)
        out_ref[lines] = a_ref[lines] + rest[k][...]


def add_after(a, b, passed, ids, after):
    return pl.pallas_call(
        add_kernel,
        out_shape=(
            jax.ShapeDtypeStruct(a.shape, a.dtype),
            jax.ShapeDtypeStruct(passed.shape, passed.dtype),
            jax.ShapeDtypeStruct(ids.shape, ids.dtype),
        ),
        in_specs=[IN_VMEM] * (PIECES + 1) + [IN_HBM, IN_VMEM, SCALARS],
        out_specs=(IN_VMEM, IN_HBM, IN_VMEM),
        input_output_aliases={PIECES + 1: 1},
        compiler_params=params(8),
    )(a, *b, passed, ids, after)


def centre_kernel(in_ref, *rest):
    out_ref = rest[-2]
    whole = in_ref[0]
    for k in range(1, in_ref.shape[0]):
        whole += in_ref[k]
    spread = jnp.where(eye(QUARTER, HDIM), whole[QUARTER : QUARTER + 1, :], 0.0)
    count = jnp.sum(spread, axis=1, keepdims=True)
    centre = (whole[:QUARTER] / count).astype(BF16)
    for k in range(out_ref.shape[0]):
        out_ref[k] = centre


def centre_of(totals, after, passed):
    return pl.pallas_call(
        centre_kernel,
        out_shape=(
            jax.ShapeDtypeStruct((totals.shape[0], QUARTER, HDIM), BF16),
            jax.ShapeDtypeStruct(passed.shape, passed.dtype),
        ),
        in_specs=[IN_VMEM] + [ANYWHERE] * len(after) + [IN_HBM],
        out_specs=(IN_VMEM, IN_HBM),
        input_output_aliases={1 + len(after): 1},
        compiler_params=params(8),
    )(totals, *after, passed)


def attention_kernel(groups, side_ref, centre_ref, *rest):
    ids_refs, sources = rest[:groups], rest[groups : groups + 4]
    out_ref, ids_out_ref, held, arrived, copied = rest[groups + 4 :]
    first = side_ref[0] * HALF

    def fetch(k):
        source = sources[k]
        if k % 2 == 0:
            source = source.at[:, pl.ds(pl.multiple_of(first * HDIM, HALF * HDIM), HALF * HDIM)]
        return pltpu.make_async_copy(source, held.at[k], arrived.at[k])

    for k in range(2):
        fetch(k).start()
    copies = [
        pltpu.make_async_copy(ids_refs[d], ids_out_ref.at[d], copied.at[d]) for d in range(groups)
    ]
    for copy in copies:
        copy.start()
    ones = jnp.ones((held.shape[1], HDIM), BF16)
    diagonal = eye(QUARTER, HDIM)
    line = lax.broadcasted_iota(jnp.int32, (TAIL, HDIM), 0)
    for i in range(HALF):
        if i == 0:
            for k in range(2):
                fetch(k).wait()
            for k in range(2, 4):
                fetch(k).start()
        cols = slice(i * HDIM, (i + 1) * HDIM)
        centre = centre_ref[i]
        own = lax.dot_general(centre, held[0, :, cols], NT, preferred_element_type=F32)
        other = lax.dot_general(centre, held[1, :, cols], NT, preferred_element_type=F32)
        peak = jnp.maximum(
            jnp.max(own, axis=1, keepdims=True), jnp.max(other, axis=1, keepdims=True)
        )
        own_w = jnp.exp2((own - peak) * LOG2_SCALE).astype(BF16)
        other_w = jnp.exp2((other - peak) * LOG2_SCALE).astype(BF16)
        if i == 0:
            for k in range(2, 4):
                fetch(k).wait()
        both = jnp.dot(
            own_w, jnp.concatenate([held[2, :, cols], ones], axis=1), preferred_element_type=F32
        ) + jnp.dot(
            other_w, jnp.concatenate([held[3, :, cols], ones], axis=1), preferred_element_type=F32
        )
        mass = both[:, HDIM:]
        part = (both[:, :HDIM] / mass).astype(BF16)
        level = peak * LOG2_SCALE + jnp.log2(mass)
        for k in range(4):
            lines = slice(k * QUARTER, (k + 1) * QUARTER)
            row = jnp.sum(jnp.where(diagonal, level[lines], 0.0), axis=0, keepdims=True)
            high = row.astype(BF16).astype(F32)
            mid = (row - high).astype(BF16).astype(F32)
            low = row - high - mid
            tail = jnp.where(
                line == 0, high, jnp.where(line == 1, mid, jnp.where(line == 2, low, 0.0))
            )
            out_ref[i * 4 + k, :QUARTER, :] = part[lines]
            out_ref[i * 4 + k, QUARTER:, :] = tail.astype(BF16)
    for copy in copies:
        copy.wait()


def attention_of(side, centre, all_ids, keys, keys_other, values, values_other):
    rows = keys.shape[0]
    groups = len(all_ids)
    return pl.pallas_call(
        functools.partial(attention_kernel, groups),
        out_shape=(
            jax.ShapeDtypeStruct((4 * HALF, QUARTER + TAIL, HDIM), BF16),
            jax.ShapeDtypeStruct((groups, *all_ids[0].shape), jnp.int32),
        ),
        in_specs=[SCALARS, IN_VMEM] + [IN_HBM] * (groups + 4),
        out_specs=(IN_VMEM, IN_VMEM),
        scratch_shapes=[
            pltpu.VMEM((4, rows, HALF * HDIM), BF16),
            pltpu.SemaphoreType.DMA((4,)),
            pltpu.SemaphoreType.DMA((groups,)),
        ],
        compiler_params=params(52),
    )(side, centre, *all_ids, keys, keys_other, values, values_other)


def combine_kernel(in_ref, out_ref):
    count = in_ref.shape[0]
    tails = [in_ref[k, QUARTER:, :].astype(F32) for k in range(count)]
    levels = [t[0:1] + t[1:2] + t[2:3] for t in tails]
    top = functools.reduce(jnp.maximum, levels)
    shares = [jnp.exp2(level - top) for level in levels]
    mass = functools.reduce(jnp.add, shares)
    diagonal = eye(QUARTER, HDIM)
    whole = jnp.zeros((QUARTER, HDIM), F32)
    for k in range(count):
        spread = jnp.where(diagonal, shares[k] / mass, 0.0)
        share = jnp.sum(spread, axis=1, keepdims=True)
        whole += share * in_ref[k, :QUARTER, :].astype(F32)
    whole = whole.astype(BF16)
    for k in range(out_ref.shape[0]):
        out_ref[k] = whole


def rows_of(ids_row, table):
    return lax.dot_general(member_of(ids_row), table, TN, preferred_element_type=F32).astype(BF16)


def group_at(i, z_ref, groups):
    return lax.rem(z_ref[0] + groups - i, groups)


def gather_kernel(side_ref, z_ref, ids_ref, table_ref, after_ref, out_ref):
    del after_ref
    group = group_at(pl.program_id(0), z_ref, pl.num_programs(0))
    for j in range(HALF):
        row = ids_ref[pl.program_id(0), pl.ds(side_ref[0] * HALF + j, 1), :]
        out_ref[:, j * HDIM : (j + 1) * HDIM] = rows_of(row, table_ref[group * HALF + j])


def gather_of(side, z, ids, table, after):
    groups, lines, tokens = ids.shape
    return pl.pallas_call(
        gather_kernel,
        out_shape=jax.ShapeDtypeStruct((groups, tokens, HALF * HDIM), BF16),
        grid=(groups,),
        in_specs=[SCALARS, SCALARS, IN_VMEM, IN_VMEM, IN_HBM],
        out_specs=pl.BlockSpec((None, tokens, HALF * HDIM), lambda i: (i, 0, 0)),
        compiler_params=params(51),
    )(side, z, ids, table, after)


def project_kernel(
    side_ref, z_ref, near_ref, ids_ref, table_ref, w_ref, out_ref, held, rows_ref, arrived, come
):
    groups, blocks = w_ref.shape[:2]
    half = HALF * HDIM
    depth = 2 * half
    width = out_ref.shape[1] // 2
    own = pl.multiple_of(side_ref[0] * half, half)
    other = pl.multiple_of(half - side_ref[0] * half, half)

    def fetch(i):
        entry = lax.rem(z_ref[0] + i, groups)
        return pltpu.make_async_copy(w_ref.at[entry], held.at[i], arrived.at[i])

    def bring(i):
        target = rows_ref.at[:, pl.ds(i * depth + own, half)]
        return pltpu.make_async_copy(near_ref.at[i], target, come.at[i])

    for i in range(groups):
        bring(i).start()
        fetch(i).start()

    @pl.loop(0, groups)
    def _(i):
        group = group_at(i, z_ref, groups)
        for j in range(HALF):
            row = ids_ref[i, pl.ds((1 - side_ref[0]) * HALF + j, 1), :]
            start = pl.multiple_of(i * depth + other + j * HDIM, HDIM)
            rows_ref[:, pl.ds(start, HDIM)] = rows_of(row, table_ref[group * HALF + j])

    for i in range(groups):
        bring(i).wait()
        fetch(i).wait()

    @pl.loop(0, 2)
    def _(b):
        each = blocks // 2
        weight = jnp.concatenate(
            [
                jnp.concatenate([held[i, b * each + k] for k in range(each)], axis=1)
                for i in range(groups)
            ],
            axis=0,
        )
        cols = pl.ds(pl.multiple_of(b * width, width), width)
        tall = out_ref.shape[0] // 2
        for m in range(2):
            lines = slice(m * tall, (m + 1) * tall)
            product = jnp.dot(rows_ref[lines, :], weight, preferred_element_type=F32)
            out_ref[lines, cols] = product.astype(BF16)


def project_of(side, z, near, ids, table, weight):
    groups, lines, tokens = ids.shape
    blocks, depth, width = weight.shape[1:]
    return pl.pallas_call(
        project_kernel,
        out_shape=jax.ShapeDtypeStruct((tokens, blocks * width), BF16),
        in_specs=[SCALARS, SCALARS, IN_HBM, IN_VMEM, IN_VMEM, IN_HBM],
        out_specs=IN_VMEM,
        scratch_shapes=[
            pltpu.VMEM(weight.shape, BF16),
            pltpu.VMEM((tokens, groups * depth), BF16),
            pltpu.SemaphoreType.DMA((groups,)),
            pltpu.SemaphoreType.DMA((groups,)),
        ],
        compiler_params=params(51),
    )(side, z, near, ids, table, weight)


def other_core(value):
    return lax.ppermute(value, "c", [(0, 1), (1, 0)])


def exchanged(value, axes):
    return lax.all_to_all(value, axes, split_axis=0, concat_axis=0, tiled=True)


def from_all_groups(value):
    size = lax.axis_size("z")
    found = [value]
    for d in range(1, size):
        found.append(lax.ppermute(value, "z", [(i, (i + d) % size) for i in range(size)]))
    return found


def local(queries, keys, values, cluster_ids, out_weight):
    core = lax.axis_index("c").astype(jnp.int32)
    side = core[None]
    z = lax.axis_index("z").astype(jnp.int32)[None]
    ids = cluster_ids.T
    size = lax.axis_size("z")
    turned = [
        (x * size + z, (2 * x - z) % size * size + x) for x in range(size) for z in range(size)
    ]
    turned_weight = lax.ppermute(out_weight, ("x", "z"), turned)

    *theirs, mine = totals_of(side, ids, queries)
    arrived = [other_core(piece) for piece in theirs]
    keys_far, values_far, token = halves_of(side, mine, keys, values)
    keys_other, values_other = other_core(keys_far), other_core(values_far)
    totals, turned_weight, ids = add_after(mine, arrived, turned_weight, ids, token)
    all_ids = from_all_groups(ids)
    centre, turned_weight = centre_of(exchanged(totals, PLANE), all_ids[1:], turned_weight)
    weight = lax.all_gather(turned_weight, SEQ, axis=0)
    weight = weight.reshape(size, -1, *weight.shape[1:])
    centre = exchanged(centre, PLANE).reshape(HALF, CLUSTERS, HDIM)
    parts, all_ids = attention_of(
        side, centre, all_ids, keys, keys_other, values, values_other
    )
    parts = exchanged(parts, PLANE)
    table = pl.pallas_call(
        combine_kernel,
        out_shape=jax.ShapeDtypeStruct((lax.axis_size(CUBE), QUARTER, HDIM), BF16),
        compiler_params=params(8),
    )(parts)
    table = exchanged(table, CUBE).reshape(size * HALF, CLUSTERS, HDIM)
    far_table = other_core(table)
    near = gather_of(side, z, all_ids, table, weight)
    return project_of(side, z, near, all_ids, far_table, weight)


def solution(mesh):
    head = mesh.shape["head"]
    finer = Mesh(mesh.devices.reshape(4, 4, 2, head), ("x", "y", "c", "z"))
    in_specs = (P(SEQ, "z"), P(SEQ, "z"), P(SEQ, "z"), P(SEQ, "z"), P("z", SEQ))
    return jax.shard_map(
        local, mesh=finer, in_specs=in_specs, out_specs=P(SEQ, "z"), check_vma=False
    )
```

```python
import functools
import math

import jax
import jax.numpy as jnp
from jax import lax
from jax.experimental import pallas as pl
from jax.experimental.pallas import tpu as pltpu
from jax.sharding import Mesh
from jax.sharding import PartitionSpec as P

HDIM = 128
CLUSTERS = 256
PIECES = 4
HALF = 4
QUARTER = CLUSTERS // 4
SEQ = ("x", "y", "c")
PLANE = ("x", "y")
CUBE = ("z", "x", "y")
EXTRA = 8
TAIL = 16
LARGE = 61
LOG2_SCALE = math.log2(math.e) / math.sqrt(HDIM)
F32 = jnp.float32
BF16 = jnp.bfloat16
NT = (((1,), (1,)), ((), ()))
TN = (((0,), (0,)), ((), ()))


def params(mib):
    return pltpu.CompilerParams(vmem_limit_bytes=mib * 2**20)


def eye(rows, cols):
    r = lax.broadcasted_iota(jnp.int32, (rows, cols), 0)
    c = lax.broadcasted_iota(jnp.int32, (rows, cols), 1)
    return r == c


def member_of(row):
    labels = lax.broadcasted_iota(jnp.int32, (CLUSTERS, row.shape[1]), 0)
    return (labels == row).astype(F32).astype(BF16)


def totals_kernel(side_ref, ids_ref, q_ref, *rest):
    theirs_refs, (mine_ref, held, arrived) = rest[:PIECES], rest[PIECES:]
    each = HALF // PIECES
    rows = q_ref.shape[0]
    firsts = (HALF - side_ref[0] * HALF, side_ref[0] * HALF)

    def fetch(k):
        start = pl.multiple_of(firsts[k] * HDIM, HALF * HDIM)
        return pltpu.make_async_copy(
            q_ref.at[:, pl.ds(start, HALF * HDIM)], held.at[k], arrived.at[k]
        )

    for k in range(2):
        fetch(k).start()
    ones = jnp.ones((rows, HDIM), BF16)
    diagonal = eye(QUARTER, HDIM)
    for k in range(2):
        fetch(k).wait()
        for i in range(HALF):
            out_ref, base = (mine_ref, i * 4) if k else (theirs_refs[i // each], i % each * 4)
            member = member_of(ids_ref[pl.ds(firsts[k] + i, 1), :])
            query = held[k, :, i * HDIM : (i + 1) * HDIM]
            both = jnp.dot(
                member, jnp.concatenate([query, ones], axis=1), preferred_element_type=F32
            )
            for q in range(4):
                lines = slice(q * QUARTER, (q + 1) * QUARTER)
                count = jnp.sum(
                    jnp.where(diagonal, both[lines, HDIM:], 0.0), axis=0, keepdims=True
                )
                out_ref[base + q, :QUARTER, :] = both[lines, :HDIM]
                out_ref[base + q, QUARTER:, :] = jnp.broadcast_to(count, (EXTRA, HDIM))


SCALARS = pl.BlockSpec(memory_space=pltpu.SMEM)
IN_VMEM = pl.BlockSpec(memory_space=pltpu.VMEM)
ANYWHERE = pl.BlockSpec(memory_space=pl.ANY)
IN_HBM = pl.BlockSpec(memory_space=pltpu.HBM)


def totals_of(side, ids, queries):
    rows = queries.shape[0]
    return pl.pallas_call(
        totals_kernel,
        out_shape=[
            jax.ShapeDtypeStruct((4 * HALF // PIECES, QUARTER + EXTRA, HDIM), F32),
        ]
        * PIECES
        + [jax.ShapeDtypeStruct((4 * HALF, QUARTER + EXTRA, HDIM), F32)],
        in_specs=[SCALARS, IN_VMEM, IN_HBM],
        out_specs=[IN_VMEM] * (PIECES + 1),
        scratch_shapes=[
            pltpu.VMEM((2, rows, HALF * HDIM), BF16),
            pltpu.SemaphoreType.DMA((2,)),
        ],
        compiler_params=params(58),
    )(side, ids, queries)


def halves_kernel(
    side_ref, after_ref, k_ref, v_ref, k_out_ref, v_out_ref, token_ref, held, come, gone
):
    del after_ref
    token_ref[0] = side_ref[0]
    start = pl.multiple_of((1 - side_ref[0]) * HALF * HDIM, HALF * HDIM)

    def fetch(k, source):
        return pltpu.make_async_copy(
            source.at[:, pl.ds(start, HALF * HDIM)], held.at[k], come.at[k]
        )

    def put(k, target):
        return pltpu.make_async_copy(held.at[k], target, gone.at[k])

    fetch(0, k_ref).start()
    fetch(1, v_ref).start()
    fetch(0, k_ref).wait()
    put(0, k_out_ref).start()
    fetch(1, v_ref).wait()
    put(1, v_out_ref).start()
    put(0, k_out_ref).wait()
    put(1, v_out_ref).wait()


def halves_of(side, after, keys, values):
    half = jax.ShapeDtypeStruct((keys.shape[0], HALF * HDIM), BF16)
    return pl.pallas_call(
        halves_kernel,
        out_shape=(half, half, jax.ShapeDtypeStruct((1,), jnp.int32)),
        in_specs=[SCALARS, IN_HBM, IN_HBM, IN_HBM],
        out_specs=(IN_HBM, IN_HBM, SCALARS),
        scratch_shapes=[
            pltpu.VMEM((2, *half.shape), BF16),
            pltpu.SemaphoreType.DMA((2,)),
            pltpu.SemaphoreType.DMA((2,)),
        ],
        compiler_params=params(LARGE),
    )(side, after, keys, values)


def add_kernel(a_ref, *rest):
    ids_ref, out_ref, ids_out_ref = rest[PIECES + 1], rest[PIECES + 3], rest[PIECES + 5]
    ids_out_ref[...] = ids_ref[...]
    size = a_ref.shape[0] // PIECES
    for k in range(PIECES):
        lines = slice(k * size, (k + 1) * size)
        out_ref[lines] = a_ref[lines] + rest[k][...]


def add_after(a, b, passed, ids, after):
    return pl.pallas_call(
        add_kernel,
        out_shape=(
            jax.ShapeDtypeStruct(a.shape, a.dtype),
            jax.ShapeDtypeStruct(passed.shape, passed.dtype),
            jax.ShapeDtypeStruct(ids.shape, ids.dtype),
        ),
        in_specs=[IN_VMEM] * (PIECES + 1) + [IN_HBM, IN_VMEM, SCALARS],
        out_specs=(IN_VMEM, IN_HBM, IN_VMEM),
        input_output_aliases={PIECES + 1: 1},
        compiler_params=params(8),
    )(a, *b, passed, ids, after)


def centre_kernel(in_ref, *rest):
    out_ref = rest[-1]
    whole = in_ref[0]
    for k in range(1, in_ref.shape[0]):
        whole += in_ref[k]
    spread = jnp.where(eye(QUARTER, HDIM), whole[QUARTER : QUARTER + 1, :], 0.0)
    count = jnp.sum(spread, axis=1, keepdims=True)
    centre = (whole[:QUARTER] / count).astype(BF16)
    for k in range(out_ref.shape[0]):
        out_ref[k] = centre


def centre_of(totals, after):
    return pl.pallas_call(
        centre_kernel,
        out_shape=jax.ShapeDtypeStruct((totals.shape[0], QUARTER, HDIM), BF16),
        in_specs=[IN_VMEM] + [ANYWHERE] * len(after),
        out_specs=IN_VMEM,
        compiler_params=params(8),
    )(totals, *after)


def attention_kernel(groups, side_ref, centre_ref, *rest):
    ids_refs, sources = rest[:groups], rest[groups : groups + 4]
    out_ref, ids_out_ref, held, arrived, copied = rest[groups + 4 :]
    first = side_ref[0] * HALF

    def fetch(k):
        source = sources[k]
        if k % 2 == 0:
            source = source.at[:, pl.ds(pl.multiple_of(first * HDIM, HALF * HDIM), HALF * HDIM)]
        return pltpu.make_async_copy(source, held.at[k], arrived.at[k])

    for k in range(2):
        fetch(k).start()
    copies = [
        pltpu.make_async_copy(ids_refs[d], ids_out_ref.at[d], copied.at[d]) for d in range(groups)
    ]
    for copy in copies:
        copy.start()
    ones = jnp.ones((held.shape[1], HDIM), BF16)
    diagonal = eye(QUARTER, HDIM)
    line = lax.broadcasted_iota(jnp.int32, (TAIL, HDIM), 0)
    for i in range(HALF):
        if i == 0:
            for k in range(2):
                fetch(k).wait()
            for k in range(2, 4):
                fetch(k).start()
        cols = slice(i * HDIM, (i + 1) * HDIM)
        centre = centre_ref[i]
        own = lax.dot_general(centre, held[0, :, cols], NT, preferred_element_type=F32)
        other = lax.dot_general(centre, held[1, :, cols], NT, preferred_element_type=F32)
        peak = jnp.maximum(
            jnp.max(own, axis=1, keepdims=True), jnp.max(other, axis=1, keepdims=True)
        )
        own_w = jnp.exp2((own - peak) * LOG2_SCALE).astype(BF16)
        other_w = jnp.exp2((other - peak) * LOG2_SCALE).astype(BF16)
        if i == 0:
            for k in range(2, 4):
                fetch(k).wait()
        both = jnp.dot(
            own_w, jnp.concatenate([held[2, :, cols], ones], axis=1), preferred_element_type=F32
        ) + jnp.dot(
            other_w, jnp.concatenate([held[3, :, cols], ones], axis=1), preferred_element_type=F32
        )
        mass = both[:, HDIM:]
        part = (both[:, :HDIM] / mass).astype(BF16)
        level = peak * LOG2_SCALE + jnp.log2(mass)
        for k in range(4):
            lines = slice(k * QUARTER, (k + 1) * QUARTER)
            row = jnp.sum(jnp.where(diagonal, level[lines], 0.0), axis=0, keepdims=True)
            high = row.astype(BF16).astype(F32)
            mid = (row - high).astype(BF16).astype(F32)
            low = row - high - mid
            tail = jnp.where(
                line == 0, high, jnp.where(line == 1, mid, jnp.where(line == 2, low, 0.0))
            )
            out_ref[i * 4 + k, :QUARTER, :] = part[lines]
            out_ref[i * 4 + k, QUARTER:, :] = tail.astype(BF16)
    for copy in copies:
        copy.wait()


def attention_of(side, centre, all_ids, keys, keys_other, values, values_other):
    rows = keys.shape[0]
    groups = len(all_ids)
    return pl.pallas_call(
        functools.partial(attention_kernel, groups),
        out_shape=(
            jax.ShapeDtypeStruct((4 * HALF, QUARTER + TAIL, HDIM), BF16),
            jax.ShapeDtypeStruct((groups, *all_ids[0].shape), jnp.int32),
        ),
        in_specs=[SCALARS, IN_VMEM] + [IN_HBM] * (groups + 4),
        out_specs=(IN_VMEM, IN_VMEM),
        scratch_shapes=[
            pltpu.VMEM((4, rows, HALF * HDIM), BF16),
            pltpu.SemaphoreType.DMA((4,)),
            pltpu.SemaphoreType.DMA((groups,)),
        ],
        compiler_params=params(52),
    )(side, centre, *all_ids, keys, keys_other, values, values_other)


def combine_kernel(in_ref, out_ref):
    count = in_ref.shape[0]
    tails = [in_ref[k, QUARTER:, :].astype(F32) for k in range(count)]
    levels = [t[0:1] + t[1:2] + t[2:3] for t in tails]
    top = functools.reduce(jnp.maximum, levels)
    shares = [jnp.exp2(level - top) for level in levels]
    mass = functools.reduce(jnp.add, shares)
    diagonal = eye(QUARTER, HDIM)
    whole = jnp.zeros((QUARTER, HDIM), F32)
    for k in range(count):
        spread = jnp.where(diagonal, shares[k] / mass, 0.0)
        share = jnp.sum(spread, axis=1, keepdims=True)
        whole += share * in_ref[k, :QUARTER, :].astype(F32)
    whole = whole.astype(BF16)
    for k in range(out_ref.shape[0]):
        out_ref[k] = whole


def columns_of(ids_row, table):
    return lax.dot_general(table, member_of(ids_row), TN, preferred_element_type=F32).astype(BF16)


def group_at(i, z_ref, groups):
    return lax.rem(z_ref[0] + groups - i, groups)


def gather_kernel(side_ref, z_ref, ids_ref, table_ref, after_ref, out_ref):
    del after_ref
    group = group_at(pl.program_id(0), z_ref, pl.num_programs(0))
    for j in range(HALF):
        row = ids_ref[pl.program_id(0), pl.ds(side_ref[0] * HALF + j, 1), :]
        out_ref[j * HDIM : (j + 1) * HDIM, :] = columns_of(row, table_ref[group * HALF + j])


def gather_of(side, z, ids, table, after):
    groups, lines, tokens = ids.shape
    return pl.pallas_call(
        gather_kernel,
        out_shape=jax.ShapeDtypeStruct((groups, HALF * HDIM, tokens), BF16),
        grid=(groups,),
        in_specs=[SCALARS, SCALARS, IN_VMEM, IN_VMEM, IN_HBM],
        out_specs=pl.BlockSpec((None, HALF * HDIM, tokens), lambda i: (i, 0, 0)),
        compiler_params=params(51),
    )(side, z, ids, table, after)


def project_kernel(
    side_ref,
    z_ref,
    near_ref,
    ids_ref,
    table_ref,
    w_ref,
    out_ref,
    held,
    columns_ref,
    done_ref,
    arrived,
    come,
    gone,
):
    groups, blocks = w_ref.shape[:2]
    half = HALF * HDIM
    depth = 2 * half
    width = out_ref.shape[1] // 2
    own = pl.multiple_of(side_ref[0] * half, half)
    other = pl.multiple_of(half - side_ref[0] * half, half)

    def fetch(i):
        entry = lax.rem(z_ref[0] + i, groups)
        return pltpu.make_async_copy(w_ref.at[entry], held.at[i], arrived.at[i])

    def bring(i):
        target = columns_ref.at[pl.ds(i * depth + own, half), :]
        return pltpu.make_async_copy(near_ref.at[i], target, come.at[i])

    for i in range(groups):
        bring(i).start()
        fetch(i).start()

    @pl.loop(0, groups)
    def _(i):
        group = group_at(i, z_ref, groups)
        for j in range(HALF):
            row = ids_ref[i, pl.ds((1 - side_ref[0]) * HALF + j, 1), :]
            start = pl.multiple_of(i * depth + other + j * HDIM, HDIM)
            columns_ref[pl.ds(start, HDIM), :] = columns_of(row, table_ref[group * HALF + j])

    def put(b):
        cols = pl.ds(pl.multiple_of(b * width, width), width)
        return pltpu.make_async_copy(done_ref.at[b], out_ref.at[:, cols], gone.at[b])

    for i in range(groups):
        bring(i).wait()
        fetch(i).wait()

    @pl.loop(0, 2)
    def _(b):
        each = blocks // 2
        weight = jnp.concatenate(
            [
                jnp.concatenate([held[i, b * each + k] for k in range(each)], axis=1)
                for i in range(groups)
            ],
            axis=0,
        )
        product = lax.dot_general(columns_ref[...], weight, TN, preferred_element_type=F32)
        done_ref[b] = product.astype(BF16)
        put(b).start()

    for b in range(2):
        put(b).wait()


def project_of(side, z, near, ids, table, weight):
    groups, lines, tokens = ids.shape
    blocks, depth, width = weight.shape[1:]
    return pl.pallas_call(
        project_kernel,
        out_shape=jax.ShapeDtypeStruct((tokens, blocks * width), BF16),
        in_specs=[SCALARS, SCALARS, IN_HBM, IN_VMEM, IN_VMEM, IN_HBM],
        out_specs=IN_HBM,
        scratch_shapes=[
            pltpu.VMEM(weight.shape, BF16),
            pltpu.VMEM((groups * depth, tokens), BF16),
            pltpu.VMEM((2, tokens, blocks * width // 2), BF16),
            pltpu.SemaphoreType.DMA((groups,)),
            pltpu.SemaphoreType.DMA((groups,)),
            pltpu.SemaphoreType.DMA((2,)),
        ],
        compiler_params=params(51),
    )(side, z, near, ids, table, weight)


def other_core(value):
    return lax.ppermute(value, "c", [(0, 1), (1, 0)])


def exchanged(value, axes):
    return lax.all_to_all(value, axes, split_axis=0, concat_axis=0, tiled=True)


def from_all_groups(value):
    size = lax.axis_size("z")
    found = [value]
    for d in range(1, size):
        found.append(lax.ppermute(value, "z", [(i, (i + d) % size) for i in range(size)]))
    return found


def local(queries, keys, values, cluster_ids, out_weight):
    core = lax.axis_index("c").astype(jnp.int32)
    side = core[None]
    z = lax.axis_index("z").astype(jnp.int32)[None]
    ids = cluster_ids.T
    size = lax.axis_size("z")
    turned = [
        (x * size + z, (2 * x - z) % size * size + x) for x in range(size) for z in range(size)
    ]
    turned_weight = lax.ppermute(out_weight, ("x", "z"), turned)

    *theirs, mine = totals_of(side, ids, queries)
    arrived = [other_core(piece) for piece in theirs]
    keys_far, values_far, token = halves_of(side, mine, keys, values)
    keys_other, values_other = other_core(keys_far), other_core(values_far)
    totals, turned_weight, ids = add_after(mine, arrived, turned_weight, ids, token)
    weight = lax.all_gather(turned_weight, SEQ, axis=0)
    weight = weight.reshape(size, -1, *weight.shape[1:])
    all_ids = from_all_groups(ids)
    centre = centre_of(exchanged(totals, PLANE), all_ids[1:])
    centre = exchanged(centre, PLANE).reshape(HALF, CLUSTERS, HDIM)
    parts, all_ids = attention_of(
        side, centre, all_ids, keys, keys_other, values, values_other
    )
    parts = exchanged(parts, PLANE)
    table = pl.pallas_call(
        combine_kernel,
        out_shape=jax.ShapeDtypeStruct((lax.axis_size(CUBE), QUARTER, HDIM), BF16),
        compiler_params=params(8),
    )(parts)
    table = exchanged(table, CUBE).reshape(size * HALF, CLUSTERS, HDIM)
    far_table = other_core(table)
    near = gather_of(side, z, all_ids, table, weight)
    return project_of(side, z, near, all_ids, far_table, weight)


def solution(mesh):
    head = mesh.shape["head"]
    finer = Mesh(mesh.devices.reshape(4, 4, 2, head), ("x", "y", "c", "z"))
    in_specs = (P(SEQ, "z"), P(SEQ, "z"), P(SEQ, "z"), P(SEQ, "z"), P("z", SEQ))
    return jax.shard_map(
        local, mesh=finer, in_specs=in_specs, out_specs=P(SEQ, "z"), check_vma=False
    )
```

```python
import functools
import math

import jax
import jax.numpy as jnp
from jax import lax
from jax.experimental import pallas as pl
from jax.experimental.pallas import tpu as pltpu
from jax.sharding import Mesh
from jax.sharding import PartitionSpec as P

HDIM = 128
CLUSTERS = 256
PIECES = 4
HALF = 4
QUARTER = CLUSTERS // 4
SEQ = ("x", "y", "c")
PLANE = ("x", "y")
CUBE = ("z", "x", "y")
EXTRA = 8
TAIL = 16
LARGE = 61
LOG2_SCALE = math.log2(math.e) / math.sqrt(HDIM)
F32 = jnp.float32
BF16 = jnp.bfloat16
NT = (((1,), (1,)), ((), ()))
TN = (((0,), (0,)), ((), ()))


def params(mib):
    return pltpu.CompilerParams(vmem_limit_bytes=mib * 2**20)


def eye(rows, cols):
    r = lax.broadcasted_iota(jnp.int32, (rows, cols), 0)
    c = lax.broadcasted_iota(jnp.int32, (rows, cols), 1)
    return r == c


def member_of(row):
    labels = lax.broadcasted_iota(jnp.int32, (CLUSTERS, row.shape[1]), 0)
    return (labels == row).astype(F32).astype(BF16)


def totals_kernel(side_ref, ids_ref, q_ref, *rest):
    theirs_refs, (mine_ref, held, arrived) = rest[:PIECES], rest[PIECES:]
    each = HALF // PIECES
    rows = q_ref.shape[0]
    firsts = (HALF - side_ref[0] * HALF, side_ref[0] * HALF)

    def fetch(k):
        start = pl.multiple_of(firsts[k] * HDIM, HALF * HDIM)
        return pltpu.make_async_copy(
            q_ref.at[:, pl.ds(start, HALF * HDIM)], held.at[k], arrived.at[k]
        )

    for k in range(2):
        fetch(k).start()
    ones = jnp.ones((rows, HDIM), BF16)
    diagonal = eye(QUARTER, HDIM)
    for k in range(2):
        fetch(k).wait()
        for i in range(HALF):
            out_ref, base = (mine_ref, i * 4) if k else (theirs_refs[i // each], i % each * 4)
            member = member_of(ids_ref[pl.ds(firsts[k] + i, 1), :])
            query = held[k, :, i * HDIM : (i + 1) * HDIM]
            both = jnp.dot(
                member, jnp.concatenate([query, ones], axis=1), preferred_element_type=F32
            )
            for q in range(4):
                lines = slice(q * QUARTER, (q + 1) * QUARTER)
                count = jnp.sum(
                    jnp.where(diagonal, both[lines, HDIM:], 0.0), axis=0, keepdims=True
                )
                out_ref[base + q, :QUARTER, :] = both[lines, :HDIM]
                out_ref[base + q, QUARTER:, :] = jnp.broadcast_to(count, (EXTRA, HDIM))


SCALARS = pl.BlockSpec(memory_space=pltpu.SMEM)
IN_VMEM = pl.BlockSpec(memory_space=pltpu.VMEM)
ANYWHERE = pl.BlockSpec(memory_space=pl.ANY)
IN_HBM = pl.BlockSpec(memory_space=pltpu.HBM)


def totals_of(side, ids, queries):
    rows = queries.shape[0]
    return pl.pallas_call(
        totals_kernel,
        out_shape=[
            jax.ShapeDtypeStruct((4 * HALF // PIECES, QUARTER + EXTRA, HDIM), F32),
        ]
        * PIECES
        + [jax.ShapeDtypeStruct((4 * HALF, QUARTER + EXTRA, HDIM), F32)],
        in_specs=[SCALARS, IN_VMEM, IN_HBM],
        out_specs=[IN_VMEM] * (PIECES + 1),
        scratch_shapes=[
            pltpu.VMEM((2, rows, HALF * HDIM), BF16),
            pltpu.SemaphoreType.DMA((2,)),
        ],
        compiler_params=params(58),
    )(side, ids, queries)


def halves_kernel(
    side_ref, after_ref, k_ref, v_ref, k_out_ref, v_out_ref, token_ref, held, come, gone
):
    del after_ref
    token_ref[0] = side_ref[0]
    start = pl.multiple_of((1 - side_ref[0]) * HALF * HDIM, HALF * HDIM)

    def fetch(k, source):
        return pltpu.make_async_copy(
            source.at[:, pl.ds(start, HALF * HDIM)], held.at[k], come.at[k]
        )

    def put(k, target):
        return pltpu.make_async_copy(held.at[k], target, gone.at[k])

    fetch(0, k_ref).start()
    fetch(1, v_ref).start()
    fetch(0, k_ref).wait()
    put(0, k_out_ref).start()
    fetch(1, v_ref).wait()
    put(1, v_out_ref).start()
    put(0, k_out_ref).wait()
    put(1, v_out_ref).wait()


def halves_of(side, after, keys, values):
    half = jax.ShapeDtypeStruct((keys.shape[0], HALF * HDIM), BF16)
    return pl.pallas_call(
        halves_kernel,
        out_shape=(half, half, jax.ShapeDtypeStruct((1,), jnp.int32)),
        in_specs=[SCALARS, IN_HBM, IN_HBM, IN_HBM],
        out_specs=(IN_HBM, IN_HBM, SCALARS),
        scratch_shapes=[
            pltpu.VMEM((2, *half.shape), BF16),
            pltpu.SemaphoreType.DMA((2,)),
            pltpu.SemaphoreType.DMA((2,)),
        ],
        compiler_params=params(LARGE),
    )(side, after, keys, values)


def add_kernel(a_ref, *rest):
    ids_ref, out_ref, ids_out_ref = rest[PIECES + 1], rest[PIECES + 3], rest[PIECES + 5]
    ids_out_ref[...] = ids_ref[...]
    size = a_ref.shape[0] // PIECES
    for k in range(PIECES):
        lines = slice(k * size, (k + 1) * size)
        out_ref[lines] = a_ref[lines] + rest[k][...]


def add_after(a, b, passed, ids, after):
    return pl.pallas_call(
        add_kernel,
        out_shape=(
            jax.ShapeDtypeStruct(a.shape, a.dtype),
            jax.ShapeDtypeStruct(passed.shape, passed.dtype),
            jax.ShapeDtypeStruct(ids.shape, ids.dtype),
        ),
        in_specs=[IN_VMEM] * (PIECES + 1) + [IN_HBM, IN_VMEM, SCALARS],
        out_specs=(IN_VMEM, IN_HBM, IN_VMEM),
        input_output_aliases={PIECES + 1: 1},
        compiler_params=params(8),
    )(a, *b, passed, ids, after)


def centre_kernel(in_ref, *rest):
    out_ref = rest[-1]
    whole = in_ref[0]
    for k in range(1, in_ref.shape[0]):
        whole += in_ref[k]
    spread = jnp.where(eye(QUARTER, HDIM), whole[QUARTER : QUARTER + 1, :], 0.0)
    count = jnp.sum(spread, axis=1, keepdims=True)
    centre = (whole[:QUARTER] / count).astype(BF16)
    for k in range(out_ref.shape[0]):
        out_ref[k] = centre


def centre_of(totals, after):
    return pl.pallas_call(
        centre_kernel,
        out_shape=jax.ShapeDtypeStruct((totals.shape[0], QUARTER, HDIM), BF16),
        in_specs=[IN_VMEM] + [ANYWHERE] * len(after),
        out_specs=IN_VMEM,
        compiler_params=params(8),
    )(totals, *after)


def attention_kernel(groups, side_ref, centre_ref, *rest):
    ids_refs, sources = rest[:groups], rest[groups : groups + 4]
    out_ref, ids_out_ref, held, arrived, copied = rest[groups + 4 :]
    first = side_ref[0] * HALF

    def fetch(k):
        source = sources[k]
        if k % 2 == 0:
            source = source.at[:, pl.ds(pl.multiple_of(first * HDIM, HALF * HDIM), HALF * HDIM)]
        return pltpu.make_async_copy(source, held.at[k], arrived.at[k])

    for k in range(2):
        fetch(k).start()
    copies = [
        pltpu.make_async_copy(ids_refs[d], ids_out_ref.at[d], copied.at[d]) for d in range(groups)
    ]
    for copy in copies:
        copy.start()
    ones = jnp.ones((held.shape[1], HDIM), BF16)
    diagonal = eye(QUARTER, HDIM)
    line = lax.broadcasted_iota(jnp.int32, (TAIL, HDIM), 0)
    for i in range(HALF):
        if i == 0:
            for k in range(2):
                fetch(k).wait()
            for k in range(2, 4):
                fetch(k).start()
        cols = slice(i * HDIM, (i + 1) * HDIM)
        centre = centre_ref[i]
        own = lax.dot_general(centre, held[0, :, cols], NT, preferred_element_type=F32)
        other = lax.dot_general(centre, held[1, :, cols], NT, preferred_element_type=F32)
        peak = jnp.maximum(
            jnp.max(own, axis=1, keepdims=True), jnp.max(other, axis=1, keepdims=True)
        )
        own_w = jnp.exp2((own - peak) * LOG2_SCALE).astype(BF16)
        other_w = jnp.exp2((other - peak) * LOG2_SCALE).astype(BF16)
        if i == 0:
            for k in range(2, 4):
                fetch(k).wait()
        both = jnp.dot(
            own_w, jnp.concatenate([held[2, :, cols], ones], axis=1), preferred_element_type=F32
        ) + jnp.dot(
            other_w, jnp.concatenate([held[3, :, cols], ones], axis=1), preferred_element_type=F32
        )
        mass = both[:, HDIM:]
        part = (both[:, :HDIM] / mass).astype(BF16)
        level = peak * LOG2_SCALE + jnp.log2(mass)
        for k in range(4):
            lines = slice(k * QUARTER, (k + 1) * QUARTER)
            row = jnp.sum(jnp.where(diagonal, level[lines], 0.0), axis=0, keepdims=True)
            high = row.astype(BF16).astype(F32)
            mid = (row - high).astype(BF16).astype(F32)
            low = row - high - mid
            tail = jnp.where(
                line == 0, high, jnp.where(line == 1, mid, jnp.where(line == 2, low, 0.0))
            )
            out_ref[i * 4 + k, :QUARTER, :] = part[lines]
            out_ref[i * 4 + k, QUARTER:, :] = tail.astype(BF16)
    for copy in copies:
        copy.wait()


def attention_of(side, centre, all_ids, keys, keys_other, values, values_other):
    rows = keys.shape[0]
    groups = len(all_ids)
    return pl.pallas_call(
        functools.partial(attention_kernel, groups),
        out_shape=(
            jax.ShapeDtypeStruct((4 * HALF, QUARTER + TAIL, HDIM), BF16),
            jax.ShapeDtypeStruct((groups, *all_ids[0].shape), jnp.int32),
        ),
        in_specs=[SCALARS, IN_VMEM] + [IN_HBM] * (groups + 4),
        out_specs=(IN_VMEM, IN_VMEM),
        scratch_shapes=[
            pltpu.VMEM((4, rows, HALF * HDIM), BF16),
            pltpu.SemaphoreType.DMA((4,)),
            pltpu.SemaphoreType.DMA((groups,)),
        ],
        compiler_params=params(52),
    )(side, centre, *all_ids, keys, keys_other, values, values_other)


def combine_kernel(in_ref, out_ref):
    count = in_ref.shape[0]
    tails = [in_ref[k, QUARTER:, :].astype(F32) for k in range(count)]
    levels = [t[0:1] + t[1:2] + t[2:3] for t in tails]
    top = functools.reduce(jnp.maximum, levels)
    shares = [jnp.exp2(level - top) for level in levels]
    mass = functools.reduce(jnp.add, shares)
    diagonal = eye(QUARTER, HDIM)
    whole = jnp.zeros((QUARTER, HDIM), F32)
    for k in range(count):
        spread = jnp.where(diagonal, shares[k] / mass, 0.0)
        share = jnp.sum(spread, axis=1, keepdims=True)
        whole += share * in_ref[k, :QUARTER, :].astype(F32)
    whole = whole.astype(BF16)
    for k in range(out_ref.shape[0]):
        out_ref[k] = whole


def columns_of(ids_row, table):
    return lax.dot_general(table, member_of(ids_row), TN, preferred_element_type=F32).astype(BF16)


def group_at(i, z_ref, groups):
    return lax.rem(z_ref[0] + groups - i, groups)


def gather_kernel(side_ref, z_ref, ids_ref, table_ref, after_ref, out_ref):
    del after_ref
    group = group_at(pl.program_id(0), z_ref, pl.num_programs(0))
    for j in range(HALF):
        row = ids_ref[pl.program_id(0), pl.ds(side_ref[0] * HALF + j, 1), :]
        out_ref[j * HDIM : (j + 1) * HDIM, :] = columns_of(row, table_ref[group * HALF + j])


def gather_of(side, z, ids, table, after):
    groups, lines, tokens = ids.shape
    return pl.pallas_call(
        gather_kernel,
        out_shape=jax.ShapeDtypeStruct((groups, HALF * HDIM, tokens), BF16),
        grid=(groups,),
        in_specs=[SCALARS, SCALARS, IN_VMEM, IN_VMEM, IN_HBM],
        out_specs=pl.BlockSpec((None, HALF * HDIM, tokens), lambda i: (i, 0, 0)),
        compiler_params=params(51),
    )(side, z, ids, table, after)


def project_kernel(
    side_ref,
    z_ref,
    near_ref,
    ids_ref,
    table_ref,
    w_ref,
    out_ref,
    held,
    columns_ref,
    done_ref,
    arrived,
    come,
    gone,
):
    groups, blocks = w_ref.shape[:2]
    half = HALF * HDIM
    depth = 2 * half
    width = out_ref.shape[1] // 2
    own = pl.multiple_of(side_ref[0] * half, half)
    other = pl.multiple_of(half - side_ref[0] * half, half)

    each = blocks // 2

    def fetch(i, b):
        entry = lax.rem(z_ref[0] + i, groups)
        part = pl.ds(b * each, each)
        return pltpu.make_async_copy(w_ref.at[entry, part], held.at[i, part], arrived.at[i, b])

    def bring(i):
        target = columns_ref.at[pl.ds(i * depth + own, half), :]
        return pltpu.make_async_copy(near_ref.at[i], target, come.at[i])

    for i in range(groups):
        bring(i).start()
        fetch(i, 0).start()
    for i in range(groups):
        fetch(i, 1).start()

    @pl.loop(0, groups)
    def _(i):
        group = group_at(i, z_ref, groups)
        for j in range(HALF):
            row = ids_ref[i, pl.ds((1 - side_ref[0]) * HALF + j, 1), :]
            start = pl.multiple_of(i * depth + other + j * HDIM, HDIM)
            columns_ref[pl.ds(start, HDIM), :] = columns_of(row, table_ref[group * HALF + j])

    def put(b):
        cols = pl.ds(pl.multiple_of(b * width, width), width)
        return pltpu.make_async_copy(done_ref.at[b], out_ref.at[:, cols], gone.at[b])

    for i in range(groups):
        bring(i).wait()

    @pl.loop(0, 2)
    def _(b):
        for i in range(groups):
            fetch(i, b).wait()
        weight = jnp.concatenate(
            [
                jnp.concatenate([held[i, b * each + k] for k in range(each)], axis=1)
                for i in range(groups)
            ],
            axis=0,
        )
        product = lax.dot_general(columns_ref[...], weight, TN, preferred_element_type=F32)
        done_ref[b] = product.astype(BF16)
        put(b).start()

    for b in range(2):
        put(b).wait()


def project_of(side, z, near, ids, table, weight):
    groups, lines, tokens = ids.shape
    blocks, depth, width = weight.shape[1:]
    return pl.pallas_call(
        project_kernel,
        out_shape=jax.ShapeDtypeStruct((tokens, blocks * width), BF16),
        in_specs=[SCALARS, SCALARS, IN_HBM, IN_VMEM, IN_VMEM, IN_HBM],
        out_specs=IN_HBM,
        scratch_shapes=[
            pltpu.VMEM(weight.shape, BF16),
            pltpu.VMEM((groups * depth, tokens), BF16),
            pltpu.VMEM((2, tokens, blocks * width // 2), BF16),
            pltpu.SemaphoreType.DMA((groups, 2)),
            pltpu.SemaphoreType.DMA((groups,)),
            pltpu.SemaphoreType.DMA((2,)),
        ],
        compiler_params=params(51),
    )(side, z, near, ids, table, weight)


def other_core(value):
    return lax.ppermute(value, "c", [(0, 1), (1, 0)])


def exchanged(value, axes):
    return lax.all_to_all(value, axes, split_axis=0, concat_axis=0, tiled=True)


def from_all_groups(value):
    size = lax.axis_size("z")
    found = [value]
    for d in range(1, size):
        found.append(lax.ppermute(value, "z", [(i, (i + d) % size) for i in range(size)]))
    return found


def local(queries, keys, values, cluster_ids, out_weight):
    core = lax.axis_index("c").astype(jnp.int32)
    side = core[None]
    z = lax.axis_index("z").astype(jnp.int32)[None]
    ids = cluster_ids.T
    size = lax.axis_size("z")
    turned = [
        (x * size + z, (2 * x - z) % size * size + x) for x in range(size) for z in range(size)
    ]
    turned_weight = lax.ppermute(out_weight, ("x", "z"), turned)

    *theirs, mine = totals_of(side, ids, queries)
    arrived = [other_core(piece) for piece in theirs]
    keys_far, values_far, token = halves_of(side, mine, keys, values)
    keys_other, values_other = other_core(keys_far), other_core(values_far)
    totals, turned_weight, ids = add_after(mine, arrived, turned_weight, ids, token)
    weight = lax.all_gather(turned_weight, SEQ, axis=0)
    weight = weight.reshape(size, -1, *weight.shape[1:])
    all_ids = from_all_groups(ids)
    centre = centre_of(exchanged(totals, PLANE), all_ids[1:])
    centre = exchanged(centre, PLANE).reshape(HALF, CLUSTERS, HDIM)
    parts, all_ids = attention_of(
        side, centre, all_ids, keys, keys_other, values, values_other
    )
    parts = exchanged(parts, PLANE)
    table = pl.pallas_call(
        combine_kernel,
        out_shape=jax.ShapeDtypeStruct((lax.axis_size(CUBE), QUARTER, HDIM), BF16),
        compiler_params=params(8),
    )(parts)
    table = exchanged(table, CUBE).reshape(size * HALF, CLUSTERS, HDIM)
    far_table = other_core(table)
    near = gather_of(side, z, all_ids, table, weight)
    return project_of(side, z, near, all_ids, far_table, weight)


def solution(mesh):
    head = mesh.shape["head"]
    finer = Mesh(mesh.devices.reshape(4, 4, 2, head), ("x", "y", "c", "z"))
    in_specs = (P(SEQ, "z"), P(SEQ, "z"), P(SEQ, "z"), P(SEQ, "z"), P("z", SEQ))
    return jax.shard_map(
        local, mesh=finer, in_specs=in_specs, out_specs=P(SEQ, "z"), check_vma=False
    )
```

```python
import functools
import math

import jax
import jax.numpy as jnp
from jax import lax
from jax.experimental import pallas as pl
from jax.experimental.pallas import tpu as pltpu
from jax.sharding import Mesh
from jax.sharding import PartitionSpec as P

HDIM = 128
CLUSTERS = 256
PIECES = 4
HALF = 4
QUARTER = CLUSTERS // 4
SEQ = ("x", "y", "c")
PLANE = ("x", "y")
CUBE = ("z", "x", "y")
EXTRA = 8
TAIL = 16
LARGE = 61
LOG2_SCALE = math.log2(math.e) / math.sqrt(HDIM)
F32 = jnp.float32
BF16 = jnp.bfloat16
NT = (((1,), (1,)), ((), ()))
TN = (((0,), (0,)), ((), ()))


def params(mib):
    return pltpu.CompilerParams(vmem_limit_bytes=mib * 2**20)


def eye(rows, cols):
    r = lax.broadcasted_iota(jnp.int32, (rows, cols), 0)
    c = lax.broadcasted_iota(jnp.int32, (rows, cols), 1)
    return r == c


def member_of(row):
    labels = lax.broadcasted_iota(jnp.int32, (CLUSTERS, row.shape[1]), 0)
    return (labels == row).astype(F32).astype(BF16)


def totals_kernel(side_ref, ids_ref, q_ref, *rest):
    theirs_refs, (mine_ref, held, arrived) = rest[:PIECES], rest[PIECES:]
    each = HALF // PIECES
    rows = q_ref.shape[0]
    firsts = (HALF - side_ref[0] * HALF, side_ref[0] * HALF)

    def fetch(k):
        start = pl.multiple_of(firsts[k] * HDIM, HALF * HDIM)
        return pltpu.make_async_copy(
            q_ref.at[:, pl.ds(start, HALF * HDIM)], held.at[k], arrived.at[k]
        )

    for k in range(2):
        fetch(k).start()
    ones = jnp.ones((rows, HDIM), BF16)
    diagonal = eye(QUARTER, HDIM)
    for k in range(2):
        fetch(k).wait()
        for i in range(HALF):
            out_ref, base = (mine_ref, i * 4) if k else (theirs_refs[i // each], i % each * 4)
            member = member_of(ids_ref[pl.ds(firsts[k] + i, 1), :])
            query = held[k, :, i * HDIM : (i + 1) * HDIM]
            both = jnp.dot(
                member, jnp.concatenate([query, ones], axis=1), preferred_element_type=F32
            )
            for q in range(4):
                lines = slice(q * QUARTER, (q + 1) * QUARTER)
                count = jnp.sum(
                    jnp.where(diagonal, both[lines, HDIM:], 0.0), axis=0, keepdims=True
                )
                out_ref[base + q, :QUARTER, :] = both[lines, :HDIM]
                out_ref[base + q, QUARTER:, :] = jnp.broadcast_to(count, (EXTRA, HDIM))


SCALARS = pl.BlockSpec(memory_space=pltpu.SMEM)
IN_VMEM = pl.BlockSpec(memory_space=pltpu.VMEM)
ANYWHERE = pl.BlockSpec(memory_space=pl.ANY)
IN_HBM = pl.BlockSpec(memory_space=pltpu.HBM)


def totals_of(side, ids, queries):
    rows = queries.shape[0]
    return pl.pallas_call(
        totals_kernel,
        out_shape=[
            jax.ShapeDtypeStruct((4 * HALF // PIECES, QUARTER + EXTRA, HDIM), F32),
        ]
        * PIECES
        + [jax.ShapeDtypeStruct((4 * HALF, QUARTER + EXTRA, HDIM), F32)],
        in_specs=[SCALARS, IN_VMEM, IN_HBM],
        out_specs=[IN_VMEM] * (PIECES + 1),
        scratch_shapes=[
            pltpu.VMEM((2, rows, HALF * HDIM), BF16),
            pltpu.SemaphoreType.DMA((2,)),
        ],
        compiler_params=params(58),
    )(side, ids, queries)


def halves_kernel(
    side_ref, after_ref, k_ref, v_ref, k_out_ref, v_out_ref, token_ref, held, come, gone
):
    del after_ref
    token_ref[0] = side_ref[0]
    start = pl.multiple_of((1 - side_ref[0]) * HALF * HDIM, HALF * HDIM)

    def fetch(k, source):
        return pltpu.make_async_copy(
            source.at[:, pl.ds(start, HALF * HDIM)], held.at[k], come.at[k]
        )

    def put(k, target):
        return pltpu.make_async_copy(held.at[k], target, gone.at[k])

    fetch(0, k_ref).start()
    fetch(1, v_ref).start()
    fetch(0, k_ref).wait()
    put(0, k_out_ref).start()
    fetch(1, v_ref).wait()
    put(1, v_out_ref).start()
    put(0, k_out_ref).wait()
    put(1, v_out_ref).wait()


def halves_of(side, after, keys, values):
    half = jax.ShapeDtypeStruct((keys.shape[0], HALF * HDIM), BF16)
    return pl.pallas_call(
        halves_kernel,
        out_shape=(half, half, jax.ShapeDtypeStruct((1,), jnp.int32)),
        in_specs=[SCALARS, IN_HBM, IN_HBM, IN_HBM],
        out_specs=(IN_HBM, IN_HBM, SCALARS),
        scratch_shapes=[
            pltpu.VMEM((2, *half.shape), BF16),
            pltpu.SemaphoreType.DMA((2,)),
            pltpu.SemaphoreType.DMA((2,)),
        ],
        compiler_params=params(LARGE),
    )(side, after, keys, values)


def add_kernel(a_ref, *rest):
    ids_ref, out_ref, ids_out_ref = rest[PIECES + 1], rest[PIECES + 3], rest[PIECES + 5]
    ids_out_ref[...] = ids_ref[...]
    size = a_ref.shape[0] // PIECES
    for k in range(PIECES):
        lines = slice(k * size, (k + 1) * size)
        out_ref[lines] = a_ref[lines] + rest[k][...]


def add_after(a, b, passed, ids, after):
    return pl.pallas_call(
        add_kernel,
        out_shape=(
            jax.ShapeDtypeStruct(a.shape, a.dtype),
            jax.ShapeDtypeStruct(passed.shape, passed.dtype),
            jax.ShapeDtypeStruct(ids.shape, ids.dtype),
        ),
        in_specs=[IN_VMEM] * (PIECES + 1) + [IN_HBM, IN_VMEM, SCALARS],
        out_specs=(IN_VMEM, IN_HBM, IN_VMEM),
        input_output_aliases={PIECES + 1: 1},
        compiler_params=params(8),
    )(a, *b, passed, ids, after)


def centre_kernel(in_ref, *rest):
    out_ref = rest[-1]
    whole = in_ref[0]
    for k in range(1, in_ref.shape[0]):
        whole += in_ref[k]
    spread = jnp.where(eye(QUARTER, HDIM), whole[QUARTER : QUARTER + 1, :], 0.0)
    count = jnp.sum(spread, axis=1, keepdims=True)
    centre = (whole[:QUARTER] / count).astype(BF16)
    for k in range(out_ref.shape[0]):
        out_ref[k] = centre


def centre_of(totals, after):
    return pl.pallas_call(
        centre_kernel,
        out_shape=jax.ShapeDtypeStruct((totals.shape[0], QUARTER, HDIM), BF16),
        in_specs=[IN_VMEM] + [ANYWHERE] * len(after),
        out_specs=IN_VMEM,
        compiler_params=params(8),
    )(totals, *after)


def attention_kernel(groups, side_ref, centre_ref, *rest):
    ids_refs, sources = rest[:groups], rest[groups : groups + 4]
    out_ref, ids_out_ref, held, arrived, copied = rest[groups + 4 :]
    first = side_ref[0] * HALF

    pair = 2 * HDIM

    def fetch(k, p):
        start = p * pair if k % 2 else pl.multiple_of(first * HDIM + p * pair, pair)
        return pltpu.make_async_copy(
            sources[k].at[:, pl.ds(start, pair)],
            held.at[k, :, pl.ds(p * pair, pair)],
            arrived.at[k, p],
        )

    for k in range(2):
        fetch(k, 0).start()
    copies = [
        pltpu.make_async_copy(ids_refs[d], ids_out_ref.at[d], copied.at[d]) for d in range(groups)
    ]
    for copy in copies:
        copy.start()
    ones = jnp.ones((held.shape[1], HDIM), BF16)
    diagonal = eye(QUARTER, HDIM)
    line = lax.broadcasted_iota(jnp.int32, (TAIL, HDIM), 0)
    for i in range(HALF):
        if i % 2 == 0:
            for k in range(2):
                fetch(k, i // 2).wait()
        if i == 0:
            for k in (2, 3):
                fetch(k, 0).start()
            for k in range(4):
                fetch(k, 1).start()
        cols = slice(i * HDIM, (i + 1) * HDIM)
        centre = centre_ref[i]
        own = lax.dot_general(centre, held[0, :, cols], NT, preferred_element_type=F32)
        other = lax.dot_general(centre, held[1, :, cols], NT, preferred_element_type=F32)
        peak = jnp.maximum(
            jnp.max(own, axis=1, keepdims=True), jnp.max(other, axis=1, keepdims=True)
        )
        own_w = jnp.exp2((own - peak) * LOG2_SCALE).astype(BF16)
        other_w = jnp.exp2((other - peak) * LOG2_SCALE).astype(BF16)
        if i % 2 == 0:
            for k in (2, 3):
                fetch(k, i // 2).wait()
        both = jnp.dot(
            own_w, jnp.concatenate([held[2, :, cols], ones], axis=1), preferred_element_type=F32
        ) + jnp.dot(
            other_w, jnp.concatenate([held[3, :, cols], ones], axis=1), preferred_element_type=F32
        )
        mass = both[:, HDIM:]
        part = (both[:, :HDIM] / mass).astype(BF16)
        level = peak * LOG2_SCALE + jnp.log2(mass)
        for k in range(4):
            lines = slice(k * QUARTER, (k + 1) * QUARTER)
            row = jnp.sum(jnp.where(diagonal, level[lines], 0.0), axis=0, keepdims=True)
            high = row.astype(BF16).astype(F32)
            mid = (row - high).astype(BF16).astype(F32)
            low = row - high - mid
            tail = jnp.where(
                line == 0, high, jnp.where(line == 1, mid, jnp.where(line == 2, low, 0.0))
            )
            out_ref[i * 4 + k, :QUARTER, :] = part[lines]
            out_ref[i * 4 + k, QUARTER:, :] = tail.astype(BF16)
    for copy in copies:
        copy.wait()


def attention_of(side, centre, all_ids, keys, keys_other, values, values_other):
    rows = keys.shape[0]
    groups = len(all_ids)
    return pl.pallas_call(
        functools.partial(attention_kernel, groups),
        out_shape=(
            jax.ShapeDtypeStruct((4 * HALF, QUARTER + TAIL, HDIM), BF16),
            jax.ShapeDtypeStruct((groups, *all_ids[0].shape), jnp.int32),
        ),
        in_specs=[SCALARS, IN_VMEM] + [IN_HBM] * (groups + 4),
        out_specs=(IN_VMEM, IN_VMEM),
        scratch_shapes=[
            pltpu.VMEM((4, rows, HALF * HDIM), BF16),
            pltpu.SemaphoreType.DMA((4, 2)),
            pltpu.SemaphoreType.DMA((groups,)),
        ],
        compiler_params=params(52),
    )(side, centre, *all_ids, keys, keys_other, values, values_other)


def combine_kernel(in_ref, out_ref):
    count = in_ref.shape[0]
    tails = [in_ref[k, QUARTER:, :].astype(F32) for k in range(count)]
    levels = [t[0:1] + t[1:2] + t[2:3] for t in tails]
    top = functools.reduce(jnp.maximum, levels)
    shares = [jnp.exp2(level - top) for level in levels]
    mass = functools.reduce(jnp.add, shares)
    diagonal = eye(QUARTER, HDIM)
    whole = jnp.zeros((QUARTER, HDIM), F32)
    for k in range(count):
        spread = jnp.where(diagonal, shares[k] / mass, 0.0)
        share = jnp.sum(spread, axis=1, keepdims=True)
        whole += share * in_ref[k, :QUARTER, :].astype(F32)
    whole = whole.astype(BF16)
    for k in range(out_ref.shape[0]):
        out_ref[k] = whole


def columns_of(ids_row, table):
    return lax.dot_general(table, member_of(ids_row), TN, preferred_element_type=F32).astype(BF16)


def group_at(i, z_ref, groups):
    return lax.rem(z_ref[0] + groups - i, groups)


def gather_kernel(side_ref, z_ref, ids_ref, table_ref, after_ref, out_ref):
    del after_ref
    group = group_at(pl.program_id(0), z_ref, pl.num_programs(0))
    for j in range(HALF):
        row = ids_ref[pl.program_id(0), pl.ds(side_ref[0] * HALF + j, 1), :]
        out_ref[j * HDIM : (j + 1) * HDIM, :] = columns_of(row, table_ref[group * HALF + j])


def gather_of(side, z, ids, table, after):
    groups, lines, tokens = ids.shape
    return pl.pallas_call(
        gather_kernel,
        out_shape=jax.ShapeDtypeStruct((groups, HALF * HDIM, tokens), BF16),
        grid=(groups,),
        in_specs=[SCALARS, SCALARS, IN_VMEM, IN_VMEM, IN_HBM],
        out_specs=pl.BlockSpec((None, HALF * HDIM, tokens), lambda i: (i, 0, 0)),
        compiler_params=params(51),
    )(side, z, ids, table, after)


def project_kernel(
    side_ref,
    z_ref,
    near_ref,
    ids_ref,
    table_ref,
    w_ref,
    out_ref,
    held,
    columns_ref,
    done_ref,
    arrived,
    come,
    gone,
):
    groups, blocks = w_ref.shape[:2]
    half = HALF * HDIM
    depth = 2 * half
    width = out_ref.shape[1] // 2
    own = pl.multiple_of(side_ref[0] * half, half)
    other = pl.multiple_of(half - side_ref[0] * half, half)

    each = blocks // 2

    def fetch(i, b):
        entry = lax.rem(z_ref[0] + i, groups)
        part = pl.ds(b * each, each)
        return pltpu.make_async_copy(w_ref.at[entry, part], held.at[i, part], arrived.at[i, b])

    def bring(i):
        target = columns_ref.at[pl.ds(i * depth + own, half), :]
        return pltpu.make_async_copy(near_ref.at[i], target, come.at[i])

    for i in range(groups):
        bring(i).start()
        fetch(i, 0).start()
    for i in range(groups):
        fetch(i, 1).start()

    @pl.loop(0, groups)
    def _(i):
        group = group_at(i, z_ref, groups)
        for j in range(HALF):
            row = ids_ref[i, pl.ds((1 - side_ref[0]) * HALF + j, 1), :]
            start = pl.multiple_of(i * depth + other + j * HDIM, HDIM)
            columns_ref[pl.ds(start, HDIM), :] = columns_of(row, table_ref[group * HALF + j])

    def put(b):
        cols = pl.ds(pl.multiple_of(b * width, width), width)
        return pltpu.make_async_copy(done_ref.at[b], out_ref.at[:, cols], gone.at[b])

    for i in range(groups):
        bring(i).wait()

    @pl.loop(0, 2)
    def _(b):
        for i in range(groups):
            fetch(i, b).wait()
        weight = jnp.concatenate(
            [
                jnp.concatenate([held[i, b * each + k] for k in range(each)], axis=1)
                for i in range(groups)
            ],
            axis=0,
        )
        product = lax.dot_general(columns_ref[...], weight, TN, preferred_element_type=F32)
        done_ref[b] = product.astype(BF16)
        put(b).start()

    for b in range(2):
        put(b).wait()


def project_of(side, z, near, ids, table, weight):
    groups, lines, tokens = ids.shape
    blocks, depth, width = weight.shape[1:]
    return pl.pallas_call(
        project_kernel,
        out_shape=jax.ShapeDtypeStruct((tokens, blocks * width), BF16),
        in_specs=[SCALARS, SCALARS, IN_HBM, IN_VMEM, IN_VMEM, IN_HBM],
        out_specs=IN_HBM,
        scratch_shapes=[
            pltpu.VMEM(weight.shape, BF16),
            pltpu.VMEM((groups * depth, tokens), BF16),
            pltpu.VMEM((2, tokens, blocks * width // 2), BF16),
            pltpu.SemaphoreType.DMA((groups, 2)),
            pltpu.SemaphoreType.DMA((groups,)),
            pltpu.SemaphoreType.DMA((2,)),
        ],
        compiler_params=params(51),
    )(side, z, near, ids, table, weight)


def other_core(value):
    return lax.ppermute(value, "c", [(0, 1), (1, 0)])


def exchanged(value, axes):
    return lax.all_to_all(value, axes, split_axis=0, concat_axis=0, tiled=True)


def from_all_groups(value):
    size = lax.axis_size("z")
    found = [value]
    for d in range(1, size):
        found.append(lax.ppermute(value, "z", [(i, (i + d) % size) for i in range(size)]))
    return found


def local(queries, keys, values, cluster_ids, out_weight):
    core = lax.axis_index("c").astype(jnp.int32)
    side = core[None]
    z = lax.axis_index("z").astype(jnp.int32)[None]
    ids = cluster_ids.T
    size = lax.axis_size("z")
    turned = [
        (x * size + z, (2 * x - z) % size * size + x) for x in range(size) for z in range(size)
    ]
    turned_weight = lax.ppermute(out_weight, ("x", "z"), turned)

    *theirs, mine = totals_of(side, ids, queries)
    arrived = [other_core(piece) for piece in theirs]
    keys_far, values_far, token = halves_of(side, mine, keys, values)
    keys_other, values_other = other_core(keys_far), other_core(values_far)
    totals, turned_weight, ids = add_after(mine, arrived, turned_weight, ids, token)
    weight = lax.all_gather(turned_weight, SEQ, axis=0)
    weight = weight.reshape(size, -1, *weight.shape[1:])
    all_ids = from_all_groups(ids)
    centre = centre_of(exchanged(totals, PLANE), all_ids[1:])
    centre = exchanged(centre, PLANE).reshape(HALF, CLUSTERS, HDIM)
    parts, all_ids = attention_of(
        side, centre, all_ids, keys, keys_other, values, values_other
    )
    parts = exchanged(parts, PLANE)
    table = pl.pallas_call(
        combine_kernel,
        out_shape=jax.ShapeDtypeStruct((lax.axis_size(CUBE), QUARTER, HDIM), BF16),
        compiler_params=params(8),
    )(parts)
    table = exchanged(table, CUBE).reshape(size * HALF, CLUSTERS, HDIM)
    far_table = other_core(table)
    near = gather_of(side, z, all_ids, table, weight)
    return project_of(side, z, near, all_ids, far_table, weight)


def solution(mesh):
    head = mesh.shape["head"]
    finer = Mesh(mesh.devices.reshape(4, 4, 2, head), ("x", "y", "c", "z"))
    in_specs = (P(SEQ, "z"), P(SEQ, "z"), P(SEQ, "z"), P(SEQ, "z"), P("z", SEQ))
    return jax.shard_map(
        local, mesh=finer, in_specs=in_specs, out_specs=P(SEQ, "z"), check_vma=False
    )
```

```python
import functools
import math

import jax
import jax.numpy as jnp
from jax import lax
from jax.experimental import pallas as pl
from jax.experimental.pallas import tpu as pltpu
from jax.sharding import Mesh
from jax.sharding import PartitionSpec as P

HDIM = 128
CLUSTERS = 256
PIECES = 4
HALF = 4
QUARTER = CLUSTERS // 4
SEQ = ("x", "y", "c")
PLANE = ("x", "y")
CUBE = ("z", "x", "y")
EXTRA = 8
TAIL = 16
LARGE = 61
LOG2_SCALE = math.log2(math.e) / math.sqrt(HDIM)
F32 = jnp.float32
BF16 = jnp.bfloat16
NT = (((1,), (1,)), ((), ()))
TN = (((0,), (0,)), ((), ()))


def params(mib):
    return pltpu.CompilerParams(vmem_limit_bytes=mib * 2**20)


def eye(rows, cols):
    r = lax.broadcasted_iota(jnp.int32, (rows, cols), 0)
    c = lax.broadcasted_iota(jnp.int32, (rows, cols), 1)
    return r == c


def member_of(row):
    labels = lax.broadcasted_iota(jnp.int32, (CLUSTERS, row.shape[1]), 0)
    return (labels == row).astype(F32).astype(BF16)


def totals_kernel(side_ref, ids_ref, q_ref, *rest):
    theirs_refs, (mine_ref, held, arrived) = rest[:PIECES], rest[PIECES:]
    each = HALF // PIECES
    rows = q_ref.shape[0]
    firsts = (HALF - side_ref[0] * HALF, side_ref[0] * HALF)

    def fetch(k):
        start = pl.multiple_of(firsts[k] * HDIM, HALF * HDIM)
        return pltpu.make_async_copy(
            q_ref.at[:, pl.ds(start, HALF * HDIM)], held.at[k], arrived.at[k]
        )

    for k in range(2):
        fetch(k).start()
    ones = jnp.ones((rows, HDIM), BF16)
    diagonal = eye(QUARTER, HDIM)
    for k in range(2):
        fetch(k).wait()
        for i in range(HALF):
            out_ref, base = (mine_ref, i * 4) if k else (theirs_refs[i // each], i % each * 4)
            member = member_of(ids_ref[pl.ds(firsts[k] + i, 1), :])
            query = held[k, :, i * HDIM : (i + 1) * HDIM]
            both = jnp.dot(
                member, jnp.concatenate([query, ones], axis=1), preferred_element_type=F32
            )
            for q in range(4):
                lines = slice(q * QUARTER, (q + 1) * QUARTER)
                count = jnp.sum(
                    jnp.where(diagonal, both[lines, HDIM:], 0.0), axis=0, keepdims=True
                )
                out_ref[base + q, :QUARTER, :] = both[lines, :HDIM]
                out_ref[base + q, QUARTER:, :] = jnp.broadcast_to(count, (EXTRA, HDIM))


SCALARS = pl.BlockSpec(memory_space=pltpu.SMEM)
IN_VMEM = pl.BlockSpec(memory_space=pltpu.VMEM)
ANYWHERE = pl.BlockSpec(memory_space=pl.ANY)
IN_HBM = pl.BlockSpec(memory_space=pltpu.HBM)


def totals_of(side, ids, queries):
    rows = queries.shape[0]
    return pl.pallas_call(
        totals_kernel,
        out_shape=[
            jax.ShapeDtypeStruct((4 * HALF // PIECES, QUARTER + EXTRA, HDIM), F32),
        ]
        * PIECES
        + [jax.ShapeDtypeStruct((4 * HALF, QUARTER + EXTRA, HDIM), F32)],
        in_specs=[SCALARS, IN_VMEM, IN_HBM],
        out_specs=[IN_VMEM] * (PIECES + 1),
        scratch_shapes=[
            pltpu.VMEM((2, rows, HALF * HDIM), BF16),
            pltpu.SemaphoreType.DMA((2,)),
        ],
        compiler_params=params(58),
    )(side, ids, queries)


def halves_kernel(
    side_ref, after_ref, k_ref, v_ref, k_out_ref, v_out_ref, token_ref, held, come, gone
):
    del after_ref
    token_ref[0] = side_ref[0]
    start = pl.multiple_of((1 - side_ref[0]) * HALF * HDIM, HALF * HDIM)

    def fetch(k, source):
        return pltpu.make_async_copy(
            source.at[:, pl.ds(start, HALF * HDIM)], held.at[k], come.at[k]
        )

    def put(k, target):
        return pltpu.make_async_copy(held.at[k], target, gone.at[k])

    fetch(0, k_ref).start()
    fetch(1, v_ref).start()
    fetch(0, k_ref).wait()
    put(0, k_out_ref).start()
    fetch(1, v_ref).wait()
    put(1, v_out_ref).start()
    put(0, k_out_ref).wait()
    put(1, v_out_ref).wait()


def halves_of(side, after, keys, values):
    half = jax.ShapeDtypeStruct((keys.shape[0], HALF * HDIM), BF16)
    return pl.pallas_call(
        halves_kernel,
        out_shape=(half, half, jax.ShapeDtypeStruct((1,), jnp.int32)),
        in_specs=[SCALARS, IN_HBM, IN_HBM, IN_HBM],
        out_specs=(IN_HBM, IN_HBM, SCALARS),
        scratch_shapes=[
            pltpu.VMEM((2, *half.shape), BF16),
            pltpu.SemaphoreType.DMA((2,)),
            pltpu.SemaphoreType.DMA((2,)),
        ],
        compiler_params=params(LARGE),
    )(side, after, keys, values)


def add_kernel(a_ref, *rest):
    ids_ref, out_ref, ids_out_ref = rest[PIECES + 1], rest[PIECES + 3], rest[PIECES + 5]
    ids_out_ref[...] = ids_ref[...]
    size = a_ref.shape[0] // PIECES
    for k in range(PIECES):
        lines = slice(k * size, (k + 1) * size)
        out_ref[lines] = a_ref[lines] + rest[k][...]


def add_after(a, b, passed, ids, after):
    return pl.pallas_call(
        add_kernel,
        out_shape=(
            jax.ShapeDtypeStruct(a.shape, a.dtype),
            jax.ShapeDtypeStruct(passed.shape, passed.dtype),
            jax.ShapeDtypeStruct(ids.shape, ids.dtype),
        ),
        in_specs=[IN_VMEM] * (PIECES + 1) + [IN_HBM, IN_VMEM, SCALARS],
        out_specs=(IN_VMEM, IN_HBM, IN_VMEM),
        input_output_aliases={PIECES + 1: 1},
        compiler_params=params(8),
    )(a, *b, passed, ids, after)


def centre_kernel(in_ref, *rest):
    out_ref = rest[-1]
    whole = in_ref[0]
    for k in range(1, in_ref.shape[0]):
        whole += in_ref[k]
    spread = jnp.where(eye(QUARTER, HDIM), whole[QUARTER : QUARTER + 1, :], 0.0)
    count = jnp.sum(spread, axis=1, keepdims=True)
    centre = (whole[:QUARTER] / count).astype(BF16)
    for k in range(out_ref.shape[0]):
        out_ref[k] = centre


def centre_of(totals, after):
    return pl.pallas_call(
        centre_kernel,
        out_shape=jax.ShapeDtypeStruct((totals.shape[0], QUARTER, HDIM), BF16),
        in_specs=[IN_VMEM] + [ANYWHERE] * len(after),
        out_specs=IN_VMEM,
        compiler_params=params(8),
    )(totals, *after)


def attention_kernel(groups, side_ref, centre_ref, *rest):
    ids_refs, others_ref = rest[:groups], rest[groups + 1]
    sources = (rest[groups], rest[groups + 2], rest[groups + 3])
    out_ref, ids_out_ref, held, arrived, copied = rest[groups + 4 :]
    first = side_ref[0] * HALF

    def fetch(k):
        source = sources[k]
        if k < 2:
            source = source.at[:, pl.ds(pl.multiple_of(first * HDIM, HALF * HDIM), HALF * HDIM)]
        return pltpu.make_async_copy(source, held.at[k], arrived.at[k])

    fetch(0).start()
    copies = [
        pltpu.make_async_copy(ids_refs[d], ids_out_ref.at[d], copied.at[d]) for d in range(groups)
    ]
    for copy in copies:
        copy.start()
    ones = jnp.ones((held.shape[1], HDIM), BF16)
    diagonal = eye(QUARTER, HDIM)
    line = lax.broadcasted_iota(jnp.int32, (TAIL, HDIM), 0)
    for i in range(HALF):
        if i == 0:
            fetch(0).wait()
            fetch(1).start()
            fetch(2).start()
        cols = slice(i * HDIM, (i + 1) * HDIM)
        centre = centre_ref[i]
        own = lax.dot_general(centre, held[0, :, cols], NT, preferred_element_type=F32)
        other = lax.dot_general(centre, others_ref[:, cols], NT, preferred_element_type=F32)
        peak = jnp.maximum(
            jnp.max(own, axis=1, keepdims=True), jnp.max(other, axis=1, keepdims=True)
        )
        own_w = jnp.exp2((own - peak) * LOG2_SCALE).astype(BF16)
        other_w = jnp.exp2((other - peak) * LOG2_SCALE).astype(BF16)
        if i == 0:
            fetch(1).wait()
            fetch(2).wait()
        both = jnp.dot(
            own_w, jnp.concatenate([held[1, :, cols], ones], axis=1), preferred_element_type=F32
        ) + jnp.dot(
            other_w, jnp.concatenate([held[2, :, cols], ones], axis=1), preferred_element_type=F32
        )
        mass = both[:, HDIM:]
        part = (both[:, :HDIM] / mass).astype(BF16)
        level = peak * LOG2_SCALE + jnp.log2(mass)
        for k in range(4):
            lines = slice(k * QUARTER, (k + 1) * QUARTER)
            row = jnp.sum(jnp.where(diagonal, level[lines], 0.0), axis=0, keepdims=True)
            high = row.astype(BF16).astype(F32)
            mid = (row - high).astype(BF16).astype(F32)
            low = row - high - mid
            tail = jnp.where(
                line == 0, high, jnp.where(line == 1, mid, jnp.where(line == 2, low, 0.0))
            )
            out_ref[i * 4 + k, :QUARTER, :] = part[lines]
            out_ref[i * 4 + k, QUARTER:, :] = tail.astype(BF16)
    for copy in copies:
        copy.wait()


def attention_of(side, centre, all_ids, keys, keys_other, values, values_other):
    rows = keys.shape[0]
    groups = len(all_ids)
    return pl.pallas_call(
        functools.partial(attention_kernel, groups),
        out_shape=(
            jax.ShapeDtypeStruct((4 * HALF, QUARTER + TAIL, HDIM), BF16),
            jax.ShapeDtypeStruct((groups, *all_ids[0].shape), jnp.int32),
        ),
        in_specs=[SCALARS, IN_VMEM] + [IN_HBM] * (groups + 1) + [IN_VMEM, IN_HBM, IN_HBM],
        out_specs=(IN_VMEM, IN_VMEM),
        scratch_shapes=[
            pltpu.VMEM((3, rows, HALF * HDIM), BF16),
            pltpu.SemaphoreType.DMA((3,)),
            pltpu.SemaphoreType.DMA((groups,)),
        ],
        compiler_params=params(52),
    )(side, centre, *all_ids, keys, keys_other, values, values_other)


def combine_kernel(in_ref, out_ref):
    count = in_ref.shape[0]
    tails = [in_ref[k, QUARTER:, :].astype(F32) for k in range(count)]
    levels = [t[0:1] + t[1:2] + t[2:3] for t in tails]
    top = functools.reduce(jnp.maximum, levels)
    shares = [jnp.exp2(level - top) for level in levels]
    mass = functools.reduce(jnp.add, shares)
    diagonal = eye(QUARTER, HDIM)
    whole = jnp.zeros((QUARTER, HDIM), F32)
    for k in range(count):
        spread = jnp.where(diagonal, shares[k] / mass, 0.0)
        share = jnp.sum(spread, axis=1, keepdims=True)
        whole += share * in_ref[k, :QUARTER, :].astype(F32)
    whole = whole.astype(BF16)
    for k in range(out_ref.shape[0]):
        out_ref[k] = whole


def columns_of(ids_row, table):
    return lax.dot_general(table, member_of(ids_row), TN, preferred_element_type=F32).astype(BF16)


def group_at(i, z_ref, groups):
    return lax.rem(z_ref[0] + groups - i, groups)


def gather_kernel(side_ref, z_ref, ids_ref, table_ref, after_ref, out_ref):
    del after_ref
    group = group_at(pl.program_id(0), z_ref, pl.num_programs(0))
    for j in range(HALF):
        row = ids_ref[pl.program_id(0), pl.ds(side_ref[0] * HALF + j, 1), :]
        out_ref[j * HDIM : (j + 1) * HDIM, :] = columns_of(row, table_ref[group * HALF + j])


def gather_of(side, z, ids, table, after):
    groups, lines, tokens = ids.shape
    return pl.pallas_call(
        gather_kernel,
        out_shape=jax.ShapeDtypeStruct((groups, HALF * HDIM, tokens), BF16),
        grid=(groups,),
        in_specs=[SCALARS, SCALARS, IN_VMEM, IN_VMEM, IN_HBM],
        out_specs=pl.BlockSpec((None, HALF * HDIM, tokens), lambda i: (i, 0, 0)),
        compiler_params=params(51),
    )(side, z, ids, table, after)


def project_kernel(
    side_ref,
    z_ref,
    near_ref,
    ids_ref,
    table_ref,
    w_ref,
    out_ref,
    held,
    columns_ref,
    done_ref,
    arrived,
    come,
    gone,
):
    groups, blocks = w_ref.shape[:2]
    half = HALF * HDIM
    depth = 2 * half
    width = out_ref.shape[1] // 2
    own = pl.multiple_of(side_ref[0] * half, half)
    other = pl.multiple_of(half - side_ref[0] * half, half)

    each = blocks // 2

    def fetch(i, b):
        entry = lax.rem(z_ref[0] + i, groups)
        part = pl.ds(b * each, each)
        return pltpu.make_async_copy(w_ref.at[entry, part], held.at[i, part], arrived.at[i, b])

    def bring(i):
        target = columns_ref.at[pl.ds(i * depth + own, half), :]
        return pltpu.make_async_copy(near_ref.at[i], target, come.at[i])

    for i in range(groups):
        bring(i).start()
        fetch(i, 0).start()
    for i in range(groups):
        fetch(i, 1).start()

    @pl.loop(0, groups)
    def _(i):
        group = group_at(i, z_ref, groups)
        for j in range(HALF):
            row = ids_ref[i, pl.ds((1 - side_ref[0]) * HALF + j, 1), :]
            start = pl.multiple_of(i * depth + other + j * HDIM, HDIM)
            columns_ref[pl.ds(start, HDIM), :] = columns_of(row, table_ref[group * HALF + j])

    def put(b):
        cols = pl.ds(pl.multiple_of(b * width, width), width)
        return pltpu.make_async_copy(done_ref.at[b], out_ref.at[:, cols], gone.at[b])

    for i in range(groups):
        bring(i).wait()

    @pl.loop(0, 2)
    def _(b):
        for i in range(groups):
            fetch(i, b).wait()
        weight = jnp.concatenate(
            [
                jnp.concatenate([held[i, b * each + k] for k in range(each)], axis=1)
                for i in range(groups)
            ],
            axis=0,
        )
        product = lax.dot_general(columns_ref[...], weight, TN, preferred_element_type=F32)
        done_ref[b] = product.astype(BF16)
        put(b).start()

    for b in range(2):
        put(b).wait()


def project_of(side, z, near, ids, table, weight):
    groups, lines, tokens = ids.shape
    blocks, depth, width = weight.shape[1:]
    return pl.pallas_call(
        project_kernel,
        out_shape=jax.ShapeDtypeStruct((tokens, blocks * width), BF16),
        in_specs=[SCALARS, SCALARS, IN_HBM, IN_VMEM, IN_VMEM, IN_HBM],
        out_specs=IN_HBM,
        scratch_shapes=[
            pltpu.VMEM(weight.shape, BF16),
            pltpu.VMEM((groups * depth, tokens), BF16),
            pltpu.VMEM((2, tokens, blocks * width // 2), BF16),
            pltpu.SemaphoreType.DMA((groups, 2)),
            pltpu.SemaphoreType.DMA((groups,)),
            pltpu.SemaphoreType.DMA((2,)),
        ],
        compiler_params=params(51),
    )(side, z, near, ids, table, weight)


def other_core(value):
    return lax.ppermute(value, "c", [(0, 1), (1, 0)])


def exchanged(value, axes):
    return lax.all_to_all(value, axes, split_axis=0, concat_axis=0, tiled=True)


def from_all_groups(value):
    size = lax.axis_size("z")
    found = [value]
    for d in range(1, size):
        found.append(lax.ppermute(value, "z", [(i, (i + d) % size) for i in range(size)]))
    return found


def local(queries, keys, values, cluster_ids, out_weight):
    core = lax.axis_index("c").astype(jnp.int32)
    side = core[None]
    z = lax.axis_index("z").astype(jnp.int32)[None]
    ids = cluster_ids.T
    size = lax.axis_size("z")
    turned = [
        (x * size + z, (2 * x - z) % size * size + x) for x in range(size) for z in range(size)
    ]
    turned_weight = lax.ppermute(out_weight, ("x", "z"), turned)

    *theirs, mine = totals_of(side, ids, queries)
    arrived = [other_core(piece) for piece in theirs]
    keys_far, values_far, token = halves_of(side, mine, keys, values)
    keys_other, values_other = other_core(keys_far), other_core(values_far)
    totals, turned_weight, ids = add_after(mine, arrived, turned_weight, ids, token)
    weight = lax.all_gather(turned_weight, SEQ, axis=0)
    weight = weight.reshape(size, -1, *weight.shape[1:])
    all_ids = from_all_groups(ids)
    centre = centre_of(exchanged(totals, PLANE), all_ids[1:])
    centre = exchanged(centre, PLANE).reshape(HALF, CLUSTERS, HDIM)
    parts, all_ids = attention_of(
        side, centre, all_ids, keys, keys_other, values, values_other
    )
    parts = exchanged(parts, PLANE)
    table = pl.pallas_call(
        combine_kernel,
        out_shape=jax.ShapeDtypeStruct((lax.axis_size(CUBE), QUARTER, HDIM), BF16),
        compiler_params=params(8),
    )(parts)
    table = exchanged(table, CUBE).reshape(size * HALF, CLUSTERS, HDIM)
    far_table = other_core(table)
    near = gather_of(side, z, all_ids, table, weight)
    return project_of(side, z, near, all_ids, far_table, weight)


def solution(mesh):
    head = mesh.shape["head"]
    finer = Mesh(mesh.devices.reshape(4, 4, 2, head), ("x", "y", "c", "z"))
    in_specs = (P(SEQ, "z"), P(SEQ, "z"), P(SEQ, "z"), P(SEQ, "z"), P("z", SEQ))
    return jax.shard_map(
        local, mesh=finer, in_specs=in_specs, out_specs=P(SEQ, "z"), check_vma=False
    )
```

```python
import functools
import math

import jax
import jax.numpy as jnp
from jax import lax
from jax.experimental import pallas as pl
from jax.experimental.pallas import tpu as pltpu
from jax.sharding import Mesh
from jax.sharding import PartitionSpec as P

HDIM = 128
CLUSTERS = 256
PIECES = 4
HALF = 4
QUARTER = CLUSTERS // 4
SEQ = ("x", "y", "c")
PLANE = ("x", "y")
CUBE = ("z", "x", "y")
EXTRA = 8
TAIL = 16
LARGE = 61
LOG2_SCALE = math.log2(math.e) / math.sqrt(HDIM)
F32 = jnp.float32
BF16 = jnp.bfloat16
NT = (((1,), (1,)), ((), ()))
TN = (((0,), (0,)), ((), ()))


def params(mib):
    return pltpu.CompilerParams(vmem_limit_bytes=mib * 2**20)


def eye(rows, cols):
    r = lax.broadcasted_iota(jnp.int32, (rows, cols), 0)
    c = lax.broadcasted_iota(jnp.int32, (rows, cols), 1)
    return r == c


def member_of(row):
    labels = lax.broadcasted_iota(jnp.int32, (CLUSTERS, row.shape[1]), 0)
    return (labels == row).astype(F32).astype(BF16)


def totals_kernel(side_ref, ids_ref, q_ref, *rest):
    theirs_refs, (mine_ref, held, arrived) = rest[:PIECES], rest[PIECES:]
    each = HALF // PIECES
    rows = q_ref.shape[0]
    firsts = (HALF - side_ref[0] * HALF, side_ref[0] * HALF)

    def fetch(k):
        start = pl.multiple_of(firsts[k] * HDIM, HALF * HDIM)
        return pltpu.make_async_copy(
            q_ref.at[:, pl.ds(start, HALF * HDIM)], held.at[k], arrived.at[k]
        )

    for k in range(2):
        fetch(k).start()
    ones = jnp.ones((rows, HDIM), BF16)
    diagonal = eye(QUARTER, HDIM)
    for k in range(2):
        fetch(k).wait()
        for i in range(HALF):
            out_ref, base = (mine_ref, i * 4) if k else (theirs_refs[i // each], i % each * 4)
            member = member_of(ids_ref[pl.ds(firsts[k] + i, 1), :])
            query = held[k, :, i * HDIM : (i + 1) * HDIM]
            both = jnp.dot(
                member, jnp.concatenate([query, ones], axis=1), preferred_element_type=F32
            )
            for q in range(4):
                lines = slice(q * QUARTER, (q + 1) * QUARTER)
                count = jnp.sum(
                    jnp.where(diagonal, both[lines, HDIM:], 0.0), axis=0, keepdims=True
                )
                out_ref[base + q, :QUARTER, :] = both[lines, :HDIM]
                out_ref[base + q, QUARTER:, :] = jnp.broadcast_to(count, (EXTRA, HDIM))


SCALARS = pl.BlockSpec(memory_space=pltpu.SMEM)
IN_VMEM = pl.BlockSpec(memory_space=pltpu.VMEM)
ANYWHERE = pl.BlockSpec(memory_space=pl.ANY)
IN_HBM = pl.BlockSpec(memory_space=pltpu.HBM)


def totals_of(side, ids, queries):
    rows = queries.shape[0]
    return pl.pallas_call(
        totals_kernel,
        out_shape=[
            jax.ShapeDtypeStruct((4 * HALF // PIECES, QUARTER + EXTRA, HDIM), F32),
        ]
        * PIECES
        + [jax.ShapeDtypeStruct((4 * HALF, QUARTER + EXTRA, HDIM), F32)],
        in_specs=[SCALARS, IN_VMEM, IN_HBM],
        out_specs=[IN_VMEM] * (PIECES + 1),
        scratch_shapes=[
            pltpu.VMEM((2, rows, HALF * HDIM), BF16),
            pltpu.SemaphoreType.DMA((2,)),
        ],
        compiler_params=params(58),
    )(side, ids, queries)


def halves_kernel(
    side_ref, after_ref, k_ref, v_ref, k_out_ref, v_out_ref, token_ref, held, come, gone
):
    del after_ref
    token_ref[0] = side_ref[0]
    start = pl.multiple_of((1 - side_ref[0]) * HALF * HDIM, HALF * HDIM)

    def fetch(k, source):
        return pltpu.make_async_copy(
            source.at[:, pl.ds(start, HALF * HDIM)], held.at[k], come.at[k]
        )

    def put(k, target):
        return pltpu.make_async_copy(held.at[k], target, gone.at[k])

    fetch(0, k_ref).start()
    fetch(1, v_ref).start()
    fetch(0, k_ref).wait()
    put(0, k_out_ref).start()
    fetch(1, v_ref).wait()
    put(1, v_out_ref).start()
    put(0, k_out_ref).wait()
    put(1, v_out_ref).wait()


def halves_of(side, after, keys, values):
    half = jax.ShapeDtypeStruct((keys.shape[0], HALF * HDIM), BF16)
    return pl.pallas_call(
        halves_kernel,
        out_shape=(half, half, jax.ShapeDtypeStruct((1,), jnp.int32)),
        in_specs=[SCALARS, IN_HBM, IN_HBM, IN_HBM],
        out_specs=(IN_HBM, IN_HBM, SCALARS),
        scratch_shapes=[
            pltpu.VMEM((2, *half.shape), BF16),
            pltpu.SemaphoreType.DMA((2,)),
            pltpu.SemaphoreType.DMA((2,)),
        ],
        compiler_params=params(LARGE),
    )(side, after, keys, values)


def add_kernel(a_ref, *rest):
    ids_ref, out_ref, ids_out_ref = rest[PIECES + 1], rest[PIECES + 3], rest[PIECES + 5]
    ids_out_ref[...] = ids_ref[...]
    size = a_ref.shape[0] // PIECES
    for k in range(PIECES):
        lines = slice(k * size, (k + 1) * size)
        out_ref[lines] = a_ref[lines] + rest[k][...]


def add_after(a, b, passed, ids, after):
    return pl.pallas_call(
        add_kernel,
        out_shape=(
            jax.ShapeDtypeStruct(a.shape, a.dtype),
            jax.ShapeDtypeStruct(passed.shape, passed.dtype),
            jax.ShapeDtypeStruct(ids.shape, ids.dtype),
        ),
        in_specs=[IN_VMEM] * (PIECES + 1) + [IN_HBM, IN_VMEM, SCALARS],
        out_specs=(IN_VMEM, IN_HBM, IN_VMEM),
        input_output_aliases={PIECES + 1: 1},
        compiler_params=params(8),
    )(a, *b, passed, ids, after)


def centre_kernel(in_ref, *rest):
    out_ref = rest[-1]
    whole = in_ref[0]
    for k in range(1, in_ref.shape[0]):
        whole += in_ref[k]
    spread = jnp.where(eye(QUARTER, HDIM), whole[QUARTER : QUARTER + 1, :], 0.0)
    count = jnp.sum(spread, axis=1, keepdims=True)
    centre = (whole[:QUARTER] / count).astype(BF16)
    for k in range(out_ref.shape[0]):
        out_ref[k] = centre


def centre_of(totals, after):
    return pl.pallas_call(
        centre_kernel,
        out_shape=jax.ShapeDtypeStruct((totals.shape[0], QUARTER, HDIM), BF16),
        in_specs=[IN_VMEM] + [ANYWHERE] * len(after),
        out_specs=IN_VMEM,
        compiler_params=params(8),
    )(totals, *after)


def attention_kernel(groups, side_ref, centre_ref, *rest):
    ids_refs, others_ref = rest[:groups], rest[groups + 1]
    sources = (rest[groups], rest[groups + 2], rest[groups + 3])
    out_ref, ids_out_ref, held, arrived, copied = rest[groups + 4 :]
    first = side_ref[0] * HALF

    def fetch(k):
        source = sources[k]
        if k < 2:
            source = source.at[:, pl.ds(pl.multiple_of(first * HDIM, HALF * HDIM), HALF * HDIM)]
        return pltpu.make_async_copy(source, held.at[k], arrived.at[k])

    fetch(0).start()
    copies = [
        pltpu.make_async_copy(ids_refs[d], ids_out_ref.at[d], copied.at[d]) for d in range(groups)
    ]
    for copy in copies:
        copy.start()
    ones = jnp.ones((held.shape[1], HDIM), BF16)
    diagonal = eye(QUARTER, HDIM)
    line = lax.broadcasted_iota(jnp.int32, (TAIL, HDIM), 0)

    def scores(i):
        cols = slice(i * HDIM, (i + 1) * HDIM)
        return (
            lax.dot_general(centre_ref[i], held[0, :, cols], NT, preferred_element_type=F32),
            lax.dot_general(centre_ref[i], others_ref[:, cols], NT, preferred_element_type=F32),
        )

    fetch(0).wait()
    fetch(1).start()
    fetch(2).start()
    coming = scores(0)
    for i in range(HALF):
        cols = slice(i * HDIM, (i + 1) * HDIM)
        own, other = coming
        coming = scores(i + 1) if i + 1 < HALF else None
        peak = jnp.maximum(
            jnp.max(own, axis=1, keepdims=True), jnp.max(other, axis=1, keepdims=True)
        )
        own_w = jnp.exp2((own - peak) * LOG2_SCALE).astype(BF16)
        other_w = jnp.exp2((other - peak) * LOG2_SCALE).astype(BF16)
        if i == 0:
            fetch(1).wait()
            fetch(2).wait()
        both = jnp.dot(
            own_w, jnp.concatenate([held[1, :, cols], ones], axis=1), preferred_element_type=F32
        ) + jnp.dot(
            other_w, jnp.concatenate([held[2, :, cols], ones], axis=1), preferred_element_type=F32
        )
        mass = both[:, HDIM:]
        part = (both[:, :HDIM] / mass).astype(BF16)
        level = peak * LOG2_SCALE + jnp.log2(mass)
        for k in range(4):
            lines = slice(k * QUARTER, (k + 1) * QUARTER)
            row = jnp.sum(jnp.where(diagonal, level[lines], 0.0), axis=0, keepdims=True)
            high = row.astype(BF16).astype(F32)
            mid = (row - high).astype(BF16).astype(F32)
            low = row - high - mid
            tail = jnp.where(
                line == 0, high, jnp.where(line == 1, mid, jnp.where(line == 2, low, 0.0))
            )
            out_ref[i * 4 + k, :QUARTER, :] = part[lines]
            out_ref[i * 4 + k, QUARTER:, :] = tail.astype(BF16)
    for copy in copies:
        copy.wait()


def attention_of(side, centre, all_ids, keys, keys_other, values, values_other):
    rows = keys.shape[0]
    groups = len(all_ids)
    return pl.pallas_call(
        functools.partial(attention_kernel, groups),
        out_shape=(
            jax.ShapeDtypeStruct((4 * HALF, QUARTER + TAIL, HDIM), BF16),
            jax.ShapeDtypeStruct((groups, *all_ids[0].shape), jnp.int32),
        ),
        in_specs=[SCALARS, IN_VMEM] + [IN_HBM] * (groups + 1) + [IN_VMEM, IN_HBM, IN_HBM],
        out_specs=(IN_VMEM, IN_VMEM),
        scratch_shapes=[
            pltpu.VMEM((3, rows, HALF * HDIM), BF16),
            pltpu.SemaphoreType.DMA((3,)),
            pltpu.SemaphoreType.DMA((groups,)),
        ],
        compiler_params=params(52),
    )(side, centre, *all_ids, keys, keys_other, values, values_other)


def combine_kernel(in_ref, out_ref):
    count = in_ref.shape[0]
    tails = [in_ref[k, QUARTER:, :].astype(F32) for k in range(count)]
    levels = [t[0:1] + t[1:2] + t[2:3] for t in tails]
    top = functools.reduce(jnp.maximum, levels)
    shares = [jnp.exp2(level - top) for level in levels]
    mass = functools.reduce(jnp.add, shares)
    diagonal = eye(QUARTER, HDIM)
    whole = jnp.zeros((QUARTER, HDIM), F32)
    for k in range(count):
        spread = jnp.where(diagonal, shares[k] / mass, 0.0)
        share = jnp.sum(spread, axis=1, keepdims=True)
        whole += share * in_ref[k, :QUARTER, :].astype(F32)
    whole = whole.astype(BF16)
    for k in range(out_ref.shape[0]):
        out_ref[k] = whole


def columns_of(ids_row, table):
    return lax.dot_general(table, member_of(ids_row), TN, preferred_element_type=F32).astype(BF16)


def group_at(i, z_ref, groups):
    return lax.rem(z_ref[0] + groups - i, groups)


def gather_kernel(side_ref, z_ref, ids_ref, table_ref, after_ref, out_ref):
    del after_ref
    group = group_at(pl.program_id(0), z_ref, pl.num_programs(0))
    for j in range(HALF):
        row = ids_ref[pl.program_id(0), pl.ds(side_ref[0] * HALF + j, 1), :]
        out_ref[j * HDIM : (j + 1) * HDIM, :] = columns_of(row, table_ref[group * HALF + j])


def gather_of(side, z, ids, table, after):
    groups, lines, tokens = ids.shape
    return pl.pallas_call(
        gather_kernel,
        out_shape=jax.ShapeDtypeStruct((groups, HALF * HDIM, tokens), BF16),
        grid=(groups,),
        in_specs=[SCALARS, SCALARS, IN_VMEM, IN_VMEM, IN_HBM],
        out_specs=pl.BlockSpec((None, HALF * HDIM, tokens), lambda i: (i, 0, 0)),
        compiler_params=params(51),
    )(side, z, ids, table, after)


def project_kernel(
    side_ref,
    z_ref,
    near_ref,
    ids_ref,
    table_ref,
    w_ref,
    out_ref,
    held,
    columns_ref,
    done_ref,
    arrived,
    come,
    gone,
):
    groups, blocks = w_ref.shape[:2]
    half = HALF * HDIM
    depth = 2 * half
    width = out_ref.shape[1] // 2
    own = pl.multiple_of(side_ref[0] * half, half)
    other = pl.multiple_of(half - side_ref[0] * half, half)

    each = blocks // 2

    def fetch(i, b):
        entry = lax.rem(z_ref[0] + i, groups)
        part = pl.ds(b * each, each)
        return pltpu.make_async_copy(w_ref.at[entry, part], held.at[i, part], arrived.at[i, b])

    def bring(i):
        target = columns_ref.at[pl.ds(i * depth + own, half), :]
        return pltpu.make_async_copy(near_ref.at[i], target, come.at[i])

    for i in range(groups):
        bring(i).start()
        fetch(i, 0).start()
    for i in range(groups):
        fetch(i, 1).start()

    @pl.loop(0, groups)
    def _(i):
        group = group_at(i, z_ref, groups)
        for j in range(HALF):
            row = ids_ref[i, pl.ds((1 - side_ref[0]) * HALF + j, 1), :]
            start = pl.multiple_of(i * depth + other + j * HDIM, HDIM)
            columns_ref[pl.ds(start, HDIM), :] = columns_of(row, table_ref[group * HALF + j])

    def put(b):
        cols = pl.ds(pl.multiple_of(b * width, width), width)
        return pltpu.make_async_copy(done_ref.at[b], out_ref.at[:, cols], gone.at[b])

    for i in range(groups):
        bring(i).wait()

    @pl.loop(0, 2)
    def _(b):
        for i in range(groups):
            fetch(i, b).wait()
        weight = jnp.concatenate(
            [
                jnp.concatenate([held[i, b * each + k] for k in range(each)], axis=1)
                for i in range(groups)
            ],
            axis=0,
        )
        product = lax.dot_general(columns_ref[...], weight, TN, preferred_element_type=F32)
        done_ref[b] = product.astype(BF16)
        put(b).start()

    for b in range(2):
        put(b).wait()


def project_of(side, z, near, ids, table, weight):
    groups, lines, tokens = ids.shape
    blocks, depth, width = weight.shape[1:]
    return pl.pallas_call(
        project_kernel,
        out_shape=jax.ShapeDtypeStruct((tokens, blocks * width), BF16),
        in_specs=[SCALARS, SCALARS, IN_HBM, IN_VMEM, IN_VMEM, IN_HBM],
        out_specs=IN_HBM,
        scratch_shapes=[
            pltpu.VMEM(weight.shape, BF16),
            pltpu.VMEM((groups * depth, tokens), BF16),
            pltpu.VMEM((2, tokens, blocks * width // 2), BF16),
            pltpu.SemaphoreType.DMA((groups, 2)),
            pltpu.SemaphoreType.DMA((groups,)),
            pltpu.SemaphoreType.DMA((2,)),
        ],
        compiler_params=params(51),
    )(side, z, near, ids, table, weight)


def other_core(value):
    return lax.ppermute(value, "c", [(0, 1), (1, 0)])


def exchanged(value, axes):
    return lax.all_to_all(value, axes, split_axis=0, concat_axis=0, tiled=True)


def from_all_groups(value):
    size = lax.axis_size("z")
    found = [value]
    for d in range(1, size):
        found.append(lax.ppermute(value, "z", [(i, (i + d) % size) for i in range(size)]))
    return found


def local(queries, keys, values, cluster_ids, out_weight):
    core = lax.axis_index("c").astype(jnp.int32)
    side = core[None]
    z = lax.axis_index("z").astype(jnp.int32)[None]
    ids = cluster_ids.T
    size = lax.axis_size("z")
    turned = [
        (x * size + z, (2 * x - z) % size * size + x) for x in range(size) for z in range(size)
    ]
    turned_weight = lax.ppermute(out_weight, ("x", "z"), turned)

    *theirs, mine = totals_of(side, ids, queries)
    arrived = [other_core(piece) for piece in theirs]
    keys_far, values_far, token = halves_of(side, mine, keys, values)
    keys_other, values_other = other_core(keys_far), other_core(values_far)
    totals, turned_weight, ids = add_after(mine, arrived, turned_weight, ids, token)
    weight = lax.all_gather(turned_weight, SEQ, axis=0)
    weight = weight.reshape(size, -1, *weight.shape[1:])
    all_ids = from_all_groups(ids)
    centre = centre_of(exchanged(totals, PLANE), all_ids[1:])
    centre = exchanged(centre, PLANE).reshape(HALF, CLUSTERS, HDIM)
    parts, all_ids = attention_of(
        side, centre, all_ids, keys, keys_other, values, values_other
    )
    parts = exchanged(parts, PLANE)
    table = pl.pallas_call(
        combine_kernel,
        out_shape=jax.ShapeDtypeStruct((lax.axis_size(CUBE), QUARTER, HDIM), BF16),
        compiler_params=params(8),
    )(parts)
    table = exchanged(table, CUBE).reshape(size * HALF, CLUSTERS, HDIM)
    far_table = other_core(table)
    near = gather_of(side, z, all_ids, table, weight)
    return project_of(side, z, near, all_ids, far_table, weight)


def solution(mesh):
    head = mesh.shape["head"]
    finer = Mesh(mesh.devices.reshape(4, 4, 2, head), ("x", "y", "c", "z"))
    in_specs = (P(SEQ, "z"), P(SEQ, "z"), P(SEQ, "z"), P(SEQ, "z"), P("z", SEQ))
    return jax.shard_map(
        local, mesh=finer, in_specs=in_specs, out_specs=P(SEQ, "z"), check_vma=False
    )
```
